512 devices in a mesh: bead: 32 (over x, z_hi, y), space: 16 (over z_lo, core).
Axes of the slice: x: 4, y: 4, z: 16 (z_hi: 2, z_lo: 8; z = z_hi * 8 + z_lo), core: 2. Of those that a mesh axis runs over, the one named last changes fastest.
Arguments:
- positions: float32 [32, 3, 8192], P('bead', None, 'space'), may hold values from -3 to 3
- momenta: float32 [32, 3, 8192], P('bead', None, 'space'), may hold values from -6 to 6
- neighbours: int32 [32, 8192], P(None, 'space'), may hold values from 0 to 767, as said below
- ghost_rows: int32 [4096], P('space'), may hold values from 0 to 511
- species: int32 [8192], P('space'), may hold values from 0 to 1
- species_scale: float32 [2], replicated, may hold values from 0.5 to 2
- mass_table: float32 [2], replicated, may hold values from 0.25 to 1
- w_in: float32 [128, 8], replicated, may hold values from -2 to 2
- w_out: float32 [8, 128], replicated, may hold values from -0.5 to 0.5
Outputs:
- new_positions: float32 [32, 3, 8192], P('bead', None, 'space')
- new_momenta: float32 [32, 3, 8192], P('bead', None, 'space')
The draws below stay inside these ranges and needn't reach their ends.
Inputs may be any that keep to these rules, and one draw needn't show every extreme that they name: `neighbours`: A neighbour entry indexes the window of its atom's domain; slots beyond an atom's live count hold the atom's own position 128 + (atom index mod 512); every atom has at least 8 live slots. `ghost_rows`: domain d's block is entries 2 * 128 * d to 2 * 128 * (d + 1) - 1; entries index atoms within domain d.
All inputs are finite; a program needn't handle non-finite values.
Results may differ from the reference program's by a relative error of at most 0.0003.
Values sent between devices are 32-bit elements; how exact they have to be, the bound alone decides.
No kernel may reach another device: no remote copies, remote signals or barrier semaphores. Data moves between devices by JAX's collectives and lax.ppermute only.
A program may use at most 64 MiB of HBM per device.

```python
import math
import jax
import jax.numpy as jnp
import numpy as np
from jax import lax

BEADS = 32
CB = 4
SPECIES = 2
H = 128
NRBF = 8
SLOTS = 32
NINNER = 3
ATOM_DEV = 512
GHOST = 128
ATOMS = 8192
GHOST_ROWS = 4096
N_SPACE = 16


def draw_neighbours(key, part):
    first_key = jax.random.fold_in(key, 11)
    second_key = jax.random.fold_in(key, 23)
    counts = jax.random.randint(first_key, (1, ATOMS), SLOTS // 4, SLOTS + 1)
    picks = jax.random.randint(second_key, (SLOTS, ATOMS), 0, ATOM_DEV + 2 * GHOST)
    slot_ids = jnp.arange(SLOTS, dtype=jnp.int32)[:, None]
    itself = GHOST + jnp.arange(ATOMS, dtype=jnp.int32) % ATOM_DEV
    return jnp.where(slot_ids < counts, picks, itself[None, :]).astype(jnp.int32)


def touch_ends(entries, stream_key, least, high):
    extent = entries.shape
    index_at = [jax.random.randint(jax.random.fold_in(stream_key, axis), (), 0, extent[axis]) for axis in range(len(extent))]
    entries = entries.at[tuple(index_at)].set(least)
    longest = extent.index(max(extent))
    index_at[longest] = (index_at[longest] + 1) % extent[longest]
    return entries.at[tuple(index_at)].set(high)


def levels(key, extent, split, smallest, largest):
    factor_of = 1.0
    for axis_at, shards_of in split:
        steps = jax.random.uniform(jax.random.fold_in(jax.random.fold_in(key, 6), axis_at), (shards_of,), jnp.float32, smallest / len(split), largest / len(split))
        factor_of = factor_of * jnp.repeat(jnp.exp(steps), extent[axis_at] // shards_of).reshape((-1,) + (1,) * (len(extent) - 1 - axis_at))
    return factor_of


def bell_draw(own_key, shape, width, bound, pieces=(), held_as=jnp.bfloat16):
    drawn = width * jax.random.normal(own_key, shape, jnp.float32)
    if pieces:
        drawn = drawn * levels(own_key, shape, pieces, -0.22, 0.18)
    return jnp.clip(drawn, -bound, bound).astype(held_as)


def setup_inputs(seed: int = 0) -> dict:
    key_list = jax.random.split(jax.random.key(seed), 10)
    positions = bell_draw(key_list[0], (BEADS, 3, ATOMS), 0.5, 3.0, ((0, 32), (2, 16)), jnp.float32)
    momenta = bell_draw(key_list[1], (BEADS, 3, ATOMS), 1.0, 6.0, ((0, 32), (2, 16)), jnp.float32)
    neighbours = draw_neighbours(jax.random.fold_in(key_list[9], 71), 0)
    ghost_rows = touch_ends(jax.random.randint(key_list[3], (GHOST_ROWS,), 0, ATOM_DEV), jax.random.fold_in(key_list[3], 1), 0, ATOM_DEV - 1).astype(jnp.int32)
    species = touch_ends(jax.random.randint(key_list[4], (ATOMS,), 0, SPECIES), jax.random.fold_in(key_list[4], 1), 0, SPECIES - 1).astype(jnp.int32)
    species_scale = jnp.clip(jnp.exp(jax.random.uniform(key_list[5], (SPECIES,), jnp.float32, math.log(0.5), math.log(2.0))), 0.5, 2.0)
    mass_table = jnp.clip(jnp.exp(jax.random.uniform(key_list[6], (SPECIES,), jnp.float32, math.log(0.25), math.log(1.0))), 0.25, 1.0)
    w_in = bell_draw(key_list[7], (H, NRBF), NRBF ** -0.5, 2.0, (), jnp.float32)
    w_out = bell_draw(key_list[8], (NRBF, H), H ** -0.5, 0.5, (), jnp.float32)
    return dict(positions=positions, momenta=momenta, neighbours=neighbours, ghost_rows=ghost_rows, species=species, species_scale=species_scale, mass_table=mass_table, w_in=w_in, w_out=w_out)


polymer_freq = 10.0
outer_step = 6.0
pair_width = 1.0
pair_strength = 1.0
highest = lax.Precision.HIGHEST

def mode_matrix(count):
    beadpos = np.arange(count)[None, :]
    modeidx = np.arange(count)[:, None]
    middle = count // 2
    cosine = np.sqrt(2.0 / count) * np.cos(2.0 * np.pi * beadpos * modeidx / count)
    sine_rows = np.sqrt(2.0 / count) * np.sin(2.0 * np.pi * beadpos * modeidx / count)
    matrix = np.where(modeidx < middle, cosine, sine_rows)
    matrix = np.where(modeidx == 0, 1.0 / np.sqrt(count), matrix)
    matrix = np.where(modeidx == middle, np.cos(np.pi * beadpos) / np.sqrt(count), matrix)
    return matrix

def mode_scales(count, inner_step):
    frequency = 2.0 * polymer_freq * np.sin(np.pi * np.arange(count) / count)
    nonzero = np.where(frequency > 0, frequency, 1.0)
    cosine = np.cos(frequency * inner_step)
    drift_gain = np.where(frequency > 0, np.sin(frequency * inner_step) / nonzero, inner_step)
    spring = frequency * np.sin(frequency * inner_step)
    return (cosine, drift_gain, spring)

def polymer_tables(count, inner_step):
    modes = mode_matrix(count)
    cosine, drift_gain, spring = mode_scales(count, inner_step)
    persist = modes.T @ (cosine[:, None] * modes)
    coupling = modes.T @ (drift_gain[:, None] * modes)
    restoring = -(modes.T @ (spring[:, None] * modes))
    return (jnp.asarray(persist, jnp.float32), jnp.asarray(coupling, jnp.float32), jnp.asarray(restoring, jnp.float32))

def contraction(count, fewer):
    full_modes = mode_matrix(count)
    small_modes = mode_matrix(fewer)
    kept = list(range(fewer // 2 + 1)) + list(range(count - fewer // 2 + 1, count))
    contract = np.sqrt(fewer / count) * (small_modes.T @ full_modes[kept])
    expand = count / fewer * contract.T
    return (jnp.asarray(contract, jnp.float32), jnp.asarray(expand, jnp.float32))

def radial_rates(count):
    return 0.2 * 2.0 ** (np.arange(count) / 2.0)

def species_lookup(species, table):
    kinds = jnp.arange(table.shape[0], dtype=jnp.int32)
    return lax.optimization_barrier(jnp.sum(jnp.where(species[None, :] == kinds[:, None], table[:, None], 0.0), axis=0))

def pair_forces(extended, targets, centres):
    others = extended[:, targets]
    middle = extended[:, centres]
    offsets = others[:3] - middle[:3, None, :]
    squared = lax.optimization_barrier(jnp.sum(offsets * offsets, axis=0))
    weights = others[3] * jnp.exp(-squared / pair_width)
    return pair_strength * middle[3] * lax.optimization_barrier(jnp.sum(weights[None] * offsets, axis=1))

def learned_forces(extended, charges, targets, centres, w_in, w_out):
    live = (targets != centres[None, :]).astype(jnp.float32)
    weights = charges[targets] * live
    others = extended[:, targets]
    middle = extended[:, centres]
    offsets = others - middle[:, None, :]
    squared = lax.optimization_barrier(jnp.sum(offsets * offsets, axis=0))
    rates = jnp.asarray(radial_rates(w_in.shape[1]), jnp.float32)
    basis = jnp.exp(-rates[:, None, None] * squared[None])
    message = lax.optimization_barrier(jnp.sum(weights[None] * basis, axis=1)) / targets.shape[0]
    hidden = jax.nn.silu(jnp.dot(w_in, message, precision=highest, preferred_element_type=jnp.float32))
    radial = jnp.dot(w_out, hidden, precision=highest, preferred_element_type=jnp.float32)
    profile = lax.optimization_barrier(jnp.sum(radial[:, None, :] * basis, axis=0))
    return lax.optimization_barrier(jnp.sum((weights * profile)[None] * offsets, axis=1))

def window(values, ghost_rows):
    channels = values.shape[0]
    blocks = values.reshape(channels, N_SPACE, ATOM_DEV)
    picked = ghost_rows.reshape(N_SPACE, 2 * GHOST)
    sends = jnp.take_along_axis(blocks, jnp.broadcast_to(picked[None], (channels, N_SPACE, 2 * GHOST)), axis=2)
    from_below = jnp.roll(sends[:, :, GHOST:], 1, axis=1)
    from_above = jnp.roll(sends[:, :, :GHOST], -1, axis=1)
    return jnp.concatenate([from_below, blocks, from_above], axis=2).reshape(channels, -1)

def reference(positions, momenta, neighbours, ghost_rows, species, species_scale, mass_table, w_in, w_out):
    inner_step = outer_step / NINNER
    persist, coupling, restoring = polymer_tables(BEADS, inner_step)
    contract, expand = contraction(BEADS, CB)
    charges = species_lookup(species, species_scale)
    masses = species_lookup(species, mass_table)
    window_length = ATOM_DEV + 2 * GHOST
    atom_ids = jnp.arange(ATOMS, dtype=jnp.int32)
    domain = atom_ids // ATOM_DEV
    targets = domain[None, :] * window_length + neighbours
    centres = domain * window_length + GHOST + atom_ids % ATOM_DEV
    charge_window = window(charges[None], ghost_rows)[0]

    def cheap_forces(coords):

        def single(bead_coords):
            extended = window(jnp.concatenate([bead_coords, charges[None]], axis=0), ghost_rows)
            return pair_forces(extended, targets, centres)
        return lax.map(single, coords)

    def expensive_forces(coords):
        reduced = jnp.einsum('cb,bxa->cxa', contract, coords, precision=highest)

        def single(reduced_coords):
            return learned_forces(window(reduced_coords, ghost_rows), charge_window, targets, centres, w_in, w_out)
        return jnp.einsum('bc,cxa->bxa', expand, lax.map(single, reduced), precision=highest)

    def propagate(coords, moments):
        new_coords = jnp.einsum('ab,bxn->axn', persist, coords, precision=highest) + jnp.einsum('ab,bxn->axn', coupling, moments, precision=highest) / masses
        new_moments = jnp.einsum('ab,bxn->axn', persist, moments, precision=highest) + jnp.einsum('ab,bxn->axn', restoring, coords, precision=highest) * masses
        return (new_coords, new_moments)
    coords = positions
    moments = momenta + 0.5 * outer_step * expensive_forces(coords)
    cheap_now = cheap_forces(coords)
    for repeat in range(NINNER):
        moments = moments + 0.5 * inner_step * cheap_now
        coords, moments = propagate(coords, moments)
        cheap_now = cheap_forces(coords)
        moments = moments + 0.5 * inner_step * cheap_now
    moments = moments + 0.5 * outer_step * expensive_forces(coords)
    return (coords, moments)
```

```python
import functools

import jax
import jax.numpy as jnp
import numpy as np
from jax import lax
from jax.experimental import pallas as pl
from jax.experimental.pallas import tpu as pltpu
from jax.sharding import PartitionSpec as P

BEADS = 32
CB = 4
NINNER = 3
NRBF = 8
H = 128
SLOTS = 32
ATOMS = 512
CHUNKS = 4
WINDOW = 6
N_SPACE = 16

polymer_freq = 10.0
outer_step = 6.0
inner_step = outer_step / NINNER
f32 = jnp.float32
bf16 = jnp.bfloat16
VMEM_LIMIT = 56 * 1024 * 1024


def mode_matrix(count):
    beadpos = np.arange(count)[None, :]
    modeidx = np.arange(count)[:, None]
    middle = count // 2
    cosine = np.sqrt(2.0 / count) * np.cos(2.0 * np.pi * beadpos * modeidx / count)
    sine_rows = np.sqrt(2.0 / count) * np.sin(2.0 * np.pi * beadpos * modeidx / count)
    matrix = np.where(modeidx < middle, cosine, sine_rows)
    matrix = np.where(modeidx == 0, 1.0 / np.sqrt(count), matrix)
    matrix = np.where(modeidx == middle, np.cos(np.pi * beadpos) / np.sqrt(count), matrix)
    return matrix


def polymer_tables(count):
    modes = mode_matrix(count)
    frequency = 2.0 * polymer_freq * np.sin(np.pi * np.arange(count) / count)
    nonzero = np.where(frequency > 0, frequency, 1.0)
    cosine = np.cos(frequency * inner_step)
    drift_gain = np.where(frequency > 0, np.sin(frequency * inner_step) / nonzero, inner_step)
    spring = frequency * np.sin(frequency * inner_step)
    persist = modes.T @ (cosine[:, None] * modes)
    coupling = modes.T @ (drift_gain[:, None] * modes)
    restoring = -(modes.T @ (spring[:, None] * modes))
    return persist, coupling, restoring


def contraction(count, fewer):
    full_modes = mode_matrix(count)
    small_modes = mode_matrix(fewer)
    kept = list(range(fewer // 2 + 1)) + list(range(count - fewer // 2 + 1, count))
    contract = np.sqrt(fewer / count) * (small_modes.T @ full_modes[kept])
    expand = count / fewer * contract.T
    return contract, expand


def three_terms(matrix):
    high = matrix.astype(np.float32).astype(jnp.bfloat16)
    low = (matrix - high.astype(np.float64)).astype(np.float32).astype(jnp.bfloat16)
    return np.concatenate([high, low, high], axis=1)


BEAD_OF_ROW = np.array([x * 8 + z * 4 + y for z in range(2) for x in range(4) for y in range(4)])


def tables():
    persist, coupling, restoring = polymer_tables(BEADS)
    contract, expand = contraction(BEADS, CB)
    order = BEAD_OF_ROW
    persist, coupling, restoring = (m[np.ix_(order, order)] for m in (persist, coupling, restoring))
    contract, expand = contract[:, order], expand[order]
    step = np.block([[persist, coupling], [restoring, persist]])
    padded_expand = np.concatenate([expand, np.zeros((BEADS, 16 - CB))], axis=1)
    kick = np.concatenate([coupling @ padded_expand, persist @ padded_expand], axis=0)
    first = three_terms(np.concatenate([step, 0.5 * outer_step * kick], axis=1))
    later = three_terms(step)
    reduce_ = three_terms(np.concatenate([contract, np.zeros((16 - CB, BEADS))], axis=0))
    return first, later, reduce_, (0.5 * outer_step * expand).astype(np.float32)


def lanes(source, index):
    return jnp.take_along_axis(source, index, axis=1)


def row8(row):
    return jnp.broadcast_to(row, (8, 128))


def split_rows(value):
    high = value.astype(bf16)
    low = (value - high.astype(f32)).astype(bf16)
    return jnp.concatenate([high, high, low], axis=0)


def dot3(matrix, value):
    return jnp.dot(matrix, split_rows(value), preferred_element_type=f32)


def by_species(species, table):
    return jnp.where(species == 0, table[0], table[1])


def ghosts_of(chunk, index):
    first = chunk(0)
    rows = first.shape[0]
    lane = jnp.broadcast_to(index & 127, (rows, 128))
    part = jnp.broadcast_to(index >> 7, (rows, 128))
    out = lanes(first, lane)
    for k in range(1, CHUNKS):
        out = jnp.where(part == k, lanes(chunk(k), lane), out)
    return out


def tile_index(neighbours, g, a):
    index = neighbours[8 * g : 8 * g + 8, 128 * a : 128 * a + 128]
    return index & 127, [(index >> 7) == k for k in range(1, WINDOW)], index


def looked_up(rows, lane, masks):
    out = lanes(rows[0], lane)
    for k in range(1, WINDOW):
        out = jnp.where(masks[k - 1], lanes(rows[k], lane), out)
    return out


def cheap_by_lanes(table, neighbours, weights, a):
    rows = [[row8(table(x, k)) for k in range(WINDOW)] for x in range(3)]
    total = [jnp.zeros((8, 128), f32) for _ in range(3)]
    for g in range(SLOTS // 8):
        lane, masks, _ = tile_index(neighbours, g, a)
        offset = [looked_up(rows[x], lane, masks) - rows[x][1 + a] for x in range(3)]
        squared = offset[0] * offset[0] + offset[1] * offset[1] + offset[2] * offset[2]
        w = weights[8 * g : 8 * g + 8, 128 * a : 128 * a + 128] * jnp.exp(-squared)
        for x in range(3):
            total[x] = total[x] + w * offset[x]
    return [jnp.sum(t, axis=0, keepdims=True) for t in total]


def powers(squared):
    even = jnp.exp(-0.2 * squared)
    odd = jnp.exp(-(0.2 * 2.0**0.5) * squared)
    out = [even, odd]
    for _ in range(3):
        even, odd = even * even, odd * odd
        out += [even, odd]
    return out


def learned_by_lanes(table, neighbours, weights, w_in, w_out, offsets, messages, radials, store):
    for c in range(CB):
        for a in range(CHUNKS):
            rows = [[row8(table(c, x, k)) for k in range(WINDOW)] for x in range(3)]
            total = [jnp.zeros((8, 128), f32) for _ in range(NRBF)]
            for g in range(SLOTS // 8):
                lane, masks, _ = tile_index(neighbours, g, a)
                offset = [looked_up(rows[x], lane, masks) - rows[x][1 + a] for x in range(3)]
                squared = offset[0] * offset[0] + offset[1] * offset[1] + offset[2] * offset[2]
                for x in range(3):
                    offsets[c, a, g, x] = offset[x]
                w = weights[8 * g : 8 * g + 8, 128 * a : 128 * a + 128]
                for r, basis in enumerate(powers(squared)):
                    total[r] = total[r] + w * basis
            at = c * ATOMS + a * 128
            for r in range(NRBF):
                messages[r : r + 1, at : at + 128] = jnp.sum(total[r], axis=0, keepdims=True) * (1.0 / SLOTS)
    highest = lax.Precision.HIGHEST
    hidden = jnp.dot(w_in[...], messages[...], precision=highest, preferred_element_type=f32)
    hidden = hidden * (1.0 / (1.0 + jnp.exp(-hidden)))
    radials[...] = jnp.dot(w_out[...], hidden, precision=highest, preferred_element_type=f32)
    for c in range(CB):
        for a in range(CHUNKS):
            at = c * ATOMS + a * 128
            radial = [row8(radials[r : r + 1, at : at + 128]) for r in range(NRBF)]
            total = [jnp.zeros((8, 128), f32) for _ in range(3)]
            for g in range(SLOTS // 8):
                offset = [offsets[c, a, g, x] for x in range(3)]
                squared = offset[0] * offset[0] + offset[1] * offset[1] + offset[2] * offset[2]
                basis = powers(squared)
                profile = radial[0] * basis[0]
                for r in range(1, NRBF):
                    profile = profile + radial[r] * basis[r]
                w = weights[8 * g : 8 * g + 8, 128 * a : 128 * a + 128] * profile
                for x in range(3):
                    total[x] = total[x] + w * offset[x]
            for x in range(3):
                store(c, x, a, jnp.sum(total[x], axis=0, keepdims=True))


def cheap_by_matmul(coords, below, above, neighbours, weights, stacked, total):
    rows = 3 * BEADS
    parts = (
        jnp.concatenate([below[...], coords[:, 0:128]], axis=1),
        coords[:, 128:384],
        jnp.concatenate([coords[:, 384:512], above[...]], axis=1),
    )
    for k, part in enumerate(parts):
        high = part.astype(bf16)
        stacked[k * rows : (k + 1) * rows, 0:256] = high
        stacked[k * rows : (k + 1) * rows, 256:512] = (part - high.astype(f32)).astype(bf16)
    rounded = coords[...].astype(bf16).astype(f32)
    rounded = rounded + (coords[...] - rounded).astype(bf16).astype(f32)
    total[...] = jnp.zeros_like(total)
    unroll = 4

    def group(i, _):
        for j in range(unroll):
            slot = i * unroll + j
            index = neighbours[pl.ds(slot, 1), :]
            place = lax.broadcasted_iota(jnp.int32, (256, ATOMS), 0)
            chosen = jnp.where(place == (index & 255), 1.0, 0.0).astype(bf16)
            picked = jnp.dot(
                stacked[...], jnp.concatenate([chosen, chosen], axis=0), preferred_element_type=f32
            )
            part = index >> 8
            other = jnp.where(
                part == 0,
                picked[0:rows],
                jnp.where(part == 1, picked[rows : 2 * rows], picked[2 * rows : 3 * rows]),
            )
            offset = other - rounded
            x, y, z = offset[0:BEADS], offset[BEADS : 2 * BEADS], offset[2 * BEADS :]
            w = weights[pl.ds(slot, 1), :] * jnp.exp(-(x * x + y * y + z * z))
            total[0:BEADS] += w * x
            total[BEADS : 2 * BEADS] += w * y
            total[2 * BEADS :] += w * z
        return 0

    lax.fori_loop(0, SLOTS // unroll, group, 0)


def propagated(coords, veloc, table, extra=None):
    wide = []
    for x in range(3):
        at = slice(x * BEADS, (x + 1) * BEADS)
        pieces = [coords[at], veloc[at]]
        if extra is not None:
            pieces.append(extra[x])
        wide.append(jnp.concatenate(pieces, axis=0))
    return dot3(table[...], jnp.concatenate(wide, axis=1))


def first_kernel(pos, mom, species, mass_table, out):
    mass = by_species(species[...], mass_table)
    out[0:12] = pos[...]
    for x in range(3):
        out[12 + 4 * x : 16 + 4 * x] = mom[4 * x : 4 * x + 4] / mass


def send_kernel(place, own, peer, species, scale, ghost_rows, down, up, rows):
    upper = place[0] == 0
    low = jnp.where(upper, own[...], peer[...])
    high = jnp.where(upper, peer[...], own[...])
    charge = by_species(species[...], scale)
    for k in range(CHUNKS):
        for x in range(3):
            rows[k, x : x + 1] = low[4 * x + k : 4 * x + k + 1]
            rows[k, 3 + x : 4 + x] = high[4 * x + k : 4 * x + k + 1]
        rows[k, 6:7] = charge[k : k + 1]
        rows[k, 7:8] = charge[k : k + 1]
    down[...] = ghosts_of(lambda k: rows[k], ghost_rows[0:1])
    up[...] = ghosts_of(lambda k: rows[k], ghost_rows[1:2])


def pack_kernel(
    place, own, peer, below, above, species, scale, mass_table, neighbours, out, weights, block, charges
):
    upper = place[0] == 0
    low = jnp.where(upper, own[...], peer[...])
    high = jnp.where(upper, peer[...], own[...])
    charge = by_species(species[...], scale)
    inverse = by_species(species[...], [1.0 / mass_table[0], 1.0 / mass_table[1]])
    charges[0:1] = below[6:7]
    charges[1:5] = charge
    charges[5:6] = above[6:7]
    for k, state in enumerate((low, high)):
        base = 32 * k
        for x in range(3):
            at = base + 6 * x
            block[at : at + 1] = below[3 * k + x : 3 * k + x + 1]
            block[at + 1 : at + 5] = state[4 * x : 4 * x + 4]
            block[at + 5 : at + 6] = above[3 * k + x : 3 * k + x + 1]
        block[base + 18 : base + 30] = state[12:24]
        block[base + 30 : base + 32] = jnp.zeros((2, 128), f32)
    for a in range(CHUNKS):
        itself = 128 + 128 * a + lax.broadcasted_iota(jnp.int32, (8, 128), 1)
        rows = [row8(charges[k : k + 1]) for k in range(WINDOW)]
        for g in range(SLOTS // 8):
            lane, masks, index = tile_index(neighbours, g, a)
            q = looked_up(rows, lane, masks)
            weights[8 * g : 8 * g + 8, 128 * a : 128 * a + 128] = jnp.where(index == itself, 0.0, q)
    for k in range(2):
        base = 32 * k
        for a in range(CHUNKS):
            force = cheap_by_lanes(
                lambda x, w: block[base + 6 * x + w : base + 6 * x + w + 1], neighbours, weights, a
            )
            gain = charge[a : a + 1] * inverse[a : a + 1]
            for x in range(3):
                at = base + 18 + 4 * x + a
                block[at : at + 1] = block[at : at + 1] + gain * force[x]
    for i in range(16):
        out[i] = block[...]


def begin_kernel(
    gathered, neighbours, weights, species, mass_table, ghost_rows, w_in, w_out, first, reduce_,
    coords, veloc, down, up,
    window, start, contracted, offsets, messages, radials, slow,
):
    inverse = by_species(species[...], [1.0 / mass_table[0], 1.0 / mass_table[1]])
    for z in range(2):
        for x in range(3):
            at = slice(x * BEADS + 16 * z, x * BEADS + 16 * z + 16)
            for k in range(WINDOW):
                window[at, 128 * k : 128 * k + 128] = gathered[:, 32 * z + 6 * x + k, :]
            for k in range(CHUNKS):
                start[at, 128 * k : 128 * k + 128] = gathered[:, 32 * z + 18 + 4 * x + k, :]
    for x in range(3):
        contracted[x] = dot3(reduce_[...], window[x * BEADS : (x + 1) * BEADS, :])
    slow[...] = jnp.zeros_like(slow)

    def store(c, x, a, value):
        slow[x, c : c + 1, 128 * a : 128 * a + 128] = value

    learned_by_lanes(
        lambda c, x, k: contracted[x, c : c + 1, 128 * k : 128 * k + 128],
        neighbours, weights, w_in, w_out, offsets, messages, radials, store,
    )
    moved = propagated(
        window[:, 128:640], start[...], first, [slow[x] * inverse for x in range(3)]
    )
    finish_step(moved, coords, veloc, ghost_rows, down, up)


def finish_step(moved, coords, veloc, ghost_rows, down, up):
    for x in range(3):
        at = slice(x * BEADS, (x + 1) * BEADS)
        coords[at] = moved[0:BEADS, ATOMS * x : ATOMS * (x + 1)]
        veloc[at] = moved[BEADS : 2 * BEADS, ATOMS * x : ATOMS * (x + 1)]
    for i in range(3 * BEADS // 8):
        chunk = lambda k: coords[8 * i : 8 * i + 8, 128 * k : 128 * k + 128]
        down[8 * i : 8 * i + 8] = ghosts_of(chunk, ghost_rows[0:1])
        up[8 * i : 8 * i + 8] = ghosts_of(chunk, ghost_rows[1:2])


def kicked(coords, veloc, below, above, neighbours, weights, species, scale, mass_table, stacked, total):
    cheap_by_matmul(coords, below, above, neighbours, weights, stacked, total)
    gain = by_species(species[...], [scale[0] / mass_table[0], scale[1] / mass_table[1]]) * inner_step
    return veloc[...] + gain * total[...]


def middle_kernel(
    coords, veloc, below, above, neighbours, weights, species, scale, mass_table, ghost_rows, later,
    new_coords, new_veloc, down, up, stacked, total,
):
    velocities = kicked(
        coords, veloc, below, above, neighbours, weights, species, scale, mass_table, stacked, total
    )
    moved = propagated(coords[...], velocities, later)
    finish_step(moved, new_coords, new_veloc, ghost_rows, down, up)


def last_kernel(
    place, coords, veloc, below, above, neighbours, weights, species, scale, mass_table, ghost_rows, later,
    reduce_, own, contracted, down, up, stacked, total, moved, rows,
):
    velocities = kicked(
        coords, veloc, below, above, neighbours, weights, species, scale, mass_table, stacked, total
    )
    moved[...] = propagated(coords[...], velocities, later)
    small = dot3(reduce_[...], moved[0:BEADS, :])
    for x in range(3):
        at = slice(ATOMS * x, ATOMS * (x + 1))
        own[x : x + 1] = moved[pl.ds(place[1], 1), at]
        own[3 + x : 4 + x] = moved[pl.ds(BEADS + place[1], 1), at]
        contracted[4 * x : 4 * x + 4] = small[0:4, at]
    own[6:8] = jnp.zeros((2, ATOMS), f32)
    contracted[12:16] = jnp.zeros((4, ATOMS), f32)
    rows[0:12] = contracted[0:12]
    for which, out in ((2, down), (3, up)):
        for x in range(3):
            rows[12 + x : 13 + x] = moved[pl.ds(place[which], 1), ATOMS * x : ATOMS * (x + 1)]
        rows[15:16] = contracted[12:13]
        index = ghost_rows[which - 2 : which - 1]
        for i in range(2):
            out[8 * i : 8 * i + 8] = ghosts_of(
                lambda k: rows[8 * i : 8 * i + 8, 128 * k : 128 * k + 128], index
            )


def end_kernel(
    place, expand, own, contracted, below, above, neighbours, weights, species, scale, mass_table, w_in, w_out,
    new_pos, new_mom,
    window, offsets, messages, radials, slow,
):
    charge = by_species(species[...], scale)
    mass = by_species(species[...], mass_table)
    window[0:16, 0:128] = below[...]
    window[0:16, 640:768] = above[...]
    window[0:12, 128:640] = contracted[0:12]
    window[12:15, 128:640] = own[0:3]

    def store(c, x, a, value):
        slow[c, x, a : a + 1] = value

    learned_by_lanes(
        lambda c, x, k: window[4 * x + c : 4 * x + c + 1, 128 * k : 128 * k + 128],
        neighbours, weights, w_in, w_out, offsets, messages, radials, store,
    )
    for a in range(CHUNKS):
        force = cheap_by_lanes(
            lambda x, k: window[12 + x : 13 + x, 128 * k : 128 * k + 128], neighbours, weights, a
        )
        at = slice(128 * a, 128 * a + 128)
        for x in range(3):
            value = mass[a : a + 1] * own[3 + x : 4 + x, at] + (0.5 * inner_step) * charge[a : a + 1] * force[x]
            for c in range(CB):
                value = value + expand[place[1], c] * slow[c, x, a : a + 1]
            new_mom[4 * x + a : 4 * x + a + 1] = value
            new_pos[4 * x + a : 4 * x + a + 1] = own[x : x + 1, at]


def call(kernel, outs, scratch, args, scalars):
    specs = [
        pl.BlockSpec(memory_space=pltpu.SMEM if i in scalars else pltpu.VMEM) for i in range(len(args))
    ]
    shapes = [jax.ShapeDtypeStruct(s, f32) for s in outs]
    return pl.pallas_call(
        kernel,
        out_shape=shapes,
        in_specs=specs,
        out_specs=[pl.BlockSpec(memory_space=pltpu.VMEM)] * len(outs),
        scratch_shapes=[pltpu.VMEM(s, d) for s, d in scratch],
        compiler_params=pltpu.CompilerParams(vmem_limit_bytes=VMEM_LIMIT),
    )(*args)


RING = ("bead", "space")


def ring(step):
    pairs = []
    for bead in range(BEADS):
        for domain in range(N_SPACE):
            to = domain + step
            other = bead if 0 <= to < N_SPACE else bead ^ 4
            pairs.append((bead * N_SPACE + domain, other * N_SPACE + to % N_SPACE))
    return pairs


def exchange(down, up):
    below = lax.ppermute(up, RING, ring(1))
    above = lax.ppermute(down, RING, ring(-1))
    return below, above


def body(
    positions, momenta, neighbours, ghost_rows, species, species_scale, mass_table, w_in, w_out
):
    first, later, reduce_, expand = tables()
    first, later, reduce_ = (jnp.asarray(t) for t in (first, later, reduce_))
    expand = jnp.asarray(expand)
    bead = lax.axis_index("bead")
    domain = lax.axis_index("space")
    half = (bead // 4) % 2
    row = half * 16 + (bead // 8) * 4 + bead % 4
    other = (1 - half) * 16 + (bead // 8) * 4 + bead % 4
    row_below = jnp.where(domain == 0, other, row)
    row_above = jnp.where(domain == N_SPACE - 1, other, row)
    place = jnp.stack([half, row, row_below, row_above]).astype(jnp.int32)

    pos = positions.reshape(12, 128)
    mom = momenta.reshape(12, 128)
    sp4 = species.reshape(4, 128)
    sp1 = species.reshape(1, ATOMS)
    ghosts = ghost_rows.reshape(2, 128)

    (own,) = call(first_kernel, [(24, 128)], [], (pos, mom, sp4, mass_table), (3,))
    peer = lax.ppermute(own, "bead", [(b, b ^ 4) for b in range(BEADS)])
    down, up = call(
        send_kernel, [(8, 128)] * 2, [((4, 8, 128), f32)], (place, own, peer, sp4, species_scale, ghosts), (0, 4)
    )
    below, above = exchange(down, up)
    block, weights = call(
        pack_kernel,
        [(16, 64, 128), (SLOTS, ATOMS)],
        [((64, 128), f32), ((8, 128), f32)],
        (place, own, peer, below, above, sp4, species_scale, mass_table, neighbours),
        (0, 6, 7),
    )
    groups = [[x * 8 + z * 4 + y for x in range(4) for y in range(4)] for z in range(2)]
    gathered = lax.all_to_all(block, "bead", 0, 0, axis_index_groups=groups, tiled=True)
    offsets = ((CB, CHUNKS, SLOTS // 8, 3, 8, 128), f32)
    coords, veloc, down, up = call(
        begin_kernel,
        [(96, ATOMS), (96, ATOMS), (96, 128), (96, 128)],
        [
            ((96, 768), f32), ((96, ATOMS), f32), ((3, 16, 768), f32), offsets, ((NRBF, CB * ATOMS), f32),
            ((NRBF, CB * ATOMS), f32), ((3, 16, ATOMS), f32),
        ],
        (gathered, neighbours, weights, sp1, mass_table, ghosts, w_in, w_out, first, reduce_),
        (4,),
    )
    big = [((3 * 96, 512), bf16), ((96, ATOMS), f32)]
    below, above = exchange(down, up)
    coords, veloc, down, up = call(
        middle_kernel,
        [(96, ATOMS), (96, ATOMS), (96, 128), (96, 128)],
        big,
        (coords, veloc, below, above, neighbours, weights, sp1, species_scale, mass_table, ghosts, later),
        (7, 8),
    )
    below, above = exchange(down, up)
    mine, contracted, down, up = call(
        last_kernel,
        [(8, ATOMS), (16, ATOMS), (16, 128), (16, 128)],
        big + [((2 * BEADS, 3 * ATOMS), f32), ((16, ATOMS), f32)],
        (place, coords, veloc, below, above, neighbours, weights, sp1, species_scale, mass_table, ghosts, later, reduce_),
        (0, 8, 9),
    )
    below, above = exchange(down, up)
    new_pos, new_mom = call(
        end_kernel,
        [(12, 128), (12, 128)],
        [
            ((16, 768), f32), offsets, ((NRBF, CB * ATOMS), f32), ((NRBF, CB * ATOMS), f32),
            ((CB, 3, CHUNKS, 128), f32),
        ],
        (place, expand, mine, contracted, below, above, neighbours, weights, sp4, species_scale, mass_table, w_in, w_out),
        (0, 1, 9, 10),
    )
    return new_pos.reshape(1, 3, ATOMS), new_mom.reshape(1, 3, ATOMS)


def solution(mesh):
    in_specs = (
        P("bead", None, "space"),
        P("bead", None, "space"),
        P(None, "space"),
        P("space"),
        P("space"),
        P(),
        P(),
        P(),
        P(),
    )
    out_specs = (P("bead", None, "space"), P("bead", None, "space"))
    return jax.shard_map(body, mesh=mesh, in_specs=in_specs, out_specs=out_specs, check_vma=False)
```

```python
import functools

import jax
import jax.numpy as jnp
import numpy as np
from jax import lax
from jax.experimental import pallas as pl
from jax.experimental.pallas import tpu as pltpu
from jax.sharding import PartitionSpec as P

BEADS = 32
CB = 4
NINNER = 3
NRBF = 8
H = 128
SLOTS = 32
ATOMS = 512
CHUNKS = 4
WINDOW = 6
N_SPACE = 16

polymer_freq = 10.0
outer_step = 6.0
inner_step = outer_step / NINNER
f32 = jnp.float32
bf16 = jnp.bfloat16
VMEM_LIMIT = 12 * 1024 * 1024


def mode_matrix(count):
    beadpos = np.arange(count)[None, :]
    modeidx = np.arange(count)[:, None]
    middle = count // 2
    cosine = np.sqrt(2.0 / count) * np.cos(2.0 * np.pi * beadpos * modeidx / count)
    sine_rows = np.sqrt(2.0 / count) * np.sin(2.0 * np.pi * beadpos * modeidx / count)
    matrix = np.where(modeidx < middle, cosine, sine_rows)
    matrix = np.where(modeidx == 0, 1.0 / np.sqrt(count), matrix)
    matrix = np.where(modeidx == middle, np.cos(np.pi * beadpos) / np.sqrt(count), matrix)
    return matrix


def polymer_tables(count):
    modes = mode_matrix(count)
    frequency = 2.0 * polymer_freq * np.sin(np.pi * np.arange(count) / count)
    nonzero = np.where(frequency > 0, frequency, 1.0)
    cosine = np.cos(frequency * inner_step)
    drift_gain = np.where(frequency > 0, np.sin(frequency * inner_step) / nonzero, inner_step)
    spring = frequency * np.sin(frequency * inner_step)
    persist = modes.T @ (cosine[:, None] * modes)
    coupling = modes.T @ (drift_gain[:, None] * modes)
    restoring = -(modes.T @ (spring[:, None] * modes))
    return persist, coupling, restoring


def contraction(count, fewer):
    full_modes = mode_matrix(count)
    small_modes = mode_matrix(fewer)
    kept = list(range(fewer // 2 + 1)) + list(range(count - fewer // 2 + 1, count))
    contract = np.sqrt(fewer / count) * (small_modes.T @ full_modes[kept])
    expand = count / fewer * contract.T
    return contract, expand


def bf16_terms(matrix):
    out, rest = [], matrix
    for _ in range(3):
        out.append(rest.astype(np.float32).astype(jnp.bfloat16))
        rest = rest - out[-1].astype(np.float64)
    return out


def three_terms(matrix):
    high, low, _ = bf16_terms(matrix)
    return np.concatenate([high, low, high], axis=1)


def six_terms(matrix):
    high, middle, low = bf16_terms(matrix)
    return np.concatenate([high, high, middle, middle, high, low], axis=1)


BEAD_OF_ROW = np.array([x * 8 + z * 4 + y for z in range(2) for x in range(4) for y in range(4)])


def tables():
    persist, coupling, restoring = polymer_tables(BEADS)
    contract, expand = contraction(BEADS, CB)
    order = BEAD_OF_ROW
    persist, coupling, restoring = (m[np.ix_(order, order)] for m in (persist, coupling, restoring))
    contract, expand = contract[:, order], expand[order]
    step = np.block([[persist, coupling], [restoring, persist]])
    padded_expand = np.concatenate([expand, np.zeros((BEADS, 16 - CB))], axis=1)
    kick = np.concatenate([coupling @ padded_expand, persist @ padded_expand], axis=0)
    first = six_terms(np.concatenate([step, 0.5 * outer_step * kick], axis=1))
    later = six_terms(step)
    reduce_ = three_terms(np.concatenate([contract, np.zeros((16 - CB, BEADS))], axis=0))
    return first, later, reduce_, (0.5 * outer_step * expand).astype(np.float32)


def lanes(source, index):
    return jnp.take_along_axis(source, index, axis=1)


def row8(row):
    return jnp.broadcast_to(row, (8, 128))


def split_rows(value):
    high = value.astype(bf16)
    low = (value - high.astype(f32)).astype(bf16)
    return jnp.concatenate([high, high, low], axis=0)


def dot3(matrix, value):
    return jnp.dot(matrix, split_rows(value), preferred_element_type=f32)


def dot6(matrix, value):
    high = value.astype(bf16)
    rest = value - high.astype(f32)
    middle = rest.astype(bf16)
    low = (rest - middle.astype(f32)).astype(bf16)
    terms = jnp.concatenate([high, middle, high, middle, low, high], axis=0)
    return jnp.dot(matrix, terms, preferred_element_type=f32)


def by_species(species, table):
    return jnp.where(species == 0, table[0], table[1])


def ghosts_of(chunk, index):
    first = chunk(0)
    rows = first.shape[0]
    lane = jnp.broadcast_to(index & 127, (rows, 128))
    part = jnp.broadcast_to(index >> 7, (rows, 128))
    out = lanes(first, lane)
    for k in range(1, CHUNKS):
        out = jnp.where(part == k, lanes(chunk(k), lane), out)
    return out


def tile_index(neighbours, g, a):
    index = neighbours[8 * g : 8 * g + 8, 128 * a : 128 * a + 128]
    return index & 127, [(index >> 7) == k for k in range(1, WINDOW)], index


def looked_up(rows, lane, masks):
    out = lanes(rows[0], lane)
    for k in range(1, WINDOW):
        out = jnp.where(masks[k - 1], lanes(rows[k], lane), out)
    return out


def cheap_by_lanes(table, neighbours, weights, a):
    rows = [[row8(table(x, k)) for k in range(WINDOW)] for x in range(3)]
    total = [jnp.zeros((8, 128), f32) for _ in range(3)]
    for g in range(SLOTS // 8):
        lane, masks, _ = tile_index(neighbours, g, a)
        offset = [looked_up(rows[x], lane, masks) - rows[x][1 + a] for x in range(3)]
        squared = offset[0] * offset[0] + offset[1] * offset[1] + offset[2] * offset[2]
        w = weights[8 * g : 8 * g + 8, 128 * a : 128 * a + 128] * jnp.exp(-squared)
        for x in range(3):
            total[x] = total[x] + w * offset[x]
    return [jnp.sum(t, axis=0, keepdims=True) for t in total]


def powers(squared):
    even = jnp.exp(-0.2 * squared)
    odd = jnp.exp(-(0.2 * 2.0**0.5) * squared)
    out = [even, odd]
    for _ in range(3):
        even, odd = even * even, odd * odd
        out += [even, odd]
    return out


def learned_by_lanes(table, neighbours, weights, w_in, w_out, offsets, messages, radials, store):
    for c in range(CB):
        for a in range(CHUNKS):
            rows = [[row8(table(c, x, k)) for k in range(WINDOW)] for x in range(3)]
            total = [jnp.zeros((8, 128), f32) for _ in range(NRBF)]
            for g in range(SLOTS // 8):
                lane, masks, _ = tile_index(neighbours, g, a)
                offset = [looked_up(rows[x], lane, masks) - rows[x][1 + a] for x in range(3)]
                squared = offset[0] * offset[0] + offset[1] * offset[1] + offset[2] * offset[2]
                for x in range(3):
                    offsets[c, a, g, x] = offset[x]
                w = weights[8 * g : 8 * g + 8, 128 * a : 128 * a + 128]
                for r, basis in enumerate(powers(squared)):
                    total[r] = total[r] + w * basis
            at = c * ATOMS + a * 128
            for r in range(NRBF):
                messages[r : r + 1, at : at + 128] = jnp.sum(total[r], axis=0, keepdims=True) * (1.0 / SLOTS)
    highest = lax.Precision.HIGHEST
    hidden = jnp.dot(w_in[...], messages[...], precision=highest, preferred_element_type=f32)
    hidden = hidden * (1.0 / (1.0 + jnp.exp(-hidden)))
    radials[...] = jnp.dot(w_out[...], hidden, precision=highest, preferred_element_type=f32)
    for c in range(CB):
        for a in range(CHUNKS):
            at = c * ATOMS + a * 128
            radial = [row8(radials[r : r + 1, at : at + 128]) for r in range(NRBF)]
            total = [jnp.zeros((8, 128), f32) for _ in range(3)]
            for g in range(SLOTS // 8):
                offset = [offsets[c, a, g, x] for x in range(3)]
                squared = offset[0] * offset[0] + offset[1] * offset[1] + offset[2] * offset[2]
                basis = powers(squared)
                profile = radial[0] * basis[0]
                for r in range(1, NRBF):
                    profile = profile + radial[r] * basis[r]
                w = weights[8 * g : 8 * g + 8, 128 * a : 128 * a + 128] * profile
                for x in range(3):
                    total[x] = total[x] + w * offset[x]
            for x in range(3):
                store(c, x, a, jnp.sum(total[x], axis=0, keepdims=True))


def cheap_by_matmul(coords, below, above, neighbours, weights, stacked, total):
    rows = 3 * BEADS
    parts = (
        jnp.concatenate([below[...], coords[:, 0:128]], axis=1),
        coords[:, 128:384],
        jnp.concatenate([coords[:, 384:512], above[...]], axis=1),
    )
    for k, part in enumerate(parts):
        high = part.astype(bf16)
        stacked[k * rows : (k + 1) * rows, 0:256] = high
        stacked[k * rows : (k + 1) * rows, 256:512] = (part - high.astype(f32)).astype(bf16)
    rounded = coords[...].astype(bf16).astype(f32)
    rounded = rounded + (coords[...] - rounded).astype(bf16).astype(f32)
    total[...] = jnp.zeros_like(total)
    unroll = 8
    place = lax.broadcasted_iota(jnp.int16, (256, ATOMS), 0)

    def group(i, _):
        for j in range(unroll):
            slot = i * unroll + j
            index = neighbours[pl.ds(slot, 1), :]
            column = jnp.broadcast_to(index & 255, (16, ATOMS)).astype(jnp.int16)
            chosen = jnp.where(place == jnp.tile(column, (16, 1)), bf16(1), bf16(0))
            picked = jnp.dot(
                stacked[...], jnp.concatenate([chosen, chosen], axis=0), preferred_element_type=f32
            )
            part = index >> 8
            other = jnp.where(
                part == 0,
                picked[0:rows],
                jnp.where(part == 1, picked[rows : 2 * rows], picked[2 * rows : 3 * rows]),
            )
            offset = other - rounded
            x, y, z = offset[0:BEADS], offset[BEADS : 2 * BEADS], offset[2 * BEADS :]
            w = weights[pl.ds(slot, 1), :] * jnp.exp(-(x * x + y * y + z * z))
            total[0:BEADS] += w * x
            total[BEADS : 2 * BEADS] += w * y
            total[2 * BEADS :] += w * z
        return 0

    lax.fori_loop(0, SLOTS // unroll, group, 0)


def propagated(coords, veloc, table, extra=None):
    wide = []
    for x in range(3):
        at = slice(x * BEADS, (x + 1) * BEADS)
        pieces = [coords[at], veloc[at]]
        if extra is not None:
            pieces.append(extra[x])
        wide.append(jnp.concatenate(pieces, axis=0))
    return dot6(table[...], jnp.concatenate(wide, axis=1))


def first_kernel(pos, mom, species, scale, mass_table, out):
    inverse = by_species(species[...], [1.0 / mass_table[0], 1.0 / mass_table[1]])
    for x in range(3):
        out[x : x + 1] = pos[x]
        out[3 + x : 4 + x] = mom[x] * inverse
    out[6:7] = by_species(species[...], scale)
    out[7:8] = inverse


def send_kernel(pair, ghost_rows, down, up, rows):
    rows[0:3] = pair[0, 0:3]
    rows[3:6] = pair[1, 0:3]
    rows[6:8] = pair[0, 6:8]
    chunk = lambda k: rows[:, 128 * k : 128 * k + 128]
    down[...] = ghosts_of(chunk, ghost_rows[0:1])
    up[...] = ghosts_of(chunk, ghost_rows[1:2])


def pack_kernel(pair, below, above, neighbours, out, weights, block, charges):
    charges[0:1] = below[6:7]
    for k in range(CHUNKS):
        charges[1 + k : 2 + k] = pair[0, 6:7, 128 * k : 128 * k + 128]
    charges[5:6] = above[6:7]
    for k in range(2):
        base = 32 * k
        for x in range(3):
            at = base + 6 * x
            block[at : at + 1] = below[3 * k + x : 3 * k + x + 1]
            for i in range(CHUNKS):
                block[at + 1 + i : at + 2 + i] = pair[k, x : x + 1, 128 * i : 128 * i + 128]
            block[at + 5 : at + 6] = above[3 * k + x : 3 * k + x + 1]
        block[base + 30 : base + 32] = jnp.zeros((2, 128), f32)
    for a in range(CHUNKS):
        itself = 128 + 128 * a + lax.broadcasted_iota(jnp.int32, (8, 128), 1)
        rows = [row8(charges[k : k + 1]) for k in range(WINDOW)]
        for g in range(SLOTS // 8):
            lane, masks, index = tile_index(neighbours, g, a)
            q = looked_up(rows, lane, masks)
            weights[8 * g : 8 * g + 8, 128 * a : 128 * a + 128] = jnp.where(index == itself, 0.0, q)
    for a in range(CHUNKS):
        at = slice(128 * a, 128 * a + 128)
        gain = pair[0, 6:7, at] * pair[0, 7:8, at] * (0.5 * inner_step)
        for k in range(2):
            base = 32 * k
            force = cheap_by_lanes(
                lambda x, w: block[base + 6 * x + w : base + 6 * x + w + 1], neighbours, weights, a
            )
            for x in range(3):
                row = base + 18 + 4 * x + a
                block[row : row + 1] = pair[k, 3 + x : 4 + x, at] + gain * force[x]
    for i in range(16):
        out[i] = block[...]


def begin_kernel(
    gathered, neighbours, weights, species, mass_table, ghost_rows, w_in, w_out, first, reduce_,
    coords, veloc, down, up,
    window, start, contracted, offsets, messages, radials, slow,
):
    inverse = by_species(species[...], [1.0 / mass_table[0], 1.0 / mass_table[1]])
    for z in range(2):
        for x in range(3):
            at = slice(x * BEADS + 16 * z, x * BEADS + 16 * z + 16)
            for k in range(WINDOW):
                window[at, 128 * k : 128 * k + 128] = gathered[:, 32 * z + 6 * x + k, :]
            for k in range(CHUNKS):
                start[at, 128 * k : 128 * k + 128] = gathered[:, 32 * z + 18 + 4 * x + k, :]
    for x in range(3):
        contracted[x] = dot3(reduce_[...], window[x * BEADS : (x + 1) * BEADS, :])
    slow[...] = jnp.zeros_like(slow)

    def store(c, x, a, value):
        slow[x, c : c + 1, 128 * a : 128 * a + 128] = value

    learned_by_lanes(
        lambda c, x, k: contracted[x, c : c + 1, 128 * k : 128 * k + 128],
        neighbours, weights, w_in, w_out, offsets, messages, radials, store,
    )
    moved = propagated(
        window[:, 128:640], start[...], first, [slow[x] * inverse for x in range(3)]
    )
    finish_step(moved, coords, veloc, ghost_rows, down, up)


def finish_step(moved, coords, veloc, ghost_rows, down, up):
    for x in range(3):
        at = slice(x * BEADS, (x + 1) * BEADS)
        coords[at] = moved[0:BEADS, ATOMS * x : ATOMS * (x + 1)]
        veloc[at] = moved[BEADS : 2 * BEADS, ATOMS * x : ATOMS * (x + 1)]
    for i in range(3 * BEADS // 8):
        chunk = lambda k: coords[8 * i : 8 * i + 8, 128 * k : 128 * k + 128]
        down[8 * i : 8 * i + 8] = ghosts_of(chunk, ghost_rows[0:1])
        up[8 * i : 8 * i + 8] = ghosts_of(chunk, ghost_rows[1:2])


def kicked(coords, veloc, below, above, neighbours, weights, species, scale, mass_table, stacked, total):
    cheap_by_matmul(coords, below, above, neighbours, weights, stacked, total)
    gain = by_species(species[...], [scale[0] / mass_table[0], scale[1] / mass_table[1]]) * inner_step
    return veloc[...] + gain * total[...]


def middle_kernel(
    coords, veloc, below, above, neighbours, weights, species, scale, mass_table, ghost_rows, later,
    new_coords, new_veloc, down, up, stacked, total,
):
    velocities = kicked(
        coords, veloc, below, above, neighbours, weights, species, scale, mass_table, stacked, total
    )
    moved = propagated(coords[...], velocities, later)
    finish_step(moved, new_coords, new_veloc, ghost_rows, down, up)


def last_kernel(
    place, coords, veloc, below, above, neighbours, weights, species, scale, mass_table, ghost_rows, later,
    reduce_, own, contracted, down, up, stacked, total, moved, rows,
):
    velocities = kicked(
        coords, veloc, below, above, neighbours, weights, species, scale, mass_table, stacked, total
    )
    moved[...] = propagated(coords[...], velocities, later)
    small = dot3(reduce_[...], moved[0:BEADS, :])
    for x in range(3):
        at = slice(ATOMS * x, ATOMS * (x + 1))
        own[x : x + 1] = moved[pl.ds(place[1], 1), at]
        own[3 + x : 4 + x] = moved[pl.ds(BEADS + place[1], 1), at]
        contracted[4 * x : 4 * x + 4] = small[0:4, at]
    own[6:8] = jnp.zeros((2, ATOMS), f32)
    contracted[12:16] = jnp.zeros((4, ATOMS), f32)
    rows[0:12] = contracted[0:12]
    for which, out in ((2, down), (3, up)):
        for x in range(3):
            rows[12 + x : 13 + x] = moved[pl.ds(place[which], 1), ATOMS * x : ATOMS * (x + 1)]
        rows[15:16] = contracted[12:13]
        index = ghost_rows[which - 2 : which - 1]
        for i in range(2):
            out[8 * i : 8 * i + 8] = ghosts_of(
                lambda k: rows[8 * i : 8 * i + 8, 128 * k : 128 * k + 128], index
            )


def end_kernel(
    place, expand, own, contracted, below, above, neighbours, weights, species, scale, mass_table, w_in, w_out,
    new_pos, new_mom,
    window, offsets, messages, radials, slow,
):
    charge = by_species(species[...], scale)
    mass = by_species(species[...], mass_table)
    window[0:16, 0:128] = below[...]
    window[0:16, 640:768] = above[...]
    window[0:12, 128:640] = contracted[0:12]
    window[12:15, 128:640] = own[0:3]

    def store(c, x, a, value):
        slow[c, x, a : a + 1] = value

    learned_by_lanes(
        lambda c, x, k: window[4 * x + c : 4 * x + c + 1, 128 * k : 128 * k + 128],
        neighbours, weights, w_in, w_out, offsets, messages, radials, store,
    )
    for a in range(CHUNKS):
        force = cheap_by_lanes(
            lambda x, k: window[12 + x : 13 + x, 128 * k : 128 * k + 128], neighbours, weights, a
        )
        at = slice(128 * a, 128 * a + 128)
        for x in range(3):
            value = mass[:, at] * own[3 + x : 4 + x, at] + (0.5 * inner_step) * charge[:, at] * force[x]
            for c in range(CB):
                value = value + expand[place[1], c] * slow[c, x, a : a + 1]
            new_mom[x, :, at] = value
            new_pos[x, :, at] = own[x : x + 1, at]


def call(kernel, outs, scratch, args, scalars):
    specs = [
        pl.BlockSpec(memory_space=pltpu.SMEM if i in scalars else pltpu.VMEM) for i in range(len(args))
    ]
    shapes = [jax.ShapeDtypeStruct(s, f32) for s in outs]
    return pl.pallas_call(
        kernel,
        out_shape=shapes,
        in_specs=specs,
        out_specs=[pl.BlockSpec(memory_space=pltpu.VMEM)] * len(outs),
        scratch_shapes=[pltpu.VMEM(s, d) for s, d in scratch],
        compiler_params=pltpu.CompilerParams(vmem_limit_bytes=VMEM_LIMIT),
    )(*args)


RING = ("bead", "space")


def ring(step):
    pairs = []
    for bead in range(BEADS):
        for domain in range(N_SPACE):
            to = domain + step
            other = bead if 0 <= to < N_SPACE else bead ^ 4
            pairs.append((bead * N_SPACE + domain, other * N_SPACE + to % N_SPACE))
    return pairs


def exchange(down, up):
    below = lax.ppermute(up, RING, ring(1))
    above = lax.ppermute(down, RING, ring(-1))
    return below, above


def body(
    positions, momenta, neighbours, ghost_rows, species, species_scale, mass_table, w_in, w_out
):
    first, later, reduce_, expand = tables()
    first, later, reduce_ = (jnp.asarray(t) for t in (first, later, reduce_))
    expand = jnp.asarray(expand)
    bead = lax.axis_index("bead")
    domain = lax.axis_index("space")
    half = (bead // 4) % 2
    row = half * 16 + (bead // 8) * 4 + bead % 4
    other = (1 - half) * 16 + (bead // 8) * 4 + bead % 4
    row_below = jnp.where(domain == 0, other, row)
    row_above = jnp.where(domain == N_SPACE - 1, other, row)
    place = jnp.stack([half, row, row_below, row_above]).astype(jnp.int32)

    pos = positions.transpose(1, 0, 2)
    mom = momenta.transpose(1, 0, 2)
    kinds = species.reshape(1, ATOMS)
    ghosts = ghost_rows.reshape(2, 128)

    (mine,) = call(first_kernel, [(8, ATOMS)], [], (pos, mom, kinds, species_scale, mass_table), (3, 4))
    halves = [[x * 8 + z * 4 + y for z in range(2)] for x in range(4) for y in range(4)]
    pair = lax.all_gather(mine, "bead", axis=0, axis_index_groups=halves)
    down, up = call(send_kernel, [(8, 128)] * 2, [((8, ATOMS), f32)], (pair, ghosts), ())
    below, above = exchange(down, up)
    block, weights = call(
        pack_kernel,
        [(16, 64, 128), (SLOTS, ATOMS)],
        [((64, 128), f32), ((8, 128), f32)],
        (pair, below, above, neighbours),
        (),
    )
    groups = [[x * 8 + z * 4 + y for x in range(4) for y in range(4)] for z in range(2)]
    gathered = lax.all_to_all(block, "bead", 0, 0, axis_index_groups=groups, tiled=True)
    offsets = ((CB, CHUNKS, SLOTS // 8, 3, 8, 128), f32)
    coords, veloc, down, up = call(
        begin_kernel,
        [(96, ATOMS), (96, ATOMS), (96, 128), (96, 128)],
        [
            ((96, 768), f32), ((96, ATOMS), f32), ((3, 16, 768), f32), offsets, ((NRBF, CB * ATOMS), f32),
            ((NRBF, CB * ATOMS), f32), ((3, 16, ATOMS), f32),
        ],
        (gathered, neighbours, weights, kinds, mass_table, ghosts, w_in, w_out, first, reduce_),
        (4,),
    )
    big = [((3 * 96, 512), bf16), ((96, ATOMS), f32)]
    below, above = exchange(down, up)
    coords, veloc, down, up = call(
        middle_kernel,
        [(96, ATOMS), (96, ATOMS), (96, 128), (96, 128)],
        big,
        (coords, veloc, below, above, neighbours, weights, kinds, species_scale, mass_table, ghosts, later),
        (7, 8),
    )
    below, above = exchange(down, up)
    own, contracted, down, up = call(
        last_kernel,
        [(8, ATOMS), (16, ATOMS), (16, 128), (16, 128)],
        big + [((2 * BEADS, 3 * ATOMS), f32), ((16, ATOMS), f32)],
        (place, coords, veloc, below, above, neighbours, weights, kinds, species_scale, mass_table, ghosts, later, reduce_),
        (0, 8, 9),
    )
    below, above = exchange(down, up)
    new_pos, new_mom = call(
        end_kernel,
        [(3, 1, ATOMS), (3, 1, ATOMS)],
        [
            ((16, 768), f32), offsets, ((NRBF, CB * ATOMS), f32), ((NRBF, CB * ATOMS), f32),
            ((CB, 3, CHUNKS, 128), f32),
        ],
        (place, expand, own, contracted, below, above, neighbours, weights, kinds, species_scale, mass_table, w_in, w_out),
        (0, 1, 9, 10),
    )
    return new_pos.transpose(1, 0, 2), new_mom.transpose(1, 0, 2)


def solution(mesh):
    in_specs = (
        P("bead", None, "space"),
        P("bead", None, "space"),
        P(None, "space"),
        P("space"),
        P("space"),
        P(),
        P(),
        P(),
        P(),
    )
    out_specs = (P("bead", None, "space"), P("bead", None, "space"))
    return jax.shard_map(body, mesh=mesh, in_specs=in_specs, out_specs=out_specs, check_vma=False)
```

```python
import functools

import jax
import jax.numpy as jnp
import numpy as np
from jax import lax
from jax.experimental import pallas as pl
from jax.experimental.pallas import tpu as pltpu
from jax.sharding import PartitionSpec as P

BEADS = 32
CB = 4
NINNER = 3
NRBF = 8
H = 128
SLOTS = 32
ATOMS = 512
CHUNKS = 4
WINDOW = 6
N_SPACE = 16

polymer_freq = 10.0
outer_step = 6.0
inner_step = outer_step / NINNER
f32 = jnp.float32
bf16 = jnp.bfloat16
VMEM_LIMIT = 12 * 1024 * 1024


def mode_matrix(count):
    beadpos = np.arange(count)[None, :]
    modeidx = np.arange(count)[:, None]
    middle = count // 2
    cosine = np.sqrt(2.0 / count) * np.cos(2.0 * np.pi * beadpos * modeidx / count)
    sine_rows = np.sqrt(2.0 / count) * np.sin(2.0 * np.pi * beadpos * modeidx / count)
    matrix = np.where(modeidx < middle, cosine, sine_rows)
    matrix = np.where(modeidx == 0, 1.0 / np.sqrt(count), matrix)
    matrix = np.where(modeidx == middle, np.cos(np.pi * beadpos) / np.sqrt(count), matrix)
    return matrix


def polymer_tables(count):
    modes = mode_matrix(count)
    frequency = 2.0 * polymer_freq * np.sin(np.pi * np.arange(count) / count)
    nonzero = np.where(frequency > 0, frequency, 1.0)
    cosine = np.cos(frequency * inner_step)
    drift_gain = np.where(frequency > 0, np.sin(frequency * inner_step) / nonzero, inner_step)
    spring = frequency * np.sin(frequency * inner_step)
    persist = modes.T @ (cosine[:, None] * modes)
    coupling = modes.T @ (drift_gain[:, None] * modes)
    restoring = -(modes.T @ (spring[:, None] * modes))
    return persist, coupling, restoring


def contraction(count, fewer):
    full_modes = mode_matrix(count)
    small_modes = mode_matrix(fewer)
    kept = list(range(fewer // 2 + 1)) + list(range(count - fewer // 2 + 1, count))
    contract = np.sqrt(fewer / count) * (small_modes.T @ full_modes[kept])
    expand = count / fewer * contract.T
    return contract, expand


def bf16_terms(matrix):
    out, rest = [], matrix
    for _ in range(3):
        out.append(rest.astype(np.float32).astype(jnp.bfloat16))
        rest = rest - out[-1].astype(np.float64)
    return out


def three_terms(matrix):
    high, low, _ = bf16_terms(matrix)
    return np.concatenate([high, low, high], axis=1)


def six_terms(matrix):
    high, middle, low = bf16_terms(matrix)
    return np.concatenate([high, high, middle, middle, high, low], axis=1)


BEAD_OF_ROW = np.array([x * 8 + z * 4 + y for z in range(2) for x in range(4) for y in range(4)])


def tables():
    persist, coupling, restoring = polymer_tables(BEADS)
    contract, expand = contraction(BEADS, CB)
    order = BEAD_OF_ROW
    persist, coupling, restoring = (m[np.ix_(order, order)] for m in (persist, coupling, restoring))
    contract, expand = contract[:, order], expand[order]
    step = np.block([[persist, coupling], [restoring, persist]])
    padded_expand = np.concatenate([expand, np.zeros((BEADS, 16 - CB))], axis=1)
    kick = np.concatenate([coupling @ padded_expand, persist @ padded_expand], axis=0)
    first = six_terms(np.concatenate([step, 0.5 * outer_step * kick], axis=1))
    later = six_terms(step)
    reduce_ = three_terms(np.concatenate([contract, np.zeros((16 - CB, BEADS))], axis=0))
    return first, later, reduce_, (0.5 * outer_step * expand).astype(np.float32)


def lanes(source, index):
    return jnp.take_along_axis(source, index, axis=1)


def row8(row):
    return jnp.broadcast_to(row, (8, 128))


def split_rows(value):
    high = value.astype(bf16)
    low = (value - high.astype(f32)).astype(bf16)
    return jnp.concatenate([high, high, low], axis=0)


def dot3(matrix, value):
    return jnp.dot(matrix, split_rows(value), preferred_element_type=f32)


def dot6(matrix, value):
    high = value.astype(bf16)
    rest = value - high.astype(f32)
    middle = rest.astype(bf16)
    low = (rest - middle.astype(f32)).astype(bf16)
    terms = jnp.concatenate([high, middle, high, middle, low, high], axis=0)
    return jnp.dot(matrix, terms, preferred_element_type=f32)


def by_species(species, table):
    return jnp.where(species == 0, table[0], table[1])


def ghosts_of(chunk, index):
    first = chunk(0)
    rows = first.shape[0]
    lane = jnp.broadcast_to(index & 127, (rows, 128))
    part = jnp.broadcast_to(index >> 7, (rows, 128))
    out = lanes(first, lane)
    for k in range(1, CHUNKS):
        out = jnp.where(part == k, lanes(chunk(k), lane), out)
    return out


def tile_index(neighbours, g, a):
    index = neighbours[8 * g : 8 * g + 8, 128 * a : 128 * a + 128]
    return index & 127, [(index >> 7) == k for k in range(1, WINDOW)], index


def looked_up(rows, lane, masks):
    out = lanes(rows[0], lane)
    for k in range(1, WINDOW):
        out = jnp.where(masks[k - 1], lanes(rows[k], lane), out)
    return out


def cheap_by_lanes(table, neighbours, weights, a):
    rows = [[row8(table(x, k)) for k in range(WINDOW)] for x in range(3)]
    total = [jnp.zeros((8, 128), f32) for _ in range(3)]
    for g in range(SLOTS // 8):
        lane, masks, _ = tile_index(neighbours, g, a)
        offset = [looked_up(rows[x], lane, masks) - rows[x][1 + a] for x in range(3)]
        squared = offset[0] * offset[0] + offset[1] * offset[1] + offset[2] * offset[2]
        w = weights[8 * g : 8 * g + 8, 128 * a : 128 * a + 128] * jnp.exp(-squared)
        for x in range(3):
            total[x] = total[x] + w * offset[x]
    return [jnp.sum(t, axis=0, keepdims=True) for t in total]


def powers(squared):
    even = jnp.exp(-0.2 * squared)
    odd = jnp.exp(-(0.2 * 2.0**0.5) * squared)
    out = [even, odd]
    for _ in range(3):
        even, odd = even * even, odd * odd
        out += [even, odd]
    return out


def learned_by_lanes(table, neighbours, weights, w_in, w_out, offsets, messages, radials, store):
    high = w_in[...].astype(bf16).astype(f32)
    first = jnp.concatenate([high, w_in[...] - high, high, jnp.zeros_like(high)], axis=0).astype(bf16)
    high = w_out[...].astype(bf16).astype(f32)
    second = jnp.concatenate([high, w_out[...] - high, high], axis=1)
    second = jnp.concatenate([second, jnp.zeros_like(second)], axis=0).astype(bf16)

    def message(c):
        for a in range(CHUNKS):
            rows = [[row8(table(c, x, k)) for k in range(WINDOW)] for x in range(3)]
            total = [jnp.zeros((8, 128), f32) for _ in range(NRBF)]
            for g in range(SLOTS // 8):
                lane, masks, _ = tile_index(neighbours, g, a)
                offset = [looked_up(rows[x], lane, masks) - rows[x][1 + a] for x in range(3)]
                squared = offset[0] * offset[0] + offset[1] * offset[1] + offset[2] * offset[2]
                for x in range(3):
                    offsets[c, a, g, x] = offset[x]
                w = weights[8 * g : 8 * g + 8, 128 * a : 128 * a + 128]
                for r, basis in enumerate(powers(squared)):
                    total[r] = total[r] + w * basis
            for r in range(NRBF):
                messages[c, r : r + 1, 128 * a : 128 * a + 128] = jnp.sum(total[r], axis=0, keepdims=True) * (
                    1.0 / SLOTS
                )

    def network(c):
        value = messages[c]
        high = value.astype(bf16).astype(f32)
        terms = jnp.concatenate([high, high, value - high, jnp.zeros_like(high)], axis=0).astype(bf16)
        hidden = lax.dot_general(first, terms, (((0,), (0,)), ((), ())), preferred_element_type=f32)
        hidden = hidden * (1.0 / (1.0 + jnp.exp(-hidden)))
        radials[c] = jnp.dot(second, split_rows(hidden), preferred_element_type=f32)[0:NRBF]

    def force(c):
        for a in range(CHUNKS):
            radial = [row8(radials[c, r : r + 1, 128 * a : 128 * a + 128]) for r in range(NRBF)]
            total = [jnp.zeros((8, 128), f32) for _ in range(3)]
            for g in range(SLOTS // 8):
                offset = [offsets[c, a, g, x] for x in range(3)]
                squared = offset[0] * offset[0] + offset[1] * offset[1] + offset[2] * offset[2]
                basis = powers(squared)
                profile = radial[0] * basis[0]
                for r in range(1, NRBF):
                    profile = profile + radial[r] * basis[r]
                w = weights[8 * g : 8 * g + 8, 128 * a : 128 * a + 128] * profile
                for x in range(3):
                    total[x] = total[x] + w * offset[x]
            for x in range(3):
                store(c, x, a, jnp.sum(total[x], axis=0, keepdims=True))

    message(0)
    for c in range(CB):
        network(c)
        if c + 1 < CB:
            message(c + 1)
        force(c)


def cheap_of_all(coords, below, above, neighbours, weights, stacked, total, table, sums):
    few = BEADS - 8
    rows = 3 * few

    def of_few(value):
        return jnp.concatenate([value[BEADS * x : BEADS * x + few] for x in range(3)], axis=0)

    own, low, high_ = of_few(coords), of_few(below), of_few(above)
    stack = jnp.concatenate(
        [
            jnp.concatenate([low, own[:, 0:128]], axis=1),
            own[:, 128:384],
            jnp.concatenate([own[:, 384:512], high_], axis=1),
            jnp.zeros((8, 256), f32),
        ],
        axis=0,
    )
    high = stack.astype(bf16)
    stacked[:, 0:256] = high
    stacked[:, 256:512] = (stack - high.astype(f32)).astype(bf16)
    rounded = own.astype(bf16).astype(f32)
    rounded = rounded + (own - rounded).astype(bf16).astype(f32)
    for x in range(3):
        at = slice(BEADS * x + few, BEADS * (x + 1))
        table[8 * x : 8 * x + 8, 0:128] = below[at]
        table[8 * x : 8 * x + 8, 128:640] = coords[at]
        table[8 * x : 8 * x + 8, 640:768] = above[at]
    total[...] = jnp.zeros_like(total)
    sums[...] = jnp.zeros_like(sums)
    place = lax.broadcasted_iota(jnp.int16, (256, ATOMS), 0)

    def by_matmul(slot):
        index = neighbours[pl.ds(slot, 1), :]
        column = jnp.broadcast_to(index & 255, (16, ATOMS)).astype(jnp.int16)
        chosen = jnp.where(place == jnp.tile(column, (16, 1)), bf16(1), bf16(0))
        picked = jnp.dot(stacked[...], jnp.concatenate([chosen, chosen], axis=0), preferred_element_type=f32)
        part = index >> 8
        other = jnp.where(
            part == 0,
            picked[0:rows],
            jnp.where(part == 1, picked[rows : 2 * rows], picked[2 * rows : 3 * rows]),
        )
        offset = other - rounded
        x, y, z = offset[0:few], offset[few : 2 * few], offset[2 * few :]
        w = weights[pl.ds(slot, 1), :] * jnp.exp(-(x * x + y * y + z * z))
        total[0:few] += w * x
        total[BEADS : BEADS + few] += w * y
        total[2 * BEADS : 2 * BEADS + few] += w * z

    def by_lanes(g, a):
        at = slice(128 * a, 128 * a + 128)
        slots = pl.ds(pl.multiple_of(8 * g, 8), 8)
        index = neighbours[slots, at]
        lane, masks = index & 127, [(index >> 7) == k for k in range(1, WINDOW)]
        weight = weights[slots, at]
        for bead in range(8):
            rows_of = lambda x, k: row8(table[8 * x + bead : 8 * x + bead + 1, 128 * k : 128 * k + 128])
            offset = [
                looked_up([rows_of(x, k) for k in range(WINDOW)], lane, masks) - rows_of(x, 1 + a)
                for x in range(3)
            ]
            w = weight * jnp.exp(-(offset[0] * offset[0] + offset[1] * offset[1] + offset[2] * offset[2]))
            for x in range(3):
                sums[8 * x + bead, :, at] += w * offset[x]

    def group(g, _):
        for j in range(8):
            by_matmul(g * 8 + j)
            if j % 2:
                by_lanes(g, j // 2)
        return 0

    lax.fori_loop(0, SLOTS // 8, group, 0)
    for x in range(3):
        for bead in range(8):
            row = BEADS * x + few + bead
            total[row : row + 1] = jnp.sum(sums[8 * x + bead], axis=0, keepdims=True)


def propagated(coords, veloc, table, extra=None):
    wide = []
    for x in range(3):
        at = slice(x * BEADS, (x + 1) * BEADS)
        pieces = [coords[at], veloc[at]]
        if extra is not None:
            pieces.append(extra[x])
        wide.append(jnp.concatenate(pieces, axis=0))
    return dot6(table[...], jnp.concatenate(wide, axis=1))


def first_kernel(
    pos, mom, species, ghost_rows, scale, mass_table, out, ghosts, pos_in, mom_in, species_in, scale_in, mass_in, sems
):
    copies = [
        pltpu.make_async_copy(source, target, sems.at[i])
        for i, (source, target) in enumerate(
            (
                (scale, scale_in), (mass_table, mass_in), (species, species_in), (mom, mom_in), (pos, pos_in),
                (ghost_rows, ghosts),
            )
        )
    ]
    for copy in copies:
        copy.start()
    for copy in copies:
        copy.wait()
    mass = by_species(species_in[...], mass_in)
    for x in range(3):
        out[x : x + 1] = pos_in[x]
        out[3 + x : 4 + x] = mom_in[x] / mass
    out[6:7] = by_species(species_in[...], scale_in)
    out[7:8] = mass


def send_kernel(pair, ghost_rows, down, up, rows):
    rows[0:3] = pair[0, 0:3]
    rows[3:6] = pair[1, 0:3]
    rows[6:8] = pair[0, 6:8]
    chunk = lambda k: rows[:, 128 * k : 128 * k + 128]
    down[...] = ghosts_of(chunk, ghost_rows[0:1])
    up[...] = ghosts_of(chunk, ghost_rows[1:2])


def pack_kernel(pair, below, above, neighbours, out, weights, block, charges):
    charges[0:1] = below[6:7]
    for k in range(CHUNKS):
        charges[1 + k : 2 + k] = pair[0, 6:7, 128 * k : 128 * k + 128]
    charges[5:6] = above[6:7]
    for k in range(2):
        base = 32 * k
        for x in range(3):
            at = base + 6 * x
            block[at : at + 1] = below[3 * k + x : 3 * k + x + 1]
            for i in range(CHUNKS):
                block[at + 1 + i : at + 2 + i] = pair[k, x : x + 1, 128 * i : 128 * i + 128]
            block[at + 5 : at + 6] = above[3 * k + x : 3 * k + x + 1]
        block[base + 30 : base + 32] = jnp.zeros((2, 128), f32)
    for a in range(CHUNKS):
        itself = 128 + 128 * a + lax.broadcasted_iota(jnp.int32, (8, 128), 1)
        rows = [row8(charges[k : k + 1]) for k in range(WINDOW)]
        for g in range(SLOTS // 8):
            lane, masks, index = tile_index(neighbours, g, a)
            q = looked_up(rows, lane, masks)
            weights[8 * g : 8 * g + 8, 128 * a : 128 * a + 128] = jnp.where(index == itself, 0.0, q)
    for a in range(CHUNKS):
        at = slice(128 * a, 128 * a + 128)
        gain = pair[0, 6:7, at] / pair[0, 7:8, at] * (0.5 * inner_step)
        for k in range(2):
            base = 32 * k
            force = cheap_by_lanes(
                lambda x, w: block[base + 6 * x + w : base + 6 * x + w + 1], neighbours, weights, a
            )
            for x in range(3):
                row = base + 18 + 4 * x + a
                block[row : row + 1] = pair[k, 3 + x : 4 + x, at] + gain * force[x]
    for i in range(16):
        out[i] = block[...]


def begin_kernel(
    gathered, neighbours, weights, mine, ghost_rows, w_in, w_out, first, reduce_,
    coords, veloc, down, up,
    window, start, contracted, offsets, messages, radials, slow,
):
    inverse = 1.0 / mine[7:8]
    for z in range(2):
        for x in range(3):
            at = slice(x * BEADS + 16 * z, x * BEADS + 16 * z + 16)
            for k in range(WINDOW):
                window[at, 128 * k : 128 * k + 128] = gathered[:, 32 * z + 6 * x + k, :]
            for k in range(CHUNKS):
                start[at, 128 * k : 128 * k + 128] = gathered[:, 32 * z + 18 + 4 * x + k, :]
    for x in range(3):
        contracted[x] = dot3(reduce_[...], window[x * BEADS : (x + 1) * BEADS, :])
    slow[...] = jnp.zeros_like(slow)

    def store(c, x, a, value):
        slow[x, c : c + 1, 128 * a : 128 * a + 128] = value

    learned_by_lanes(
        lambda c, x, k: contracted[x, c : c + 1, 128 * k : 128 * k + 128],
        neighbours, weights, w_in, w_out, offsets, messages, radials, store,
    )
    moved = propagated(
        window[:, 128:640], start[...], first, [slow[x] * inverse for x in range(3)]
    )
    finish_step(moved, coords, veloc, ghost_rows, down, up)


def finish_step(moved, coords, veloc, ghost_rows, down, up):
    for x in range(3):
        at = slice(x * BEADS, (x + 1) * BEADS)
        coords[at] = moved[0:BEADS, ATOMS * x : ATOMS * (x + 1)]
        veloc[at] = moved[BEADS : 2 * BEADS, ATOMS * x : ATOMS * (x + 1)]
    for i in range(3 * BEADS // 8):
        chunk = lambda k: coords[8 * i : 8 * i + 8, 128 * k : 128 * k + 128]
        down[8 * i : 8 * i + 8] = ghosts_of(chunk, ghost_rows[0:1])
        up[8 * i : 8 * i + 8] = ghosts_of(chunk, ghost_rows[1:2])


def kicked(coords, veloc, below, above, neighbours, weights, mine, scratch):
    total = scratch[1]
    cheap_of_all(coords, below, above, neighbours, weights, *scratch)
    return veloc[...] + inner_step * mine[6:7] / mine[7:8] * total[...]


def middle_kernel(
    coords, veloc, below, above, neighbours, weights, mine, ghost_rows, later, new_coords, new_veloc, down, up, *scratch
):
    velocities = kicked(coords, veloc, below, above, neighbours, weights, mine, scratch)
    moved = propagated(coords[...], velocities, later)
    finish_step(moved, new_coords, new_veloc, ghost_rows, down, up)


def last_kernel(
    place, coords, veloc, below, above, neighbours, weights, mine, ghost_rows, later, reduce_,
    own, contracted, down, up, moved, rows, *scratch,
):
    velocities = kicked(coords, veloc, below, above, neighbours, weights, mine, scratch)
    moved[...] = propagated(coords[...], velocities, later)
    small = dot3(reduce_[...], moved[0:BEADS, :])
    for x in range(3):
        at = slice(ATOMS * x, ATOMS * (x + 1))
        own[x : x + 1] = moved[pl.ds(place[1], 1), at]
        own[3 + x : 4 + x] = moved[pl.ds(BEADS + place[1], 1), at]
        contracted[4 * x : 4 * x + 4] = small[0:4, at]
    own[6:8] = mine[6:8]
    contracted[12:16] = jnp.zeros((4, ATOMS), f32)
    rows[0:12] = contracted[0:12]
    for which, out in ((2, down), (3, up)):
        for x in range(3):
            rows[12 + x : 13 + x] = moved[pl.ds(place[which], 1), ATOMS * x : ATOMS * (x + 1)]
        rows[15:16] = contracted[12:13]
        index = ghost_rows[which - 2 : which - 1]
        for i in range(2):
            out[8 * i : 8 * i + 8] = ghosts_of(
                lambda k: rows[8 * i : 8 * i + 8, 128 * k : 128 * k + 128], index
            )


def end_kernel(
    place, expand, own, contracted, below, above, neighbours, weights, w_in, w_out,
    new_pos, new_mom,
    window, offsets, messages, radials, slow,
):
    charge, mass = own[6:7], own[7:8]
    window[0:16, 0:128] = below[...]
    window[0:16, 640:768] = above[...]
    window[0:12, 128:640] = contracted[0:12]
    window[12:15, 128:640] = own[0:3]

    def store(c, x, a, value):
        slow[c, x, a : a + 1] = value

    learned_by_lanes(
        lambda c, x, k: window[4 * x + c : 4 * x + c + 1, 128 * k : 128 * k + 128],
        neighbours, weights, w_in, w_out, offsets, messages, radials, store,
    )
    for a in range(CHUNKS):
        force = cheap_by_lanes(
            lambda x, k: window[12 + x : 13 + x, 128 * k : 128 * k + 128], neighbours, weights, a
        )
        at = slice(128 * a, 128 * a + 128)
        for x in range(3):
            value = mass[:, at] * own[3 + x : 4 + x, at] + (0.5 * inner_step) * charge[:, at] * force[x]
            for c in range(CB):
                value = value + expand[place[1], c] * slow[c, x, a : a + 1]
            new_mom[x, :, at] = value
            new_pos[x, :, at] = own[x : x + 1, at]


def call(kernel, outs, scratch, args, scalars=(), space=pltpu.VMEM):
    specs = [pl.BlockSpec(memory_space=pltpu.SMEM if i in scalars else space) for i in range(len(args))]
    shapes = [s if isinstance(s, jax.ShapeDtypeStruct) else jax.ShapeDtypeStruct(s, f32) for s in outs]
    return pl.pallas_call(
        kernel,
        out_shape=shapes,
        in_specs=specs,
        out_specs=[pl.BlockSpec(memory_space=pltpu.VMEM)] * len(outs),
        scratch_shapes=[pltpu.VMEM(*s) if isinstance(s, tuple) else s for s in scratch],
        compiler_params=pltpu.CompilerParams(vmem_limit_bytes=VMEM_LIMIT),
    )(*args)


RING = ("bead", "space")


def ring(step):
    pairs = []
    for bead in range(BEADS):
        for domain in range(N_SPACE):
            to = domain + step
            other = bead if 0 <= to < N_SPACE else bead ^ 4
            pairs.append((bead * N_SPACE + domain, other * N_SPACE + to % N_SPACE))
    return pairs


def exchange(down, up):
    below = lax.ppermute(up, RING, ring(1))
    above = lax.ppermute(down, RING, ring(-1))
    return below, above


def body(
    positions, momenta, neighbours, ghost_rows, species, species_scale, mass_table, w_in, w_out
):
    first, later, reduce_, expand = tables()
    first, later, reduce_ = (jnp.asarray(t) for t in (first, later, reduce_))
    expand = jnp.asarray(expand)
    bead = lax.axis_index("bead")
    domain = lax.axis_index("space")
    half = (bead // 4) % 2
    row = half * 16 + (bead // 8) * 4 + bead % 4
    other = (1 - half) * 16 + (bead // 8) * 4 + bead % 4
    row_below = jnp.where(domain == 0, other, row)
    row_above = jnp.where(domain == N_SPACE - 1, other, row)
    place = jnp.stack([half, row, row_below, row_above]).astype(jnp.int32)

    pos = positions.transpose(1, 0, 2)
    mom = momenta.transpose(1, 0, 2)
    kinds = species.reshape(1, ATOMS)
    ghosts = ghost_rows.reshape(2, 128)

    mine, ghosts = call(
        first_kernel,
        [(8, ATOMS), jax.ShapeDtypeStruct((2, 128), jnp.int32)],
        [
            ((3, 1, ATOMS), f32), ((3, 1, ATOMS), f32), ((1, ATOMS), jnp.int32),
            pltpu.SMEM((2,), f32), pltpu.SMEM((2,), f32), pltpu.SemaphoreType.DMA((6,)),
        ],
        (pos, mom, kinds, ghosts, species_scale, mass_table),
        space=pltpu.HBM,
    )
    halves = [[x * 8 + z * 4 + y for z in range(2)] for x in range(4) for y in range(4)]
    pair = lax.all_gather(mine, "bead", axis=0, axis_index_groups=halves)
    down, up = call(send_kernel, [(8, 128)] * 2, [((8, ATOMS), f32)], (pair, ghosts), ())
    below, above = exchange(down, up)
    block, weights = call(
        pack_kernel,
        [(16, 64, 128), (SLOTS, ATOMS)],
        [((64, 128), f32), ((8, 128), f32)],
        (pair, below, above, neighbours),
        (),
    )
    groups = [[x * 8 + z * 4 + y for x in range(4) for y in range(4)] for z in range(2)]
    gathered = lax.all_to_all(block, "bead", 0, 0, axis_index_groups=groups, tiled=True)
    offsets = ((CB, CHUNKS, SLOTS // 8, 3, 8, 128), f32)
    network = ((CB, NRBF, ATOMS), f32)
    w_in = w_in.T
    coords, veloc, down, up = call(
        begin_kernel,
        [(96, ATOMS), (96, ATOMS), (96, 128), (96, 128)],
        [
            ((96, 768), f32), ((96, ATOMS), f32), ((3, 16, 768), f32), offsets, network, network,
            ((3, 16, ATOMS), f32),
        ],
        (gathered, neighbours, weights, mine, ghosts, w_in, w_out, first, reduce_),
    )
    big = [((3 * 72 + 8, 512), bf16), ((96, ATOMS), f32), ((24, 768), f32), ((24, 8, ATOMS), f32)]
    below, above = exchange(down, up)
    coords, veloc, down, up = call(
        middle_kernel,
        [(96, ATOMS), (96, ATOMS), (96, 128), (96, 128)],
        big,
        (coords, veloc, below, above, neighbours, weights, mine, ghosts, later),
    )
    below, above = exchange(down, up)
    own, contracted, down, up = call(
        last_kernel,
        [(8, ATOMS), (16, ATOMS), (16, 128), (16, 128)],
        [((2 * BEADS, 3 * ATOMS), f32), ((16, ATOMS), f32)] + big,
        (place, coords, veloc, below, above, neighbours, weights, mine, ghosts, later, reduce_),
        (0,),
    )
    below, above = exchange(down, up)
    new_pos, new_mom = call(
        end_kernel,
        [(3, 1, ATOMS), (3, 1, ATOMS)],
        [((16, 768), f32), offsets, network, network, ((CB, 3, CHUNKS, 128), f32)],
        (place, expand, own, contracted, below, above, neighbours, weights, w_in, w_out),
        (0, 1),
    )
    return new_pos.transpose(1, 0, 2), new_mom.transpose(1, 0, 2)


def solution(mesh):
    in_specs = (
        P("bead", None, "space"),
        P("bead", None, "space"),
        P(None, "space"),
        P("space"),
        P("space"),
        P(),
        P(),
        P(),
        P(),
    )
    out_specs = (P("bead", None, "space"), P("bead", None, "space"))
    return jax.shard_map(body, mesh=mesh, in_specs=in_specs, out_specs=out_specs, check_vma=False)
```

```python
import functools

import jax
import jax.numpy as jnp
import numpy as np
from jax import lax
from jax.experimental import pallas as pl
from jax.experimental.pallas import tpu as pltpu
from jax.sharding import PartitionSpec as P

BEADS = 32
CB = 4
NINNER = 3
NRBF = 8
H = 128
SLOTS = 32
ATOMS = 512
CHUNKS = 4
WINDOW = 6
N_SPACE = 16

polymer_freq = 10.0
outer_step = 6.0
inner_step = outer_step / NINNER
f32 = jnp.float32
bf16 = jnp.bfloat16
VMEM_LIMIT = 12 * 1024 * 1024


def mode_matrix(count):
    beadpos = np.arange(count)[None, :]
    modeidx = np.arange(count)[:, None]
    middle = count // 2
    cosine = np.sqrt(2.0 / count) * np.cos(2.0 * np.pi * beadpos * modeidx / count)
    sine_rows = np.sqrt(2.0 / count) * np.sin(2.0 * np.pi * beadpos * modeidx / count)
    matrix = np.where(modeidx < middle, cosine, sine_rows)
    matrix = np.where(modeidx == 0, 1.0 / np.sqrt(count), matrix)
    matrix = np.where(modeidx == middle, np.cos(np.pi * beadpos) / np.sqrt(count), matrix)
    return matrix


def polymer_tables(count):
    modes = mode_matrix(count)
    frequency = 2.0 * polymer_freq * np.sin(np.pi * np.arange(count) / count)
    nonzero = np.where(frequency > 0, frequency, 1.0)
    cosine = np.cos(frequency * inner_step)
    drift_gain = np.where(frequency > 0, np.sin(frequency * inner_step) / nonzero, inner_step)
    spring = frequency * np.sin(frequency * inner_step)
    persist = modes.T @ (cosine[:, None] * modes)
    coupling = modes.T @ (drift_gain[:, None] * modes)
    restoring = -(modes.T @ (spring[:, None] * modes))
    return persist, coupling, restoring


def contraction(count, fewer):
    full_modes = mode_matrix(count)
    small_modes = mode_matrix(fewer)
    kept = list(range(fewer // 2 + 1)) + list(range(count - fewer // 2 + 1, count))
    contract = np.sqrt(fewer / count) * (small_modes.T @ full_modes[kept])
    expand = count / fewer * contract.T
    return contract, expand


def bf16_terms(matrix):
    out, rest = [], matrix
    for _ in range(3):
        out.append(rest.astype(np.float32).astype(jnp.bfloat16))
        rest = rest - out[-1].astype(np.float64)
    return out


def three_terms(matrix):
    high, low, _ = bf16_terms(matrix)
    return np.concatenate([high, low, high], axis=1)


def six_terms(matrix):
    high, middle, low = bf16_terms(matrix)
    return np.concatenate([high, high, middle, middle, high, low], axis=1)


BEAD_OF_ROW = np.array([x * 8 + z * 4 + y for z in range(2) for x in range(4) for y in range(4)])


def tables():
    persist, coupling, restoring = polymer_tables(BEADS)
    contract, expand = contraction(BEADS, CB)
    order = BEAD_OF_ROW
    persist, coupling, restoring = (m[np.ix_(order, order)] for m in (persist, coupling, restoring))
    contract, expand = contract[:, order], expand[order]
    step = np.block([[persist, coupling], [restoring, persist]])
    padded_expand = np.concatenate([expand, np.zeros((BEADS, 16 - CB))], axis=1)
    kick = np.concatenate([coupling @ padded_expand, persist @ padded_expand], axis=0)
    first = six_terms(np.concatenate([step, 0.5 * outer_step * kick], axis=1))
    later = six_terms(step)
    padded_contract = np.concatenate([contract, np.zeros((16 - CB, BEADS))], axis=0)
    last = six_terms(np.concatenate([step, padded_contract @ step[:BEADS]], axis=0))
    reduce_ = three_terms(padded_contract)
    return first, later, last, reduce_, (0.5 * outer_step * expand).astype(np.float32)


def lanes(source, index):
    return jnp.take_along_axis(source, index, axis=1)


def row8(row):
    return jnp.broadcast_to(row, (8, 128))


def split_rows(value):
    high = value.astype(bf16)
    low = (value - high.astype(f32)).astype(bf16)
    return jnp.concatenate([high, high, low], axis=0)


def dot3(matrix, value):
    return jnp.dot(matrix, split_rows(value), preferred_element_type=f32)


def dot6(matrix, value):
    high = value.astype(bf16)
    rest = value - high.astype(f32)
    middle = rest.astype(bf16)
    low = (rest - middle.astype(f32)).astype(bf16)
    terms = jnp.concatenate([high, middle, high, middle, low, high], axis=0)
    return jnp.dot(matrix, terms, preferred_element_type=f32)


def by_species(species, table):
    return jnp.where(species == 0, table[0], table[1])


def ghosts_of(chunk, index):
    first = chunk(0)
    rows = first.shape[0]
    lane = jnp.broadcast_to(index & 127, (rows, 128))
    part = jnp.broadcast_to(index >> 7, (rows, 128))
    out = lanes(first, lane)
    for k in range(1, CHUNKS):
        out = jnp.where(part == k, lanes(chunk(k), lane), out)
    return out


def tile_index(neighbours, g, a):
    index = neighbours[8 * g : 8 * g + 8, 128 * a : 128 * a + 128]
    return index & 127, [(index >> 7) == k for k in range(1, WINDOW)], index


def looked_up(rows, lane, masks):
    out = lanes(rows[0], lane)
    for k in range(1, WINDOW):
        out = jnp.where(masks[k - 1], lanes(rows[k], lane), out)
    return out


def cheap_by_lanes(table, neighbours, weights, a):
    rows = [[row8(table(x, k)) for k in range(WINDOW)] for x in range(3)]
    total = [jnp.zeros((8, 128), f32) for _ in range(3)]
    for g in range(SLOTS // 8):
        lane, masks, _ = tile_index(neighbours, g, a)
        offset = [looked_up(rows[x], lane, masks) - rows[x][1 + a] for x in range(3)]
        squared = offset[0] * offset[0] + offset[1] * offset[1] + offset[2] * offset[2]
        w = weights[8 * g : 8 * g + 8, 128 * a : 128 * a + 128] * jnp.exp(-squared)
        for x in range(3):
            total[x] = total[x] + w * offset[x]
    return [jnp.sum(t, axis=0, keepdims=True) for t in total]


def powers(squared):
    even = jnp.exp(-0.2 * squared)
    odd = jnp.exp(-(0.2 * 2.0**0.5) * squared)
    out = [even, odd]
    for _ in range(3):
        even, odd = even * even, odd * odd
        out += [even, odd]
    return out


def learned_by_lanes(table, neighbours, weights, w_in, w_out, offsets, messages, radials, store):
    high = w_in[...].astype(bf16).astype(f32)
    first = jnp.concatenate([high, w_in[...] - high, high, jnp.zeros_like(high)], axis=0).astype(bf16)
    high = w_out[...].astype(bf16).astype(f32)
    second = jnp.concatenate([high, w_out[...] - high, high], axis=1)
    second = jnp.concatenate([second, jnp.zeros_like(second)], axis=0).astype(bf16)

    def message(c):
        for a in range(CHUNKS):
            rows = [[row8(table(c, x, k)) for k in range(WINDOW)] for x in range(3)]
            total = [jnp.zeros((8, 128), f32) for _ in range(NRBF)]
            for g in range(SLOTS // 8):
                lane, masks, _ = tile_index(neighbours, g, a)
                offset = [looked_up(rows[x], lane, masks) - rows[x][1 + a] for x in range(3)]
                squared = offset[0] * offset[0] + offset[1] * offset[1] + offset[2] * offset[2]
                for x in range(3):
                    offsets[c, a, g, x] = offset[x]
                w = weights[8 * g : 8 * g + 8, 128 * a : 128 * a + 128]
                for r, basis in enumerate(powers(squared)):
                    total[r] = total[r] + w * basis
            for r in range(NRBF):
                messages[c, r : r + 1, 128 * a : 128 * a + 128] = jnp.sum(total[r], axis=0, keepdims=True) * (
                    1.0 / SLOTS
                )

    def network(c):
        value = messages[c]
        high = value.astype(bf16).astype(f32)
        terms = jnp.concatenate([high, high, value - high, jnp.zeros_like(high)], axis=0).astype(bf16)
        hidden = lax.dot_general(first, terms, (((0,), (0,)), ((), ())), preferred_element_type=f32)
        hidden = hidden * (1.0 / (1.0 + jnp.exp(-hidden)))
        radials[c] = jnp.dot(second, split_rows(hidden), preferred_element_type=f32)[0:NRBF]

    def force(c):
        for a in range(CHUNKS):
            radial = [row8(radials[c, r : r + 1, 128 * a : 128 * a + 128]) for r in range(NRBF)]
            total = [jnp.zeros((8, 128), f32) for _ in range(3)]
            for g in range(SLOTS // 8):
                offset = [offsets[c, a, g, x] for x in range(3)]
                squared = offset[0] * offset[0] + offset[1] * offset[1] + offset[2] * offset[2]
                basis = powers(squared)
                profile = radial[0] * basis[0]
                for r in range(1, NRBF):
                    profile = profile + radial[r] * basis[r]
                w = weights[8 * g : 8 * g + 8, 128 * a : 128 * a + 128] * profile
                for x in range(3):
                    total[x] = total[x] + w * offset[x]
            for x in range(3):
                store(c, x, a, jnp.sum(total[x], axis=0, keepdims=True))

    message(0)
    for c in range(CB):
        network(c)
        if c + 1 < CB:
            message(c + 1)
        force(c)


def cheap_of_all(coords, below, above, neighbours, weights, stacked, total, table, sums):
    few = BEADS - 8
    rows = 3 * few

    def of_few(value):
        return jnp.concatenate([value[BEADS * x : BEADS * x + few] for x in range(3)], axis=0)

    own, low, high_ = of_few(coords), of_few(below), of_few(above)
    stack = jnp.concatenate(
        [
            jnp.concatenate([low, own[:, 0:128]], axis=1),
            own[:, 128:384],
            jnp.concatenate([own[:, 384:512], high_], axis=1),
            jnp.zeros((8, 256), f32),
        ],
        axis=0,
    )
    high = stack.astype(bf16)
    stacked[:, 0:256] = high
    stacked[:, 256:512] = (stack - high.astype(f32)).astype(bf16)
    rounded = own.astype(bf16).astype(f32)
    rounded = rounded + (own - rounded).astype(bf16).astype(f32)
    for x in range(3):
        at = slice(BEADS * x + few, BEADS * (x + 1))
        table[8 * x : 8 * x + 8, 0:128] = below[at]
        table[8 * x : 8 * x + 8, 128:640] = coords[at]
        table[8 * x : 8 * x + 8, 640:768] = above[at]
    total[...] = jnp.zeros_like(total)
    sums[...] = jnp.zeros_like(sums)
    place = lax.broadcasted_iota(jnp.int16, (256, ATOMS), 0)

    def by_matmul(slot):
        index = neighbours[pl.ds(slot, 1), :]
        column = jnp.broadcast_to(index & 255, (16, ATOMS)).astype(jnp.int16)
        chosen = jnp.where(place == jnp.tile(column, (16, 1)), bf16(1), bf16(0))
        picked = jnp.dot(stacked[...], jnp.concatenate([chosen, chosen], axis=0), preferred_element_type=f32)
        part = index >> 8
        other = jnp.where(
            part == 0,
            picked[0:rows],
            jnp.where(part == 1, picked[rows : 2 * rows], picked[2 * rows : 3 * rows]),
        )
        offset = other - rounded
        x, y, z = offset[0:few], offset[few : 2 * few], offset[2 * few :]
        w = weights[pl.ds(slot, 1), :] * jnp.exp(-(x * x + y * y + z * z))
        total[0:few] += w * x
        total[BEADS : BEADS + few] += w * y
        total[2 * BEADS : 2 * BEADS + few] += w * z

    def by_lanes(g, a):
        at = slice(128 * a, 128 * a + 128)
        slots = pl.ds(pl.multiple_of(8 * g, 8), 8)
        index = neighbours[slots, at]
        lane, masks = index & 127, [(index >> 7) == k for k in range(1, WINDOW)]
        weight = weights[slots, at]
        for bead in range(8):
            rows_of = lambda x, k: row8(table[8 * x + bead : 8 * x + bead + 1, 128 * k : 128 * k + 128])
            offset = [
                looked_up([rows_of(x, k) for k in range(WINDOW)], lane, masks) - rows_of(x, 1 + a)
                for x in range(3)
            ]
            w = weight * jnp.exp(-(offset[0] * offset[0] + offset[1] * offset[1] + offset[2] * offset[2]))
            for x in range(3):
                sums[8 * x + bead, :, at] += w * offset[x]

    def group(g, _):
        for j in range(8):
            by_matmul(g * 8 + j)
            if j % 2:
                by_lanes(g, j // 2)
        return 0

    lax.fori_loop(0, SLOTS // 8, group, 0)
    for x in range(3):
        for bead in range(8):
            row = BEADS * x + few + bead
            total[row : row + 1] = jnp.sum(sums[8 * x + bead], axis=0, keepdims=True)


def propagated(coords, veloc, table, extra=None):
    wide = []
    for x in range(3):
        at = slice(x * BEADS, (x + 1) * BEADS)
        pieces = [coords[at], veloc[at]]
        if extra is not None:
            pieces.append(extra[x])
        wide.append(jnp.concatenate(pieces, axis=0))
    return dot6(table[...], jnp.concatenate(wide, axis=1))


def first_kernel(
    pos, mom, species, ghost_rows, scale, mass_table, out, ghosts, pos_in, mom_in, species_in, scale_in, mass_in, sems
):
    copies = [
        pltpu.make_async_copy(source, target, sems.at[i])
        for i, (source, target) in enumerate(
            (
                (scale, scale_in), (mass_table, mass_in), (species, species_in), (mom, mom_in), (pos, pos_in),
                (ghost_rows, ghosts),
            )
        )
    ]
    for copy in copies:
        copy.start()
    for copy in copies:
        copy.wait()
    mass = by_species(species_in[...], mass_in)
    for x in range(3):
        out[x : x + 1] = pos_in[x]
        out[3 + x : 4 + x] = mom_in[x] / mass
    out[6:7] = by_species(species_in[...], scale_in)
    out[7:8] = mass


def send_kernel(pair, ghost_rows, down, up, rows):
    rows[0:3] = pair[0, 0:3]
    rows[3:6] = pair[1, 0:3]
    rows[6:8] = pair[0, 6:8]
    chunk = lambda k: rows[:, 128 * k : 128 * k + 128]
    down[...] = ghosts_of(chunk, ghost_rows[0:1])
    up[...] = ghosts_of(chunk, ghost_rows[1:2])


def pack_kernel(pair, below, above, neighbours, out, weights, block, charges):
    charges[0:1] = below[6:7]
    for k in range(CHUNKS):
        charges[1 + k : 2 + k] = pair[0, 6:7, 128 * k : 128 * k + 128]
    charges[5:6] = above[6:7]
    for k in range(2):
        base = 32 * k
        for x in range(3):
            at = base + 6 * x
            block[at : at + 1] = below[3 * k + x : 3 * k + x + 1]
            for i in range(CHUNKS):
                block[at + 1 + i : at + 2 + i] = pair[k, x : x + 1, 128 * i : 128 * i + 128]
            block[at + 5 : at + 6] = above[3 * k + x : 3 * k + x + 1]
        block[base + 30 : base + 32] = jnp.zeros((2, 128), f32)
    for a in range(CHUNKS):
        itself = 128 + 128 * a + lax.broadcasted_iota(jnp.int32, (8, 128), 1)
        rows = [row8(charges[k : k + 1]) for k in range(WINDOW)]
        for g in range(SLOTS // 8):
            lane, masks, index = tile_index(neighbours, g, a)
            q = looked_up(rows, lane, masks)
            weights[8 * g : 8 * g + 8, 128 * a : 128 * a + 128] = jnp.where(index == itself, 0.0, q)
    for a in range(CHUNKS):
        at = slice(128 * a, 128 * a + 128)
        gain = pair[0, 6:7, at] / pair[0, 7:8, at] * (0.5 * inner_step)
        for k in range(2):
            base = 32 * k
            force = cheap_by_lanes(
                lambda x, w: block[base + 6 * x + w : base + 6 * x + w + 1], neighbours, weights, a
            )
            for x in range(3):
                row = base + 18 + 4 * x + a
                block[row : row + 1] = pair[k, 3 + x : 4 + x, at] + gain * force[x]
    for i in range(16):
        out[i] = block[...]


def begin_kernel(
    gathered, neighbours, weights, mine, ghost_rows, w_in, w_out, first, reduce_,
    coords, veloc, down, up,
    window, start, contracted, offsets, messages, radials, slow,
):
    inverse = 1.0 / mine[7:8]
    for z in range(2):
        for x in range(3):
            at = slice(x * BEADS + 16 * z, x * BEADS + 16 * z + 16)
            for k in range(WINDOW):
                window[at, 128 * k : 128 * k + 128] = gathered[:, 32 * z + 6 * x + k, :]
            for k in range(CHUNKS):
                start[at, 128 * k : 128 * k + 128] = gathered[:, 32 * z + 18 + 4 * x + k, :]
    for x in range(3):
        contracted[x] = dot3(reduce_[...], window[x * BEADS : (x + 1) * BEADS, :])
    slow[...] = jnp.zeros_like(slow)

    def store(c, x, a, value):
        slow[x, c : c + 1, 128 * a : 128 * a + 128] = value

    learned_by_lanes(
        lambda c, x, k: contracted[x, c : c + 1, 128 * k : 128 * k + 128],
        neighbours, weights, w_in, w_out, offsets, messages, radials, store,
    )
    moved = propagated(
        window[:, 128:640], start[...], first, [slow[x] * inverse for x in range(3)]
    )
    finish_step(moved, coords, veloc, ghost_rows, down, up)


def finish_step(moved, coords, veloc, ghost_rows, down, up):
    for x in range(3):
        at = slice(x * BEADS, (x + 1) * BEADS)
        coords[at] = moved[0:BEADS, ATOMS * x : ATOMS * (x + 1)]
        veloc[at] = moved[BEADS : 2 * BEADS, ATOMS * x : ATOMS * (x + 1)]
    for i in range(3 * BEADS // 8):
        chunk = lambda k: coords[8 * i : 8 * i + 8, 128 * k : 128 * k + 128]
        down[8 * i : 8 * i + 8] = ghosts_of(chunk, ghost_rows[0:1])
        up[8 * i : 8 * i + 8] = ghosts_of(chunk, ghost_rows[1:2])


def kicked(coords, veloc, below, above, neighbours, weights, mine, scratch):
    total = scratch[1]
    cheap_of_all(coords, below, above, neighbours, weights, *scratch)
    return veloc[...] + inner_step * mine[6:7] / mine[7:8] * total[...]


def middle_kernel(
    coords, veloc, below, above, neighbours, weights, mine, ghost_rows, later, new_coords, new_veloc, down, up, *scratch
):
    velocities = kicked(coords, veloc, below, above, neighbours, weights, mine, scratch)
    moved = propagated(coords[...], velocities, later)
    finish_step(moved, new_coords, new_veloc, ghost_rows, down, up)


def last_kernel(
    place, coords, veloc, below, above, neighbours, weights, mine, ghost_rows, last,
    own, contracted, down, up, moved, rows, *scratch,
):
    velocities = kicked(coords, veloc, below, above, neighbours, weights, mine, scratch)
    moved[...] = propagated(coords[...], velocities, last)
    for x in range(3):
        at = slice(ATOMS * x, ATOMS * (x + 1))
        own[x : x + 1] = moved[pl.ds(place[1], 1), at]
        own[3 + x : 4 + x] = moved[pl.ds(BEADS + place[1], 1), at]
        contracted[4 * x : 4 * x + 4] = moved[2 * BEADS : 2 * BEADS + CB, at]
    own[6:8] = mine[6:8]
    contracted[12:16] = jnp.zeros((4, ATOMS), f32)
    rows[0:12] = contracted[0:12]
    for which, out in ((2, down), (3, up)):
        for x in range(3):
            rows[12 + x : 13 + x] = moved[pl.ds(place[which], 1), ATOMS * x : ATOMS * (x + 1)]
        rows[15:16] = contracted[12:13]
        index = ghost_rows[which - 2 : which - 1]
        for i in range(2):
            out[8 * i : 8 * i + 8] = ghosts_of(
                lambda k: rows[8 * i : 8 * i + 8, 128 * k : 128 * k + 128], index
            )


def end_kernel(
    place, expand, own, contracted, below, above, neighbours, weights, w_in, w_out,
    new_pos, new_mom,
    window, offsets, messages, radials, slow,
):
    charge, mass = own[6:7], own[7:8]
    window[0:16, 0:128] = below[...]
    window[0:16, 640:768] = above[...]
    window[0:12, 128:640] = contracted[0:12]
    window[12:15, 128:640] = own[0:3]

    def store(c, x, a, value):
        slow[c, x, a : a + 1] = value

    learned_by_lanes(
        lambda c, x, k: window[4 * x + c : 4 * x + c + 1, 128 * k : 128 * k + 128],
        neighbours, weights, w_in, w_out, offsets, messages, radials, store,
    )
    for a in range(CHUNKS):
        force = cheap_by_lanes(
            lambda x, k: window[12 + x : 13 + x, 128 * k : 128 * k + 128], neighbours, weights, a
        )
        at = slice(128 * a, 128 * a + 128)
        for x in range(3):
            value = mass[:, at] * own[3 + x : 4 + x, at] + (0.5 * inner_step) * charge[:, at] * force[x]
            for c in range(CB):
                value = value + expand[place[1], c] * slow[c, x, a : a + 1]
            new_mom[x, :, at] = value
            new_pos[x, :, at] = own[x : x + 1, at]


def call(kernel, outs, scratch, args, scalars=(), space=pltpu.VMEM):
    specs = [pl.BlockSpec(memory_space=pltpu.SMEM if i in scalars else space) for i in range(len(args))]
    shapes = [s if isinstance(s, jax.ShapeDtypeStruct) else jax.ShapeDtypeStruct(s, f32) for s in outs]
    return pl.pallas_call(
        kernel,
        out_shape=shapes,
        in_specs=specs,
        out_specs=[pl.BlockSpec(memory_space=pltpu.VMEM)] * len(outs),
        scratch_shapes=[pltpu.VMEM(*s) if isinstance(s, tuple) else s for s in scratch],
        compiler_params=pltpu.CompilerParams(vmem_limit_bytes=VMEM_LIMIT),
    )(*args)


RING = ("bead", "space")


def ring(step):
    pairs = []
    for bead in range(BEADS):
        for domain in range(N_SPACE):
            to = domain + step
            other = bead if 0 <= to < N_SPACE else bead ^ 4
            pairs.append((bead * N_SPACE + domain, other * N_SPACE + to % N_SPACE))
    return pairs


def exchange(down, up):
    below = lax.ppermute(up, RING, ring(1))
    above = lax.ppermute(down, RING, ring(-1))
    return below, above


def body(
    positions, momenta, neighbours, ghost_rows, species, species_scale, mass_table, w_in, w_out
):
    first, later, last, reduce_, expand = tables()
    first, later, last, reduce_ = (jnp.asarray(t) for t in (first, later, last, reduce_))
    expand = jnp.asarray(expand)
    bead = lax.axis_index("bead")
    domain = lax.axis_index("space")
    half = (bead // 4) % 2
    row = half * 16 + (bead // 8) * 4 + bead % 4
    other = (1 - half) * 16 + (bead // 8) * 4 + bead % 4
    row_below = jnp.where(domain == 0, other, row)
    row_above = jnp.where(domain == N_SPACE - 1, other, row)
    place = jnp.stack([half, row, row_below, row_above]).astype(jnp.int32)

    pos = positions.transpose(1, 0, 2)
    mom = momenta.transpose(1, 0, 2)
    kinds = species.reshape(1, ATOMS)
    ghosts = ghost_rows.reshape(2, 128)

    mine, ghosts = call(
        first_kernel,
        [(8, ATOMS), jax.ShapeDtypeStruct((2, 128), jnp.int32)],
        [
            ((3, 1, ATOMS), f32), ((3, 1, ATOMS), f32), ((1, ATOMS), jnp.int32),
            pltpu.SMEM((2,), f32), pltpu.SMEM((2,), f32), pltpu.SemaphoreType.DMA((6,)),
        ],
        tuple(
            pltpu.with_memory_space_constraint(v, pltpu.HBM)
            for v in (pos, mom, kinds, ghosts, species_scale, mass_table)
        ),
        space=pltpu.HBM,
    )
    halves = [[x * 8 + z * 4 + y for z in range(2)] for x in range(4) for y in range(4)]
    pair = lax.all_gather(mine, "bead", axis=0, axis_index_groups=halves)
    down, up = call(send_kernel, [(8, 128)] * 2, [((8, ATOMS), f32)], (pair, ghosts), ())
    below, above = exchange(down, up)
    block, weights = call(
        pack_kernel,
        [(16, 64, 128), (SLOTS, ATOMS)],
        [((64, 128), f32), ((8, 128), f32)],
        (pair, below, above, neighbours),
        (),
    )
    groups = [[x * 8 + z * 4 + y for x in range(4) for y in range(4)] for z in range(2)]
    gathered = lax.all_to_all(block, "bead", 0, 0, axis_index_groups=groups, tiled=True)
    offsets = ((CB, CHUNKS, SLOTS // 8, 3, 8, 128), f32)
    network = ((CB, NRBF, ATOMS), f32)
    w_in = w_in.T
    coords, veloc, down, up = call(
        begin_kernel,
        [(96, ATOMS), (96, ATOMS), (96, 128), (96, 128)],
        [
            ((96, 768), f32), ((96, ATOMS), f32), ((3, 16, 768), f32), offsets, network, network,
            ((3, 16, ATOMS), f32),
        ],
        (gathered, neighbours, weights, mine, ghosts, w_in, w_out, first, reduce_),
    )
    big = [((3 * 72 + 8, 512), bf16), ((96, ATOMS), f32), ((24, 768), f32), ((24, 8, ATOMS), f32)]
    below, above = exchange(down, up)
    coords, veloc, down, up = call(
        middle_kernel,
        [(96, ATOMS), (96, ATOMS), (96, 128), (96, 128)],
        big,
        (coords, veloc, below, above, neighbours, weights, mine, ghosts, later),
    )
    below, above = exchange(down, up)
    own, contracted, down, up = call(
        last_kernel,
        [(8, ATOMS), (16, ATOMS), (16, 128), (16, 128)],
        [((2 * BEADS + 16, 3 * ATOMS), f32), ((16, ATOMS), f32)] + big,
        (place, coords, veloc, below, above, neighbours, weights, mine, ghosts, last),
        (0,),
    )
    below, above = exchange(down, up)
    new_pos, new_mom = call(
        end_kernel,
        [(3, 1, ATOMS), (3, 1, ATOMS)],
        [((16, 768), f32), offsets, network, network, ((CB, 3, CHUNKS, 128), f32)],
        (place, expand, own, contracted, below, above, neighbours, weights, w_in, w_out),
        (0, 1),
    )
    return new_pos.transpose(1, 0, 2), new_mom.transpose(1, 0, 2)


def solution(mesh):
    in_specs = (
        P("bead", None, "space"),
        P("bead", None, "space"),
        P(None, "space"),
        P("space"),
        P("space"),
        P(),
        P(),
        P(),
        P(),
    )
    out_specs = (P("bead", None, "space"), P("bead", None, "space"))
    return jax.shard_map(body, mesh=mesh, in_specs=in_specs, out_specs=out_specs, check_vma=False)
```

```python
import functools

import jax
import jax.numpy as jnp
import numpy as np
from jax import lax
from jax.experimental import pallas as pl
from jax.experimental.pallas import tpu as pltpu
from jax.sharding import PartitionSpec as P

BEADS = 32
CB = 4
NINNER = 3
NRBF = 8
H = 128
SLOTS = 32
ATOMS = 512
CHUNKS = 4
WINDOW = 6
N_SPACE = 16

polymer_freq = 10.0
outer_step = 6.0
inner_step = outer_step / NINNER
f32 = jnp.float32
bf16 = jnp.bfloat16
VMEM_LIMIT = 12 * 1024 * 1024


def mode_matrix(count):
    beadpos = np.arange(count)[None, :]
    modeidx = np.arange(count)[:, None]
    middle = count // 2
    cosine = np.sqrt(2.0 / count) * np.cos(2.0 * np.pi * beadpos * modeidx / count)
    sine_rows = np.sqrt(2.0 / count) * np.sin(2.0 * np.pi * beadpos * modeidx / count)
    matrix = np.where(modeidx < middle, cosine, sine_rows)
    matrix = np.where(modeidx == 0, 1.0 / np.sqrt(count), matrix)
    matrix = np.where(modeidx == middle, np.cos(np.pi * beadpos) / np.sqrt(count), matrix)
    return matrix


def polymer_tables(count):
    modes = mode_matrix(count)
    frequency = 2.0 * polymer_freq * np.sin(np.pi * np.arange(count) / count)
    nonzero = np.where(frequency > 0, frequency, 1.0)
    cosine = np.cos(frequency * inner_step)
    drift_gain = np.where(frequency > 0, np.sin(frequency * inner_step) / nonzero, inner_step)
    spring = frequency * np.sin(frequency * inner_step)
    persist = modes.T @ (cosine[:, None] * modes)
    coupling = modes.T @ (drift_gain[:, None] * modes)
    restoring = -(modes.T @ (spring[:, None] * modes))
    return persist, coupling, restoring


def contraction(count, fewer):
    full_modes = mode_matrix(count)
    small_modes = mode_matrix(fewer)
    kept = list(range(fewer // 2 + 1)) + list(range(count - fewer // 2 + 1, count))
    contract = np.sqrt(fewer / count) * (small_modes.T @ full_modes[kept])
    expand = count / fewer * contract.T
    return contract, expand


def bf16_terms(matrix):
    out, rest = [], matrix
    for _ in range(3):
        out.append(rest.astype(np.float32).astype(jnp.bfloat16))
        rest = rest - out[-1].astype(np.float64)
    return out


def three_terms(matrix):
    high, low, _ = bf16_terms(matrix)
    return np.concatenate([high, low, high], axis=1)


def six_terms(matrix):
    high, middle, low = bf16_terms(matrix)
    return np.concatenate([high, high, middle, middle, high, low], axis=1)


BEAD_OF_ROW = np.array([x * 8 + z * 4 + y for z in range(2) for x in range(4) for y in range(4)])


def tables():
    persist, coupling, restoring = polymer_tables(BEADS)
    contract, expand = contraction(BEADS, CB)
    order = BEAD_OF_ROW
    persist, coupling, restoring = (m[np.ix_(order, order)] for m in (persist, coupling, restoring))
    contract, expand = contract[:, order], expand[order]
    step = np.block([[persist, coupling], [restoring, persist]])
    padded_expand = np.concatenate([expand, np.zeros((BEADS, 16 - CB))], axis=1)
    kick = np.concatenate([coupling @ padded_expand, persist @ padded_expand], axis=0)
    first = six_terms(np.concatenate([step, 0.5 * outer_step * kick], axis=1))
    later = six_terms(step)
    padded_contract = np.concatenate([contract, np.zeros((16 - CB, BEADS))], axis=0)
    last = six_terms(np.concatenate([step, padded_contract @ step[:BEADS]], axis=0))
    reduce_ = three_terms(padded_contract)
    return first, later, last, reduce_, (0.5 * outer_step * expand).astype(np.float32)


def lanes(source, index):
    return jnp.take_along_axis(source, index, axis=1)


def row8(row):
    return jnp.broadcast_to(row, (8, 128))


def split_rows(value):
    high = value.astype(bf16)
    low = (value - high.astype(f32)).astype(bf16)
    return jnp.concatenate([high, high, low], axis=0)


def dot3(matrix, value):
    return jnp.dot(matrix, split_rows(value), preferred_element_type=f32)


def dot6(matrix, value):
    high = value.astype(bf16)
    rest = value - high.astype(f32)
    middle = rest.astype(bf16)
    low = (rest - middle.astype(f32)).astype(bf16)
    terms = jnp.concatenate([high, middle, high, middle, low, high], axis=0)
    return jnp.dot(matrix, terms, preferred_element_type=f32)


def by_species(species, table):
    return jnp.where(species == 0, table[0], table[1])


def ghosts_of(chunk, index):
    first = chunk(0)
    rows = first.shape[0]
    lane = jnp.broadcast_to(index & 127, (rows, 128))
    part = jnp.broadcast_to(index >> 7, (rows, 128))
    out = lanes(first, lane)
    for k in range(1, CHUNKS):
        out = jnp.where(part == k, lanes(chunk(k), lane), out)
    return out


def tile_index(neighbours, g, a):
    index = neighbours[8 * g : 8 * g + 8, 128 * a : 128 * a + 128]
    return index & 127, [(index >> 7) == k for k in range(1, WINDOW)], index


def looked_up(rows, lane, masks):
    out = lanes(rows[0], lane)
    for k in range(1, WINDOW):
        out = jnp.where(masks[k - 1], lanes(rows[k], lane), out)
    return out


def own_lookup(row, neighbours, g, a):
    index = neighbours[8 * g : 8 * g + 8, 128 * a : 128 * a + 128]
    lane, part = index & 127, index >> 7
    out = lanes(row8(row(0)), lane)
    for k in range(1, CHUNKS):
        out = jnp.where(part == k + 1, lanes(row8(row(k)), lane), out)
    return out


def with_ghosts(early, low, high, index):
    lane, part = index & 127, index >> 7
    out = jnp.where(part == 0, lanes(row8(low), lane), early)
    return jnp.where(part == WINDOW - 1, lanes(row8(high), lane), out)


def cheap_by_lanes(looked, centre, neighbours, weights, a):
    centre = [row8(row) for row in centre]
    total = [jnp.zeros((8, 128), f32) for _ in range(3)]
    for g in range(SLOTS // 8):
        index = neighbours[8 * g : 8 * g + 8, 128 * a : 128 * a + 128]
        offset = [looked(x, g, index) - centre[x] for x in range(3)]
        squared = offset[0] * offset[0] + offset[1] * offset[1] + offset[2] * offset[2]
        w = weights[8 * g : 8 * g + 8, 128 * a : 128 * a + 128] * jnp.exp(-squared)
        for x in range(3):
            total[x] = total[x] + w * offset[x]
    return [jnp.sum(t, axis=0, keepdims=True) for t in total]


def powers(squared):
    even = jnp.exp(-0.2 * squared)
    odd = jnp.exp(-(0.2 * 2.0**0.5) * squared)
    out = [even, odd]
    for _ in range(3):
        even, odd = even * even, odd * odd
        out += [even, odd]
    return out


def learned_by_lanes(looked, centre, neighbours, weights, w_in, w_out, offsets, messages, radials, store):
    high = w_in[...].astype(bf16).astype(f32)
    first = jnp.concatenate([high, w_in[...] - high, high, jnp.zeros_like(high)], axis=0).astype(bf16)
    high = w_out[...].astype(bf16).astype(f32)
    second = jnp.concatenate([high, w_out[...] - high, high], axis=1)
    second = jnp.concatenate([second, jnp.zeros_like(second)], axis=0).astype(bf16)

    def message(c):
        for a in range(CHUNKS):
            middle = [row8(centre(c, x, a)) for x in range(3)]
            total = [jnp.zeros((8, 128), f32) for _ in range(NRBF)]
            for g in range(SLOTS // 8):
                offset = [looked(c, x, a, g) - middle[x] for x in range(3)]
                squared = offset[0] * offset[0] + offset[1] * offset[1] + offset[2] * offset[2]
                for x in range(3):
                    offsets[c, a, g, x] = offset[x]
                w = weights[8 * g : 8 * g + 8, 128 * a : 128 * a + 128]
                for r, basis in enumerate(powers(squared)):
                    total[r] = total[r] + w * basis
            for r in range(NRBF):
                messages[c, r : r + 1, 128 * a : 128 * a + 128] = jnp.sum(total[r], axis=0, keepdims=True) * (
                    1.0 / SLOTS
                )

    def network(c):
        value = messages[c]
        high = value.astype(bf16).astype(f32)
        terms = jnp.concatenate([high, high, value - high, jnp.zeros_like(high)], axis=0).astype(bf16)
        hidden = lax.dot_general(first, terms, (((0,), (0,)), ((), ())), preferred_element_type=f32)
        hidden = hidden * (1.0 / (1.0 + jnp.exp(-hidden)))
        radials[c] = jnp.dot(second, split_rows(hidden), preferred_element_type=f32)[0:NRBF]

    def force(c):
        for a in range(CHUNKS):
            radial = [row8(radials[c, r : r + 1, 128 * a : 128 * a + 128]) for r in range(NRBF)]
            total = [jnp.zeros((8, 128), f32) for _ in range(3)]
            for g in range(SLOTS // 8):
                offset = [offsets[c, a, g, x] for x in range(3)]
                squared = offset[0] * offset[0] + offset[1] * offset[1] + offset[2] * offset[2]
                basis = powers(squared)
                profile = radial[0] * basis[0]
                for r in range(1, NRBF):
                    profile = profile + radial[r] * basis[r]
                w = weights[8 * g : 8 * g + 8, 128 * a : 128 * a + 128] * profile
                for x in range(3):
                    total[x] = total[x] + w * offset[x]
            for x in range(3):
                store(c, x, a, jnp.sum(total[x], axis=0, keepdims=True))

    message(0)
    for c in range(CB):
        network(c)
        if c + 1 < CB:
            message(c + 1)
        force(c)


def cheap_of_all(coords, below, above, neighbours, weights, stacked, total, table, sums):
    few = BEADS - 8
    rows = 3 * few

    def of_few(value):
        return jnp.concatenate([value[BEADS * x : BEADS * x + few] for x in range(3)], axis=0)

    own, low, high_ = of_few(coords), of_few(below), of_few(above)
    stack = jnp.concatenate(
        [
            jnp.concatenate([low, own[:, 0:128]], axis=1),
            own[:, 128:384],
            jnp.concatenate([own[:, 384:512], high_], axis=1),
            jnp.zeros((8, 256), f32),
        ],
        axis=0,
    )
    high = stack.astype(bf16)
    stacked[:, 0:256] = high
    stacked[:, 256:512] = (stack - high.astype(f32)).astype(bf16)
    rounded = own.astype(bf16).astype(f32)
    rounded = rounded + (own - rounded).astype(bf16).astype(f32)
    for x in range(3):
        at = slice(BEADS * x + few, BEADS * (x + 1))
        table[8 * x : 8 * x + 8, 0:128] = below[at]
        table[8 * x : 8 * x + 8, 128:640] = coords[at]
        table[8 * x : 8 * x + 8, 640:768] = above[at]
    total[...] = jnp.zeros_like(total)
    sums[...] = jnp.zeros_like(sums)
    place = lax.broadcasted_iota(jnp.int16, (256, ATOMS), 0)

    def by_matmul(slot):
        index = neighbours[pl.ds(slot, 1), :]
        column = jnp.broadcast_to(index & 255, (16, ATOMS)).astype(jnp.int16)
        chosen = jnp.where(place == jnp.tile(column, (16, 1)), bf16(1), bf16(0))
        picked = jnp.dot(stacked[...], jnp.concatenate([chosen, chosen], axis=0), preferred_element_type=f32)
        part = index >> 8
        other = jnp.where(
            part == 0,
            picked[0:rows],
            jnp.where(part == 1, picked[rows : 2 * rows], picked[2 * rows : 3 * rows]),
        )
        offset = other - rounded
        x, y, z = offset[0:few], offset[few : 2 * few], offset[2 * few :]
        w = weights[pl.ds(slot, 1), :] * jnp.exp(-(x * x + y * y + z * z))
        total[0:few] += w * x
        total[BEADS : BEADS + few] += w * y
        total[2 * BEADS : 2 * BEADS + few] += w * z

    def by_lanes(g, a):
        at = slice(128 * a, 128 * a + 128)
        slots = pl.ds(pl.multiple_of(8 * g, 8), 8)
        index = neighbours[slots, at]
        lane, masks = index & 127, [(index >> 7) == k for k in range(1, WINDOW)]
        weight = weights[slots, at]
        for bead in range(8):
            rows_of = lambda x, k: row8(table[8 * x + bead : 8 * x + bead + 1, 128 * k : 128 * k + 128])
            offset = [
                looked_up([rows_of(x, k) for k in range(WINDOW)], lane, masks) - rows_of(x, 1 + a)
                for x in range(3)
            ]
            w = weight * jnp.exp(-(offset[0] * offset[0] + offset[1] * offset[1] + offset[2] * offset[2]))
            for x in range(3):
                sums[8 * x + bead, :, at] += w * offset[x]

    def group(g, _):
        for j in range(8):
            by_matmul(g * 8 + j)
            if j % 2:
                by_lanes(g, j // 2)
        return 0

    lax.fori_loop(0, SLOTS // 8, group, 0)
    for x in range(3):
        for bead in range(8):
            row = BEADS * x + few + bead
            total[row : row + 1] = jnp.sum(sums[8 * x + bead], axis=0, keepdims=True)


def propagated(coords, veloc, table, extra=None):
    wide = []
    for x in range(3):
        at = slice(x * BEADS, (x + 1) * BEADS)
        pieces = [coords[at], veloc[at]]
        if extra is not None:
            pieces.append(extra[x])
        wide.append(jnp.concatenate(pieces, axis=0))
    return dot6(table[...], jnp.concatenate(wide, axis=1))


def first_kernel(
    pos, mom, species, ghost_rows, scale, mass_table, out, ghosts, pos_in, mom_in, species_in, scale_in, mass_in, sems
):
    copies = [
        pltpu.make_async_copy(source, target, sems.at[i])
        for i, (source, target) in enumerate(
            (
                (scale, scale_in), (mass_table, mass_in), (species, species_in), (mom, mom_in), (pos, pos_in),
                (ghost_rows, ghosts),
            )
        )
    ]
    for copy in copies:
        copy.start()
    for copy in copies:
        copy.wait()
    mass = by_species(species_in[...], mass_in)
    for x in range(3):
        out[x : x + 1] = pos_in[x]
        out[3 + x : 4 + x] = mom_in[x] / mass
    out[6:7] = by_species(species_in[...], scale_in)
    out[7:8] = mass


def send_kernel(pair, ghost_rows, down, up, rows):
    rows[0:3] = pair[0, 0:3]
    rows[3:6] = pair[1, 0:3]
    rows[6:8] = pair[0, 6:8]
    chunk = lambda k: rows[:, 128 * k : 128 * k + 128]
    down[...] = ghosts_of(chunk, ghost_rows[0:1])
    up[...] = ghosts_of(chunk, ghost_rows[1:2])


def early_pack_kernel(pair, neighbours, early):
    for a in range(CHUNKS):
        for g in range(SLOTS // 8):
            for k in range(2):
                for x in range(3):
                    early[3 * k + x, a, g] = own_lookup(
                        lambda i: pair[k, x : x + 1, 128 * i : 128 * i + 128], neighbours, g, a
                    )
            early[6, a, g] = own_lookup(lambda i: pair[0, 6:7, 128 * i : 128 * i + 128], neighbours, g, a)


def pack_kernel(pair, early, below, above, neighbours, out, weights, block):
    for k in range(2):
        base = 32 * k
        for x in range(3):
            at = base + 6 * x
            block[at : at + 1] = below[3 * k + x : 3 * k + x + 1]
            for i in range(CHUNKS):
                block[at + 1 + i : at + 2 + i] = pair[k, x : x + 1, 128 * i : 128 * i + 128]
            block[at + 5 : at + 6] = above[3 * k + x : 3 * k + x + 1]
        block[base + 30 : base + 32] = jnp.zeros((2, 128), f32)
    for a in range(CHUNKS):
        itself = 128 + 128 * a + lax.broadcasted_iota(jnp.int32, (8, 128), 1)
        for g in range(SLOTS // 8):
            index = neighbours[8 * g : 8 * g + 8, 128 * a : 128 * a + 128]
            q = with_ghosts(early[6, a, g], below[6:7], above[6:7], index)
            weights[8 * g : 8 * g + 8, 128 * a : 128 * a + 128] = jnp.where(index == itself, 0.0, q)
    for a in range(CHUNKS):
        at = slice(128 * a, 128 * a + 128)
        gain = pair[0, 6:7, at] / pair[0, 7:8, at] * (0.5 * inner_step)
        for k in range(2):
            base = 32 * k

            def looked(x, g, index):
                i = 3 * k + x
                return with_ghosts(early[i, a, g], below[i : i + 1], above[i : i + 1], index)

            force = cheap_by_lanes(looked, [pair[k, x : x + 1, at] for x in range(3)], neighbours, weights, a)
            for x in range(3):
                row = base + 18 + 4 * x + a
                block[row : row + 1] = pair[k, 3 + x : 4 + x, at] + gain * force[x]
    for i in range(16):
        out[i] = block[...]


def begin_kernel(
    gathered, neighbours, weights, mine, ghost_rows, w_in, w_out, first, reduce_,
    coords, veloc, down, up,
    window, start, contracted, offsets, messages, radials, slow,
):
    inverse = 1.0 / mine[7:8]
    for z in range(2):
        for x in range(3):
            at = slice(x * BEADS + 16 * z, x * BEADS + 16 * z + 16)
            for k in range(WINDOW):
                window[at, 128 * k : 128 * k + 128] = gathered[:, 32 * z + 6 * x + k, :]
            for k in range(CHUNKS):
                start[at, 128 * k : 128 * k + 128] = gathered[:, 32 * z + 18 + 4 * x + k, :]
    for x in range(3):
        contracted[x] = dot3(reduce_[...], window[x * BEADS : (x + 1) * BEADS, :])
    slow[...] = jnp.zeros_like(slow)

    def store(c, x, a, value):
        slow[x, c : c + 1, 128 * a : 128 * a + 128] = value

    def looked(c, x, a, g):
        rows = [row8(contracted[x, c : c + 1, 128 * k : 128 * k + 128]) for k in range(WINDOW)]
        lane, masks, _ = tile_index(neighbours, g, a)
        return looked_up(rows, lane, masks)

    learned_by_lanes(
        looked, lambda c, x, a: contracted[x, c : c + 1, 128 + 128 * a : 256 + 128 * a], neighbours, weights, w_in, w_out, offsets, messages, radials, store,
    )
    moved = propagated(
        window[:, 128:640], start[...], first, [slow[x] * inverse for x in range(3)]
    )
    finish_step(moved, coords, veloc, ghost_rows, down, up)


def finish_step(moved, coords, veloc, ghost_rows, down, up):
    for x in range(3):
        at = slice(x * BEADS, (x + 1) * BEADS)
        coords[at] = moved[0:BEADS, ATOMS * x : ATOMS * (x + 1)]
        veloc[at] = moved[BEADS : 2 * BEADS, ATOMS * x : ATOMS * (x + 1)]
    for i in range(3 * BEADS // 8):
        chunk = lambda k: coords[8 * i : 8 * i + 8, 128 * k : 128 * k + 128]
        down[8 * i : 8 * i + 8] = ghosts_of(chunk, ghost_rows[0:1])
        up[8 * i : 8 * i + 8] = ghosts_of(chunk, ghost_rows[1:2])


def kicked(coords, veloc, below, above, neighbours, weights, mine, scratch):
    total = scratch[1]
    cheap_of_all(coords, below, above, neighbours, weights, *scratch)
    return veloc[...] + inner_step * mine[6:7] / mine[7:8] * total[...]


def middle_kernel(
    coords, veloc, below, above, neighbours, weights, mine, ghost_rows, later, new_coords, new_veloc, down, up, *scratch
):
    velocities = kicked(coords, veloc, below, above, neighbours, weights, mine, scratch)
    moved = propagated(coords[...], velocities, later)
    finish_step(moved, new_coords, new_veloc, ghost_rows, down, up)


def last_kernel(
    place, coords, veloc, below, above, neighbours, weights, mine, ghost_rows, last,
    own, contracted, down, up, moved, rows, *scratch,
):
    velocities = kicked(coords, veloc, below, above, neighbours, weights, mine, scratch)
    moved[...] = propagated(coords[...], velocities, last)
    for x in range(3):
        at = slice(ATOMS * x, ATOMS * (x + 1))
        own[x : x + 1] = moved[pl.ds(place[1], 1), at]
        own[3 + x : 4 + x] = moved[pl.ds(BEADS + place[1], 1), at]
        contracted[4 * x : 4 * x + 4] = moved[2 * BEADS : 2 * BEADS + CB, at]
    own[6:8] = mine[6:8]
    contracted[12:16] = jnp.zeros((4, ATOMS), f32)
    for which, out in ((0, down), (1, up)):
        rows[which, 0:4] = contracted[8:12]
        for x in range(3):
            rows[which, 4 + x : 5 + x] = moved[pl.ds(place[2 + which], 1), ATOMS * x : ATOMS * (x + 1)]
        rows[which, 7:8] = contracted[12:13]
        index = ghost_rows[which : which + 1]
        out[0:8] = ghosts_of(lambda k: contracted[0:8, 128 * k : 128 * k + 128], index)
        out[8:16] = ghosts_of(lambda k: rows[which, :, 128 * k : 128 * k + 128], index)


def early_end_kernel(own, contracted, neighbours, early):
    for a in range(CHUNKS):
        for g in range(SLOTS // 8):
            for i in range(15):
                source, row = (contracted, i) if i < 12 else (own, i - 12)
                early[i, a, g] = own_lookup(
                    lambda k: source[row : row + 1, 128 * k : 128 * k + 128], neighbours, g, a
                )


def end_kernel(
    place, expand, own, contracted, early, below, above, neighbours, weights, w_in, w_out,
    new_pos, new_mom,
    offsets, messages, radials, slow,
):
    charge, mass = own[6:7], own[7:8]

    def store(c, x, a, value):
        slow[c, x, a : a + 1] = value

    def looked_at(i, a, g):
        index = neighbours[8 * g : 8 * g + 8, 128 * a : 128 * a + 128]
        return with_ghosts(early[i, a, g], below[i : i + 1], above[i : i + 1], index)

    learned_by_lanes(
        lambda c, x, a, g: looked_at(4 * x + c, a, g),
        lambda c, x, a: contracted[4 * x + c : 4 * x + c + 1, 128 * a : 128 * a + 128],
        neighbours, weights, w_in, w_out, offsets, messages, radials, store,
    )
    for a in range(CHUNKS):
        at = slice(128 * a, 128 * a + 128)
        force = cheap_by_lanes(
            lambda x, g, index: looked_at(12 + x, a, g), [own[x : x + 1, at] for x in range(3)], neighbours, weights, a
        )
        for x in range(3):
            value = mass[:, at] * own[3 + x : 4 + x, at] + (0.5 * inner_step) * charge[:, at] * force[x]
            for c in range(CB):
                value = value + expand[place[1], c] * slow[c, x, a : a + 1]
            new_mom[x, :, at] = value
            new_pos[x, :, at] = own[x : x + 1, at]


def call(kernel, outs, scratch, args, scalars=(), space=pltpu.VMEM, cost=None):
    specs = [pl.BlockSpec(memory_space=pltpu.SMEM if i in scalars else space) for i in range(len(args))]
    shapes = [s if isinstance(s, jax.ShapeDtypeStruct) else jax.ShapeDtypeStruct(s, f32) for s in outs]
    return pl.pallas_call(
        kernel,
        out_shape=shapes,
        in_specs=specs,
        out_specs=[pl.BlockSpec(memory_space=pltpu.VMEM)] * len(outs),
        scratch_shapes=[pltpu.VMEM(*s) if isinstance(s, tuple) else s for s in scratch],
        compiler_params=pltpu.CompilerParams(vmem_limit_bytes=VMEM_LIMIT),
        cost_estimate=cost,
    )(*args)


RING = ("bead", "space")


def ring(step):
    pairs = []
    for bead in range(BEADS):
        for domain in range(N_SPACE):
            to = domain + step
            other = bead if 0 <= to < N_SPACE else bead ^ 4
            pairs.append((bead * N_SPACE + domain, other * N_SPACE + to % N_SPACE))
    return pairs


def exchange(down, up):
    below = lax.ppermute(up, RING, ring(1))
    above = lax.ppermute(down, RING, ring(-1))
    return below, above


def body(
    positions, momenta, neighbours, ghost_rows, species, species_scale, mass_table, w_in, w_out
):
    first, later, last, reduce_, expand = tables()
    first, later, last, reduce_ = (jnp.asarray(t) for t in (first, later, last, reduce_))
    expand = jnp.asarray(expand)
    bead = lax.axis_index("bead")
    domain = lax.axis_index("space")
    half = (bead // 4) % 2
    row = half * 16 + (bead // 8) * 4 + bead % 4
    other = (1 - half) * 16 + (bead // 8) * 4 + bead % 4
    row_below = jnp.where(domain == 0, other, row)
    row_above = jnp.where(domain == N_SPACE - 1, other, row)
    place = jnp.stack([half, row, row_below, row_above]).astype(jnp.int32)

    pos = positions.transpose(1, 0, 2)
    mom = momenta.transpose(1, 0, 2)
    kinds = species.reshape(1, ATOMS)
    ghosts = ghost_rows.reshape(2, 128)

    mine, ghosts = call(
        first_kernel,
        [(8, ATOMS), jax.ShapeDtypeStruct((2, 128), jnp.int32)],
        [
            ((3, 1, ATOMS), f32), ((3, 1, ATOMS), f32), ((1, ATOMS), jnp.int32),
            pltpu.SMEM((2,), f32), pltpu.SMEM((2,), f32), pltpu.SemaphoreType.DMA((6,)),
        ],
        tuple(
            pltpu.with_memory_space_constraint(v, pltpu.HBM)
            for v in (pos, mom, kinds, ghosts, species_scale, mass_table)
        ),
        space=pltpu.HBM,
    )
    cost = pl.CostEstimate(flops=10**9, bytes_accessed=10**6, transcendentals=0)
    halves = [[x * 8 + z * 4 + y for z in range(2)] for x in range(4) for y in range(4)]
    pair = lax.all_gather(mine, "bead", axis=0, axis_index_groups=halves)
    down, up = call(send_kernel, [(8, 128)] * 2, [((8, ATOMS), f32)], (pair, ghosts), ())
    below, above = exchange(down, up)
    (early,) = call(
        early_pack_kernel, [(7, CHUNKS, SLOTS // 8, 8, 128)], [], (pair, neighbours), cost=cost
    )
    block, weights = call(
        pack_kernel,
        [(16, 64, 128), (SLOTS, ATOMS)],
        [((64, 128), f32)],
        (pair, early, below, above, neighbours),
    )
    groups = [[x * 8 + z * 4 + y for x in range(4) for y in range(4)] for z in range(2)]
    gathered = lax.all_to_all(block, "bead", 0, 0, axis_index_groups=groups, tiled=True)
    offsets = ((CB, CHUNKS, SLOTS // 8, 3, 8, 128), f32)
    network = ((CB, NRBF, ATOMS), f32)
    w_in = w_in.T
    coords, veloc, down, up = call(
        begin_kernel,
        [(96, ATOMS), (96, ATOMS), (96, 128), (96, 128)],
        [
            ((96, 768), f32), ((96, ATOMS), f32), ((3, 16, 768), f32), offsets, network, network,
            ((3, 16, ATOMS), f32),
        ],
        (gathered, neighbours, weights, mine, ghosts, w_in, w_out, first, reduce_),
    )
    big = [((3 * 72 + 8, 512), bf16), ((96, ATOMS), f32), ((24, 768), f32), ((24, 8, ATOMS), f32)]
    below, above = exchange(down, up)
    coords, veloc, down, up = call(
        middle_kernel,
        [(96, ATOMS), (96, ATOMS), (96, 128), (96, 128)],
        big,
        (coords, veloc, below, above, neighbours, weights, mine, ghosts, later),
    )
    below, above = exchange(down, up)
    own, contracted, down, up = call(
        last_kernel,
        [(8, ATOMS), (16, ATOMS), (16, 128), (16, 128)],
        [((2 * BEADS + 16, 3 * ATOMS), f32), ((2, 8, ATOMS), f32)] + big,
        (place, coords, veloc, below, above, neighbours, weights, mine, ghosts, last),
        (0,),
    )
    below, above = exchange(down, up)
    (early,) = call(
        early_end_kernel, [(15, CHUNKS, SLOTS // 8, 8, 128)], [], (own, contracted, neighbours), cost=cost
    )
    new_pos, new_mom = call(
        end_kernel,
        [(3, 1, ATOMS), (3, 1, ATOMS)],
        [offsets, network, network, ((CB, 3, CHUNKS, 128), f32)],
        (place, expand, own, contracted, early, below, above, neighbours, weights, w_in, w_out),
        (0, 1),
    )
    return new_pos.transpose(1, 0, 2), new_mom.transpose(1, 0, 2)


def solution(mesh):
    in_specs = (
        P("bead", None, "space"),
        P("bead", None, "space"),
        P(None, "space"),
        P("space"),
        P("space"),
        P(),
        P(),
        P(),
        P(),
    )
    out_specs = (P("bead", None, "space"), P("bead", None, "space"))
    return jax.shard_map(body, mesh=mesh, in_specs=in_specs, out_specs=out_specs, check_vma=False)
```

```python
import functools

import jax
import jax.numpy as jnp
import numpy as np
from jax import lax
from jax.experimental import pallas as pl
from jax.experimental.pallas import tpu as pltpu
from jax.sharding import PartitionSpec as P

BEADS = 32
CB = 4
NINNER = 3
NRBF = 8
H = 128
SLOTS = 32
ATOMS = 512
CHUNKS = 4
WINDOW = 6
N_SPACE = 16

polymer_freq = 10.0
outer_step = 6.0
inner_step = outer_step / NINNER
f32 = jnp.float32
bf16 = jnp.bfloat16
VMEM_LIMIT = 12 * 1024 * 1024


def mode_matrix(count):
    beadpos = np.arange(count)[None, :]
    modeidx = np.arange(count)[:, None]
    middle = count // 2
    cosine = np.sqrt(2.0 / count) * np.cos(2.0 * np.pi * beadpos * modeidx / count)
    sine_rows = np.sqrt(2.0 / count) * np.sin(2.0 * np.pi * beadpos * modeidx / count)
    matrix = np.where(modeidx < middle, cosine, sine_rows)
    matrix = np.where(modeidx == 0, 1.0 / np.sqrt(count), matrix)
    matrix = np.where(modeidx == middle, np.cos(np.pi * beadpos) / np.sqrt(count), matrix)
    return matrix


def polymer_tables(count):
    modes = mode_matrix(count)
    frequency = 2.0 * polymer_freq * np.sin(np.pi * np.arange(count) / count)
    nonzero = np.where(frequency > 0, frequency, 1.0)
    cosine = np.cos(frequency * inner_step)
    drift_gain = np.where(frequency > 0, np.sin(frequency * inner_step) / nonzero, inner_step)
    spring = frequency * np.sin(frequency * inner_step)
    persist = modes.T @ (cosine[:, None] * modes)
    coupling = modes.T @ (drift_gain[:, None] * modes)
    restoring = -(modes.T @ (spring[:, None] * modes))
    return persist, coupling, restoring


def contraction(count, fewer):
    full_modes = mode_matrix(count)
    small_modes = mode_matrix(fewer)
    kept = list(range(fewer // 2 + 1)) + list(range(count - fewer // 2 + 1, count))
    contract = np.sqrt(fewer / count) * (small_modes.T @ full_modes[kept])
    expand = count / fewer * contract.T
    return contract, expand


def bf16_terms(matrix):
    out, rest = [], matrix
    for _ in range(3):
        out.append(rest.astype(np.float32).astype(jnp.bfloat16))
        rest = rest - out[-1].astype(np.float64)
    return out


def three_terms(matrix):
    high, low, _ = bf16_terms(matrix)
    return np.concatenate([high, low, high], axis=1)


def six_terms(matrix):
    high, middle, low = bf16_terms(matrix)
    return np.concatenate([high, high, middle, middle, high, low], axis=1)


BEAD_OF_ROW = np.array([x * 8 + z * 4 + y for z in range(2) for x in range(4) for y in range(4)])


def tables():
    persist, coupling, restoring = polymer_tables(BEADS)
    contract, expand = contraction(BEADS, CB)
    order = BEAD_OF_ROW
    persist, coupling, restoring = (m[np.ix_(order, order)] for m in (persist, coupling, restoring))
    contract, expand = contract[:, order], expand[order]
    step = np.block([[persist, coupling], [restoring, persist]])
    padded_expand = np.concatenate([expand, np.zeros((BEADS, 16 - CB))], axis=1)
    kick = np.concatenate([coupling @ padded_expand, persist @ padded_expand], axis=0)
    first = six_terms(np.concatenate([step, 0.5 * outer_step * kick], axis=1))
    later = six_terms(step)
    padded_contract = np.concatenate([contract, np.zeros((16 - CB, BEADS))], axis=0)
    last = six_terms(np.concatenate([step, padded_contract @ step[:BEADS]], axis=0))
    reduce_ = three_terms(padded_contract)
    return first, later, last.astype(np.float32), reduce_, (0.5 * outer_step * expand).astype(np.float32)


def lanes(source, index):
    return jnp.take_along_axis(source, index, axis=1)


def row8(row):
    return jnp.broadcast_to(row, (8, 128))


def split_rows(value):
    high = value.astype(bf16)
    low = (value - high.astype(f32)).astype(bf16)
    return jnp.concatenate([high, high, low], axis=0)


def dot3(matrix, value):
    return jnp.dot(matrix, split_rows(value), preferred_element_type=f32)


def dot6(matrix, value):
    high = value.astype(bf16)
    rest = value - high.astype(f32)
    middle = rest.astype(bf16)
    low = (rest - middle.astype(f32)).astype(bf16)
    terms = jnp.concatenate([high, middle, high, middle, low, high], axis=0)
    return jnp.dot(matrix, terms, preferred_element_type=f32)


def by_species(species, table):
    return jnp.where(species == 0, table[0], table[1])


def ghosts_of(chunk, index):
    first = chunk(0)
    rows = first.shape[0]
    lane = jnp.broadcast_to(index & 127, (rows, 128))
    part = jnp.broadcast_to(index >> 7, (rows, 128))
    out = lanes(first, lane)
    for k in range(1, CHUNKS):
        out = jnp.where(part == k, lanes(chunk(k), lane), out)
    return out


def tile_index(neighbours, g, a):
    index = neighbours[8 * g : 8 * g + 8, 128 * a : 128 * a + 128]
    return index & 127, [(index >> 7) == k for k in range(1, WINDOW)], index


def looked_up(rows, lane, masks):
    out = lanes(rows[0], lane)
    for k in range(1, WINDOW):
        out = jnp.where(masks[k - 1], lanes(rows[k], lane), out)
    return out


def own_lookup(row, neighbours, g, a):
    index = neighbours[8 * g : 8 * g + 8, 128 * a : 128 * a + 128]
    lane, part = index & 127, index >> 7
    out = lanes(row8(row(0)), lane)
    for k in range(1, CHUNKS):
        out = jnp.where(part == k + 1, lanes(row8(row(k)), lane), out)
    return out


def with_ghosts(early, low, high, index):
    lane, part = index & 127, index >> 7
    out = jnp.where(part == 0, lanes(row8(low), lane), early)
    return jnp.where(part == WINDOW - 1, lanes(row8(high), lane), out)


def cheap_by_lanes(looked, centre, neighbours, weights, a):
    centre = [row8(row) for row in centre]
    total = [jnp.zeros((8, 128), f32) for _ in range(3)]
    for g in range(SLOTS // 8):
        index = neighbours[8 * g : 8 * g + 8, 128 * a : 128 * a + 128]
        offset = [looked(x, g, index) - centre[x] for x in range(3)]
        squared = offset[0] * offset[0] + offset[1] * offset[1] + offset[2] * offset[2]
        w = weights[8 * g : 8 * g + 8, 128 * a : 128 * a + 128] * jnp.exp2(-LOG2E * squared)
        for x in range(3):
            total[x] = total[x] + w * offset[x]
    return [jnp.sum(t, axis=0, keepdims=True) for t in total]


LOG2E = 1.4426950408889634


def roots(squared):
    return jnp.exp2((-0.2 * LOG2E) * squared), jnp.exp2((-0.2 * 2.0**0.5 * LOG2E) * squared)


def powers(even, odd):
    out = [even, odd]
    for _ in range(3):
        even, odd = even * even, odd * odd
        out += [even, odd]
    return out


def learned_by_lanes(looked, centre, neighbours, weights, w_in, w_out, offsets, messages, radials, store):
    high = w_in[...].astype(bf16).astype(f32)
    first = jnp.concatenate([high, w_in[...] - high, high, jnp.zeros_like(high)], axis=0).astype(bf16)
    high = w_out[...].astype(bf16).astype(f32)
    second = jnp.concatenate([high, w_out[...] - high, high], axis=1)
    second = jnp.concatenate([second, jnp.zeros_like(second)], axis=0).astype(bf16)

    def message(c):
        for a in range(CHUNKS):
            middle = [row8(centre(c, x, a)) for x in range(3)]
            total = [jnp.zeros((8, 128), f32) for _ in range(NRBF)]
            for g in range(SLOTS // 8):
                offset = [looked(c, x, a, g) - middle[x] for x in range(3)]
                squared = offset[0] * offset[0] + offset[1] * offset[1] + offset[2] * offset[2]
                even, odd = roots(squared)
                for x in range(3):
                    offsets[c, a, g, x] = offset[x]
                offsets[c, a, g, 3] = even
                offsets[c, a, g, 4] = odd
                w = weights[8 * g : 8 * g + 8, 128 * a : 128 * a + 128]
                for r, basis in enumerate(powers(even, odd)):
                    total[r] = total[r] + w * basis
            for r in range(NRBF):
                messages[c, r : r + 1, 128 * a : 128 * a + 128] = jnp.sum(total[r], axis=0, keepdims=True) * (
                    1.0 / SLOTS
                )

    def network(c):
        value = messages[c]
        high = value.astype(bf16).astype(f32)
        terms = jnp.concatenate([high, high, value - high, jnp.zeros_like(high)], axis=0).astype(bf16)
        hidden = lax.dot_general(first, terms, (((0,), (0,)), ((), ())), preferred_element_type=f32)
        half = 0.5 * hidden
        hidden = half + half * jnp.tanh(half)
        radials[c] = jnp.dot(second, split_rows(hidden), preferred_element_type=f32)[0:NRBF]

    def force(c):
        for a in range(CHUNKS):
            radial = [row8(radials[c, r : r + 1, 128 * a : 128 * a + 128]) for r in range(NRBF)]
            total = [jnp.zeros((8, 128), f32) for _ in range(3)]
            for g in range(SLOTS // 8):
                offset = [offsets[c, a, g, x] for x in range(3)]
                basis = powers(offsets[c, a, g, 3], offsets[c, a, g, 4])
                profile = radial[0] * basis[0]
                for r in range(1, NRBF):
                    profile = profile + radial[r] * basis[r]
                w = weights[8 * g : 8 * g + 8, 128 * a : 128 * a + 128] * profile
                for x in range(3):
                    total[x] = total[x] + w * offset[x]
            for x in range(3):
                store(c, x, a, jnp.sum(total[x], axis=0, keepdims=True))

    message(0)
    for c in range(CB):
        network(c)
        if c + 1 < CB:
            message(c + 1)
        force(c)


def cheap_of_all(coords, below, above, neighbours, weights, stacked, total, table, sums):
    few = BEADS - 8
    rows = 3 * few

    def of_few(value):
        return jnp.concatenate([value[BEADS * x : BEADS * x + few] for x in range(3)], axis=0)

    own, low, high_ = of_few(coords), of_few(below), of_few(above)
    stack = jnp.concatenate(
        [
            jnp.concatenate([low, own[:, 0:128]], axis=1),
            own[:, 128:384],
            jnp.concatenate([own[:, 384:512], high_], axis=1),
            jnp.zeros((8, 256), f32),
        ],
        axis=0,
    )
    high = stack.astype(bf16)
    stacked[:, 0:256] = high
    stacked[:, 256:512] = (stack - high.astype(f32)).astype(bf16)
    rounded = own.astype(bf16).astype(f32)
    rounded = rounded + (own - rounded).astype(bf16).astype(f32)
    for x in range(3):
        at = slice(BEADS * x + few, BEADS * (x + 1))
        table[8 * x : 8 * x + 8, 0:128] = below[at]
        table[8 * x : 8 * x + 8, 128:640] = coords[at]
        table[8 * x : 8 * x + 8, 640:768] = above[at]
    total[...] = jnp.zeros_like(total)
    sums[...] = jnp.zeros_like(sums)
    place = lax.broadcasted_iota(jnp.int16, (256, ATOMS), 0)

    def by_matmul(slot):
        index = neighbours[slot : slot + 1, :]
        column = jnp.broadcast_to(index & 255, (16, ATOMS)).astype(jnp.int16)
        chosen = jnp.where(place == jnp.tile(column, (16, 1)), bf16(1), bf16(0))
        picked = jnp.dot(stacked[...], jnp.concatenate([chosen, chosen], axis=0), preferred_element_type=f32)
        part = index >> 8
        other = jnp.where(
            part == 0,
            picked[0:rows],
            jnp.where(part == 1, picked[rows : 2 * rows], picked[2 * rows : 3 * rows]),
        )
        offset = other - rounded
        x, y, z = offset[0:few], offset[few : 2 * few], offset[2 * few :]
        w = weights[slot : slot + 1, :] * jnp.exp2(-LOG2E * (x * x + y * y + z * z))
        total[0:few] += w * x
        total[BEADS : BEADS + few] += w * y
        total[2 * BEADS : 2 * BEADS + few] += w * z

    def by_lanes(g, a):
        at = slice(128 * a, 128 * a + 128)
        slots = slice(8 * g, 8 * g + 8)
        index = neighbours[slots, at]
        lane, masks = index & 127, [(index >> 7) == k for k in range(1, WINDOW)]
        weight = weights[slots, at]
        for bead in range(8):
            rows_of = lambda x, k: row8(table[8 * x + bead : 8 * x + bead + 1, 128 * k : 128 * k + 128])
            offset = [
                looked_up([rows_of(x, k) for k in range(WINDOW)], lane, masks) - rows_of(x, 1 + a)
                for x in range(3)
            ]
            squared = offset[0] * offset[0] + offset[1] * offset[1] + offset[2] * offset[2]
            w = weight * jnp.exp2(-LOG2E * squared)
            for x in range(3):
                sums[8 * x + bead, :, at] += w * offset[x]

    for g in range(SLOTS // 8):
        for j in range(8):
            by_matmul(g * 8 + j)
            if j % 2:
                by_lanes(g, j // 2)
    for x in range(3):
        for bead in range(8):
            row = BEADS * x + few + bead
            total[row : row + 1] = jnp.sum(sums[8 * x + bead], axis=0, keepdims=True)


def propagated(coords, veloc, table, extra=None):
    wide = []
    for x in range(3):
        at = slice(x * BEADS, (x + 1) * BEADS)
        pieces = [coords[at], veloc[at]]
        if extra is not None:
            pieces.append(extra[x])
        wide.append(jnp.concatenate(pieces, axis=0))
    return dot6(table[...], jnp.concatenate(wide, axis=1))


def first_kernel(
    pos, mom, species, ghost_rows, scale, mass_table, out, ghosts, pos_in, mom_in, species_in, scale_in, mass_in, sems
):
    copies = [
        pltpu.make_async_copy(source, target, sems.at[i])
        for i, (source, target) in enumerate(
            (
                (scale, scale_in), (mass_table, mass_in), (species, species_in), (mom, mom_in), (pos, pos_in),
                (ghost_rows, ghosts),
            )
        )
    ]
    for copy in copies:
        copy.start()
    for copy in copies:
        copy.wait()
    mass = by_species(species_in[...], mass_in)
    for x in range(3):
        out[x : x + 1] = pos_in[x]
        out[3 + x : 4 + x] = mom_in[x] / mass
    out[6:7] = by_species(species_in[...], scale_in)
    out[7:8] = mass


def send_kernel(pair, ghost_rows, down, up, rows):
    rows[0:3] = pair[0, 0:3]
    rows[3:6] = pair[1, 0:3]
    rows[6:8] = pair[0, 6:8]
    chunk = lambda k: rows[:, 128 * k : 128 * k + 128]
    down[...] = ghosts_of(chunk, ghost_rows[0:1])
    up[...] = ghosts_of(chunk, ghost_rows[1:2])


def early_pack_kernel(pair, neighbours, early):
    for a in range(CHUNKS):
        for g in range(SLOTS // 8):
            for k in range(2):
                for x in range(3):
                    early[3 * k + x, a, g] = own_lookup(
                        lambda i: pair[k, x : x + 1, 128 * i : 128 * i + 128], neighbours, g, a
                    )
            early[6, a, g] = own_lookup(lambda i: pair[0, 6:7, 128 * i : 128 * i + 128], neighbours, g, a)


def pack_kernel(pair, early, below, above, neighbours, out, weights, block):
    for k in range(2):
        base = 32 * k
        for x in range(3):
            at = base + 6 * x
            block[at : at + 1] = below[3 * k + x : 3 * k + x + 1]
            for i in range(CHUNKS):
                block[at + 1 + i : at + 2 + i] = pair[k, x : x + 1, 128 * i : 128 * i + 128]
            block[at + 5 : at + 6] = above[3 * k + x : 3 * k + x + 1]
        block[base + 30 : base + 32] = jnp.zeros((2, 128), f32)
    for a in range(CHUNKS):
        itself = 128 + 128 * a + lax.broadcasted_iota(jnp.int32, (8, 128), 1)
        for g in range(SLOTS // 8):
            index = neighbours[8 * g : 8 * g + 8, 128 * a : 128 * a + 128]
            q = with_ghosts(early[6, a, g], below[6:7], above[6:7], index)
            weights[8 * g : 8 * g + 8, 128 * a : 128 * a + 128] = jnp.where(index == itself, 0.0, q)
    for a in range(CHUNKS):
        at = slice(128 * a, 128 * a + 128)
        gain = pair[0, 6:7, at] / pair[0, 7:8, at] * (0.5 * inner_step)
        for k in range(2):
            base = 32 * k

            def looked(x, g, index):
                i = 3 * k + x
                return with_ghosts(early[i, a, g], below[i : i + 1], above[i : i + 1], index)

            force = cheap_by_lanes(looked, [pair[k, x : x + 1, at] for x in range(3)], neighbours, weights, a)
            for x in range(3):
                row = base + 18 + 4 * x + a
                block[row : row + 1] = pair[k, 3 + x : 4 + x, at] + gain * force[x]
    for i in range(16):
        out[i] = block[...]


def begin_kernel(
    gathered, neighbours, weights, mine, ghost_rows, w_in, w_out, first, reduce_,
    coords, veloc, down, up,
    window, start, contracted, offsets, messages, radials, slow,
):
    inverse = 1.0 / mine[7:8]
    for z in range(2):
        for x in range(3):
            at = slice(x * BEADS + 16 * z, x * BEADS + 16 * z + 16)
            for k in range(WINDOW):
                window[at, 128 * k : 128 * k + 128] = gathered[:, 32 * z + 6 * x + k, :]
            for k in range(CHUNKS):
                start[at, 128 * k : 128 * k + 128] = gathered[:, 32 * z + 18 + 4 * x + k, :]
    for x in range(3):
        contracted[x] = dot3(reduce_[...], window[x * BEADS : (x + 1) * BEADS, :])
    slow[...] = jnp.zeros_like(slow)

    def store(c, x, a, value):
        slow[x, c : c + 1, 128 * a : 128 * a + 128] = value

    def looked(c, x, a, g):
        rows = [row8(contracted[x, c : c + 1, 128 * k : 128 * k + 128]) for k in range(WINDOW)]
        lane, masks, _ = tile_index(neighbours, g, a)
        return looked_up(rows, lane, masks)

    learned_by_lanes(
        looked, lambda c, x, a: contracted[x, c : c + 1, 128 + 128 * a : 256 + 128 * a], neighbours, weights, w_in, w_out, offsets, messages, radials, store,
    )
    moved = propagated(
        window[:, 128:640], start[...], first, [slow[x] * inverse for x in range(3)]
    )
    finish_step(moved, coords, veloc, ghost_rows, down, up)


def finish_step(moved, coords, veloc, ghost_rows, down, up):
    for x in range(3):
        at = slice(x * BEADS, (x + 1) * BEADS)
        coords[at] = moved[0:BEADS, ATOMS * x : ATOMS * (x + 1)]
        veloc[at] = moved[BEADS : 2 * BEADS, ATOMS * x : ATOMS * (x + 1)]
    for i in range(3 * BEADS // 8):
        chunk = lambda k: coords[8 * i : 8 * i + 8, 128 * k : 128 * k + 128]
        down[8 * i : 8 * i + 8] = ghosts_of(chunk, ghost_rows[0:1])
        up[8 * i : 8 * i + 8] = ghosts_of(chunk, ghost_rows[1:2])


def kicked(coords, veloc, below, above, neighbours, weights, mine, scratch):
    total = scratch[1]
    cheap_of_all(coords, below, above, neighbours, weights, *scratch)
    return veloc[...] + inner_step * mine[6:7] / mine[7:8] * total[...]


def middle_kernel(
    coords, veloc, below, above, neighbours, weights, mine, ghost_rows, later, new_coords, new_veloc, down, up, *scratch
):
    velocities = kicked(coords, veloc, below, above, neighbours, weights, mine, scratch)
    moved = propagated(coords[...], velocities, later)
    finish_step(moved, new_coords, new_veloc, ghost_rows, down, up)


def last_kernel(
    place, coords, veloc, below, above, neighbours, weights, mine, ghost_rows, last,
    own, contracted, down, up, chosen, rows, *scratch,
):
    chosen[...] = jnp.zeros_like(chosen)
    for i, row in enumerate((place[1], BEADS + place[1], place[2], place[3])):
        chosen[i : i + 1] = last[pl.ds(row, 1)]
    chosen[4:8] = last[2 * BEADS : 2 * BEADS + CB]
    table = chosen[...].astype(bf16)
    velocities = kicked(coords, veloc, below, above, neighbours, weights, mine, scratch)
    moved = propagated(coords[...], velocities, table)
    for x in range(3):
        part = moved[:, ATOMS * x : ATOMS * (x + 1)]
        own[x : x + 1] = part[0:1]
        own[3 + x : 4 + x] = part[1:2]
        contracted[4 * x : 4 * x + 4] = part[4:8]
        rows[0, 4 + x : 5 + x] = part[2:3]
        rows[1, 4 + x : 5 + x] = part[3:4]
    own[6:8] = mine[6:8]
    contracted[12:16] = jnp.zeros((4, ATOMS), f32)
    for which, out in ((0, down), (1, up)):
        rows[which, 0:4] = contracted[8:12]
        rows[which, 7:8] = mine[6:7]
        index = ghost_rows[which : which + 1]
        out[0:8] = ghosts_of(lambda k: contracted[0:8, 128 * k : 128 * k + 128], index)
        out[8:16] = ghosts_of(lambda k: rows[which, :, 128 * k : 128 * k + 128], index)


def early_end_kernel(own, contracted, neighbours, early):
    for a in range(CHUNKS):
        for g in range(SLOTS // 8):
            for i in range(15):
                source, row = (contracted, i) if i < 12 else (own, i - 12)
                early[i, a, g] = own_lookup(
                    lambda k: source[row : row + 1, 128 * k : 128 * k + 128], neighbours, g, a
                )


def end_kernel(
    place, expand, own, contracted, early, below, above, neighbours, weights, w_in, w_out,
    new_pos, new_mom,
    offsets, messages, radials, slow,
):
    charge, mass = own[6:7], own[7:8]

    def store(c, x, a, value):
        slow[c, x, a : a + 1] = value

    def looked_at(i, a, g):
        index = neighbours[8 * g : 8 * g + 8, 128 * a : 128 * a + 128]
        return with_ghosts(early[i, a, g], below[i : i + 1], above[i : i + 1], index)

    learned_by_lanes(
        lambda c, x, a, g: looked_at(4 * x + c, a, g),
        lambda c, x, a: contracted[4 * x + c : 4 * x + c + 1, 128 * a : 128 * a + 128],
        neighbours, weights, w_in, w_out, offsets, messages, radials, store,
    )
    for a in range(CHUNKS):
        at = slice(128 * a, 128 * a + 128)
        force = cheap_by_lanes(
            lambda x, g, index: looked_at(12 + x, a, g), [own[x : x + 1, at] for x in range(3)], neighbours, weights, a
        )
        for x in range(3):
            value = mass[:, at] * own[3 + x : 4 + x, at] + (0.5 * inner_step) * charge[:, at] * force[x]
            for c in range(CB):
                value = value + expand[place[1], c] * slow[c, x, a : a + 1]
            new_mom[x, :, at] = value
            new_pos[x, :, at] = own[x : x + 1, at]


def call(kernel, outs, scratch, args, scalars=(), space=pltpu.VMEM, cost=None):
    specs = [pl.BlockSpec(memory_space=pltpu.SMEM if i in scalars else space) for i in range(len(args))]
    shapes = [s if isinstance(s, jax.ShapeDtypeStruct) else jax.ShapeDtypeStruct(s, f32) for s in outs]
    return pl.pallas_call(
        kernel,
        out_shape=shapes,
        in_specs=specs,
        out_specs=[pl.BlockSpec(memory_space=pltpu.VMEM)] * len(outs),
        scratch_shapes=[pltpu.VMEM(*s) if isinstance(s, tuple) else s for s in scratch],
        compiler_params=pltpu.CompilerParams(vmem_limit_bytes=VMEM_LIMIT),
        cost_estimate=cost,
    )(*args)


RING = ("bead", "space")


def ring(step):
    pairs = []
    for bead in range(BEADS):
        for domain in range(N_SPACE):
            to = domain + step
            other = bead if 0 <= to < N_SPACE else bead ^ 4
            pairs.append((bead * N_SPACE + domain, other * N_SPACE + to % N_SPACE))
    return pairs


def exchange(down, up):
    below = lax.ppermute(up, RING, ring(1))
    above = lax.ppermute(down, RING, ring(-1))
    return below, above


def body(
    positions, momenta, neighbours, ghost_rows, species, species_scale, mass_table, w_in, w_out
):
    first, later, last, reduce_, expand = tables()
    first, later, last, reduce_ = (jnp.asarray(t) for t in (first, later, last, reduce_))
    expand = jnp.asarray(expand)
    bead = lax.axis_index("bead")
    domain = lax.axis_index("space")
    half = (bead // 4) % 2
    row = half * 16 + (bead // 8) * 4 + bead % 4
    other = (1 - half) * 16 + (bead // 8) * 4 + bead % 4
    row_below = jnp.where(domain == 0, other, row)
    row_above = jnp.where(domain == N_SPACE - 1, other, row)
    place = jnp.stack([half, row, row_below, row_above]).astype(jnp.int32)

    pos = positions.transpose(1, 0, 2)
    mom = momenta.transpose(1, 0, 2)
    kinds = species.reshape(1, ATOMS)
    ghosts = ghost_rows.reshape(2, 128)

    mine, ghosts = call(
        first_kernel,
        [(8, ATOMS), jax.ShapeDtypeStruct((2, 128), jnp.int32)],
        [
            ((3, 1, ATOMS), f32), ((3, 1, ATOMS), f32), ((1, ATOMS), jnp.int32),
            pltpu.SMEM((2,), f32), pltpu.SMEM((2,), f32), pltpu.SemaphoreType.DMA((6,)),
        ],
        tuple(
            pltpu.with_memory_space_constraint(v, pltpu.HBM)
            for v in (pos, mom, kinds, ghosts, species_scale, mass_table)
        ),
        space=pltpu.HBM,
    )
    cost = pl.CostEstimate(flops=10**9, bytes_accessed=10**6, transcendentals=0)
    halves = [[x * 8 + z * 4 + y for z in range(2)] for x in range(4) for y in range(4)]
    pair = lax.all_gather(mine, "bead", axis=0, axis_index_groups=halves)
    down, up = call(send_kernel, [(8, 128)] * 2, [((8, ATOMS), f32)], (pair, ghosts), ())
    below, above = exchange(down, up)
    (early,) = call(
        early_pack_kernel, [(7, CHUNKS, SLOTS // 8, 8, 128)], [], (pair, neighbours), cost=cost
    )
    block, weights = call(
        pack_kernel,
        [(16, 64, 128), (SLOTS, ATOMS)],
        [((64, 128), f32)],
        (pair, early, below, above, neighbours),
    )
    groups = [[x * 8 + z * 4 + y for x in range(4) for y in range(4)] for z in range(2)]
    gathered = lax.all_to_all(block, "bead", 0, 0, axis_index_groups=groups, tiled=True)
    offsets = ((CB, CHUNKS, SLOTS // 8, 5, 8, 128), f32)
    network = ((CB, NRBF, ATOMS), f32)
    w_in = w_in.T
    coords, veloc, down, up = call(
        begin_kernel,
        [(96, ATOMS), (96, ATOMS), (96, 128), (96, 128)],
        [
            ((96, 768), f32), ((96, ATOMS), f32), ((3, 16, 768), f32), offsets, network, network,
            ((3, 16, ATOMS), f32),
        ],
        (gathered, neighbours, weights, mine, ghosts, w_in, w_out, first, reduce_),
    )
    big = [((3 * 72 + 8, 512), bf16), ((96, ATOMS), f32), ((24, 768), f32), ((24, 8, ATOMS), f32)]
    below, above = exchange(down, up)
    coords, veloc, down, up = call(
        middle_kernel,
        [(96, ATOMS), (96, ATOMS), (96, 128), (96, 128)],
        big,
        (coords, veloc, below, above, neighbours, weights, mine, ghosts, later),
    )
    below, above = exchange(down, up)
    own, contracted, down, up = call(
        last_kernel,
        [(8, ATOMS), (16, ATOMS), (16, 128), (16, 128)],
        [((16, 384), f32), ((2, 8, ATOMS), f32)] + big,
        (place, coords, veloc, below, above, neighbours, weights, mine, ghosts, last),
        (0,),
    )
    below, above = exchange(down, up)
    (early,) = call(
        early_end_kernel, [(15, CHUNKS, SLOTS // 8, 8, 128)], [], (own, contracted, neighbours), cost=cost
    )
    new_pos, new_mom = call(
        end_kernel,
        [(3, 1, ATOMS), (3, 1, ATOMS)],
        [offsets, network, network, ((CB, 3, CHUNKS, 128), f32)],
        (place, expand, own, contracted, early, below, above, neighbours, weights, w_in, w_out),
        (0, 1),
    )
    return new_pos.transpose(1, 0, 2), new_mom.transpose(1, 0, 2)


def solution(mesh):
    in_specs = (
        P("bead", None, "space"),
        P("bead", None, "space"),
        P(None, "space"),
        P("space"),
        P("space"),
        P(),
        P(),
        P(),
        P(),
    )
    out_specs = (P("bead", None, "space"), P("bead", None, "space"))
    return jax.shard_map(body, mesh=mesh, in_specs=in_specs, out_specs=out_specs, check_vma=False)
```

```python
import functools

import jax
import jax.numpy as jnp
import numpy as np
from jax import lax
from jax.experimental import pallas as pl
from jax.experimental.pallas import tpu as pltpu
from jax.sharding import PartitionSpec as P

BEADS = 32
CB = 4
NINNER = 3
NRBF = 8
H = 128
SLOTS = 32
ATOMS = 512
CHUNKS = 4
WINDOW = 6
N_SPACE = 16

polymer_freq = 10.0
outer_step = 6.0
inner_step = outer_step / NINNER
f32 = jnp.float32
bf16 = jnp.bfloat16
VMEM_LIMIT = 12 * 1024 * 1024


def mode_matrix(count):
    beadpos = np.arange(count)[None, :]
    modeidx = np.arange(count)[:, None]
    middle = count // 2
    cosine = np.sqrt(2.0 / count) * np.cos(2.0 * np.pi * beadpos * modeidx / count)
    sine_rows = np.sqrt(2.0 / count) * np.sin(2.0 * np.pi * beadpos * modeidx / count)
    matrix = np.where(modeidx < middle, cosine, sine_rows)
    matrix = np.where(modeidx == 0, 1.0 / np.sqrt(count), matrix)
    matrix = np.where(modeidx == middle, np.cos(np.pi * beadpos) / np.sqrt(count), matrix)
    return matrix


def polymer_tables(count):
    modes = mode_matrix(count)
    frequency = 2.0 * polymer_freq * np.sin(np.pi * np.arange(count) / count)
    nonzero = np.where(frequency > 0, frequency, 1.0)
    cosine = np.cos(frequency * inner_step)
    drift_gain = np.where(frequency > 0, np.sin(frequency * inner_step) / nonzero, inner_step)
    spring = frequency * np.sin(frequency * inner_step)
    persist = modes.T @ (cosine[:, None] * modes)
    coupling = modes.T @ (drift_gain[:, None] * modes)
    restoring = -(modes.T @ (spring[:, None] * modes))
    return persist, coupling, restoring


def contraction(count, fewer):
    full_modes = mode_matrix(count)
    small_modes = mode_matrix(fewer)
    kept = list(range(fewer // 2 + 1)) + list(range(count - fewer // 2 + 1, count))
    contract = np.sqrt(fewer / count) * (small_modes.T @ full_modes[kept])
    expand = count / fewer * contract.T
    return contract, expand


def bf16_terms(matrix):
    out, rest = [], matrix
    for _ in range(3):
        out.append(rest.astype(np.float32).astype(jnp.bfloat16))
        rest = rest - out[-1].astype(np.float64)
    return out


def three_terms(matrix):
    high, low, _ = bf16_terms(matrix)
    return np.concatenate([high, low, high], axis=1)


def six_terms(matrix):
    high, middle, low = bf16_terms(matrix)
    return np.concatenate([high, high, middle, middle, high, low], axis=1)


BEAD_OF_ROW = np.array([x * 8 + z * 4 + y for z in range(2) for x in range(4) for y in range(4)])


def tables():
    persist, coupling, restoring = polymer_tables(BEADS)
    contract, expand = contraction(BEADS, CB)
    order = BEAD_OF_ROW
    persist, coupling, restoring = (m[np.ix_(order, order)] for m in (persist, coupling, restoring))
    contract, expand = contract[:, order], expand[order]
    step = np.block([[persist, coupling], [restoring, persist]])
    padded_expand = np.concatenate([expand, np.zeros((BEADS, 16 - CB))], axis=1)
    kick = np.concatenate([coupling @ padded_expand, persist @ padded_expand], axis=0)
    first = six_terms(np.concatenate([step, 0.5 * outer_step * kick], axis=1))
    later = six_terms(step)
    padded_contract = np.concatenate([contract, np.zeros((16 - CB, BEADS))], axis=0)
    reduce_ = three_terms(padded_contract)
    contracted = contract @ step[:BEADS]
    last = np.zeros((BEADS, 3, 16, 6 * 2 * BEADS), jnp.bfloat16)
    gains = np.zeros((BEADS, 8, 128), np.float32)
    for row, bead in enumerate(order):
        gains[bead, :CB] = 0.5 * outer_step * expand[row][:, None]
        for place in range(3):
            below = row ^ 16 if place == 0 else row
            above = row ^ 16 if place == 2 else row
            last[bead, place, :8] = six_terms(np.concatenate([step[[row, BEADS + row, below, above]], contracted]))
    return first, later, last.reshape(3 * BEADS, 16, -1), reduce_, gains


def lanes(source, index):
    return jnp.take_along_axis(source, index, axis=1)


def row8(row):
    return jnp.broadcast_to(row, (8, 128))


def split_rows(value):
    high = value.astype(bf16)
    low = (value - high.astype(f32)).astype(bf16)
    return jnp.concatenate([high, high, low], axis=0)


def dot3(matrix, value):
    return jnp.dot(matrix, split_rows(value), preferred_element_type=f32)


def dot6(matrix, value):
    high = value.astype(bf16)
    rest = value - high.astype(f32)
    middle = rest.astype(bf16)
    low = (rest - middle.astype(f32)).astype(bf16)
    terms = jnp.concatenate([high, middle, high, middle, low, high], axis=0)
    return jnp.dot(matrix, terms, preferred_element_type=f32)


def by_species(species, table):
    return jnp.where(species == 0, table[0], table[1])


def ghosts_of(chunk, index):
    first = chunk(0)
    rows = first.shape[0]
    lane = jnp.broadcast_to(index & 127, (rows, 128))
    part = jnp.broadcast_to(index >> 7, (rows, 128))
    out = lanes(first, lane)
    for k in range(1, CHUNKS):
        out = jnp.where(part == k, lanes(chunk(k), lane), out)
    return out


def tile_index(neighbours, g, a):
    index = neighbours[8 * g : 8 * g + 8, 128 * a : 128 * a + 128]
    return index & 127, [(index >> 7) == k for k in range(1, WINDOW)], index


def looked_up(rows, lane, masks):
    out = lanes(rows[0], lane)
    for k in range(1, WINDOW):
        out = jnp.where(masks[k - 1], lanes(rows[k], lane), out)
    return out


def own_lookup(row, neighbours, g, a):
    index = neighbours[8 * g : 8 * g + 8, 128 * a : 128 * a + 128]
    lane, part = index & 127, index >> 7
    out = lanes(row8(row(0)), lane)
    for k in range(1, CHUNKS):
        out = jnp.where(part == k + 1, lanes(row8(row(k)), lane), out)
    return out


def with_ghosts(early, low, high, index):
    lane, part = index & 127, index >> 7
    out = jnp.where(part == 0, lanes(row8(low), lane), early)
    return jnp.where(part == WINDOW - 1, lanes(row8(high), lane), out)


def cheap_by_lanes(looked, centre, neighbours, weights, a):
    centre = [row8(row) for row in centre]
    total = [jnp.zeros((8, 128), f32) for _ in range(3)]
    for g in range(SLOTS // 8):
        index = neighbours[8 * g : 8 * g + 8, 128 * a : 128 * a + 128]
        offset = [looked(x, g, index) - centre[x] for x in range(3)]
        squared = offset[0] * offset[0] + offset[1] * offset[1] + offset[2] * offset[2]
        w = weights[8 * g : 8 * g + 8, 128 * a : 128 * a + 128] * jnp.exp2(-LOG2E * squared)
        for x in range(3):
            total[x] = total[x] + w * offset[x]
    return [jnp.sum(t, axis=0, keepdims=True) for t in total]


LOG2E = 1.4426950408889634


def roots(squared):
    return jnp.exp2((-0.2 * LOG2E) * squared), jnp.exp2((-0.2 * 2.0**0.5 * LOG2E) * squared)


def powers(even, odd):
    out = [even, odd]
    for _ in range(3):
        even, odd = even * even, odd * odd
        out += [even, odd]
    return out


def learned_by_lanes(looked, centre, neighbours, weights, w_in, w_out, offsets, messages, radials, store):
    high = w_in[...].astype(bf16).astype(f32)
    first = jnp.concatenate([high, w_in[...] - high, high, jnp.zeros_like(high)], axis=0).astype(bf16)
    high = w_out[...].astype(bf16).astype(f32)
    second = jnp.concatenate([high, w_out[...] - high, high], axis=1)
    second = jnp.concatenate([second, jnp.zeros_like(second)], axis=0).astype(bf16)

    def message(c):
        for a in range(CHUNKS):
            middle = [row8(centre(c, x, a)) for x in range(3)]
            total = [jnp.zeros((8, 128), f32) for _ in range(NRBF)]
            for g in range(SLOTS // 8):
                offset = [looked(c, x, a, g) - middle[x] for x in range(3)]
                squared = offset[0] * offset[0] + offset[1] * offset[1] + offset[2] * offset[2]
                even, odd = roots(squared)
                for x in range(3):
                    offsets[c, a, g, x] = offset[x]
                offsets[c, a, g, 3] = even
                offsets[c, a, g, 4] = odd
                w = weights[8 * g : 8 * g + 8, 128 * a : 128 * a + 128]
                for r, basis in enumerate(powers(even, odd)):
                    total[r] = total[r] + w * basis
            for r in range(NRBF):
                messages[c, r : r + 1, 128 * a : 128 * a + 128] = jnp.sum(total[r], axis=0, keepdims=True) * (
                    1.0 / SLOTS
                )

    def network(c):
        value = messages[c]
        high = value.astype(bf16).astype(f32)
        terms = jnp.concatenate([high, high, value - high, jnp.zeros_like(high)], axis=0).astype(bf16)
        hidden = lax.dot_general(first, terms, (((0,), (0,)), ((), ())), preferred_element_type=f32)
        half = 0.5 * hidden
        hidden = half + half * jnp.tanh(half)
        radials[c] = jnp.dot(second, split_rows(hidden), preferred_element_type=f32)[0:NRBF]

    def force(c):
        for a in range(CHUNKS):
            radial = [row8(radials[c, r : r + 1, 128 * a : 128 * a + 128]) for r in range(NRBF)]
            total = [jnp.zeros((8, 128), f32) for _ in range(3)]
            for g in range(SLOTS // 8):
                offset = [offsets[c, a, g, x] for x in range(3)]
                basis = powers(offsets[c, a, g, 3], offsets[c, a, g, 4])
                profile = radial[0] * basis[0]
                for r in range(1, NRBF):
                    profile = profile + radial[r] * basis[r]
                w = weights[8 * g : 8 * g + 8, 128 * a : 128 * a + 128] * profile
                for x in range(3):
                    total[x] = total[x] + w * offset[x]
            for x in range(3):
                store(c, x, a, jnp.sum(total[x], axis=0, keepdims=True))

    message(0)
    for c in range(CB):
        network(c)
        if c + 1 < CB:
            message(c + 1)
        force(c)


def cheap_of_all(coords, below, above, neighbours, weights, stacked, total, table, sums):
    few = BEADS - 8
    rows = 3 * few

    def of_few(value):
        return jnp.concatenate([value[BEADS * x : BEADS * x + few] for x in range(3)], axis=0)

    own, low, high_ = of_few(coords), of_few(below), of_few(above)
    stack = jnp.concatenate(
        [
            jnp.concatenate([low, own[:, 0:128]], axis=1),
            own[:, 128:384],
            jnp.concatenate([own[:, 384:512], high_], axis=1),
            jnp.zeros((8, 256), f32),
        ],
        axis=0,
    )
    high = stack.astype(bf16)
    stacked[:, 0:256] = high
    stacked[:, 256:512] = (stack - high.astype(f32)).astype(bf16)
    rounded = own.astype(bf16).astype(f32)
    rounded = rounded + (own - rounded).astype(bf16).astype(f32)
    for x in range(3):
        at = slice(BEADS * x + few, BEADS * (x + 1))
        table[8 * x : 8 * x + 8, 0:128] = below[at]
        table[8 * x : 8 * x + 8, 128:640] = coords[at]
        table[8 * x : 8 * x + 8, 640:768] = above[at]
    total[...] = jnp.zeros_like(total)
    sums[...] = jnp.zeros_like(sums)
    place = lax.broadcasted_iota(jnp.int16, (256, ATOMS), 0)

    def by_matmul(slot):
        index = neighbours[slot : slot + 1, :]
        column = jnp.broadcast_to(index & 255, (16, ATOMS)).astype(jnp.int16)
        chosen = jnp.where(place == jnp.tile(column, (16, 1)), bf16(1), bf16(0))
        picked = jnp.dot(stacked[...], jnp.concatenate([chosen, chosen], axis=0), preferred_element_type=f32)
        part = index >> 8
        other = jnp.where(
            part == 0,
            picked[0:rows],
            jnp.where(part == 1, picked[rows : 2 * rows], picked[2 * rows : 3 * rows]),
        )
        offset = other - rounded
        x, y, z = offset[0:few], offset[few : 2 * few], offset[2 * few :]
        w = weights[slot : slot + 1, :] * jnp.exp2(-LOG2E * (x * x + y * y + z * z))
        total[0:few] += w * x
        total[BEADS : BEADS + few] += w * y
        total[2 * BEADS : 2 * BEADS + few] += w * z

    def by_lanes(g, a):
        at = slice(128 * a, 128 * a + 128)
        slots = slice(8 * g, 8 * g + 8)
        index = neighbours[slots, at]
        lane, masks = index & 127, [(index >> 7) == k for k in range(1, WINDOW)]
        weight = weights[slots, at]
        for bead in range(8):
            rows_of = lambda x, k: row8(table[8 * x + bead : 8 * x + bead + 1, 128 * k : 128 * k + 128])
            offset = [
                looked_up([rows_of(x, k) for k in range(WINDOW)], lane, masks) - rows_of(x, 1 + a)
                for x in range(3)
            ]
            squared = offset[0] * offset[0] + offset[1] * offset[1] + offset[2] * offset[2]
            w = weight * jnp.exp2(-LOG2E * squared)
            for x in range(3):
                sums[8 * x + bead, :, at] += w * offset[x]

    for g in range(SLOTS // 8):
        for j in range(8):
            by_matmul(g * 8 + j)
            if j % 2:
                by_lanes(g, j // 2)
    for x in range(3):
        for bead in range(8):
            row = BEADS * x + few + bead
            total[row : row + 1] = jnp.sum(sums[8 * x + bead], axis=0, keepdims=True)


def propagated(coords, veloc, table, extra=None):
    wide = []
    for x in range(3):
        at = slice(x * BEADS, (x + 1) * BEADS)
        pieces = [coords[at], veloc[at]]
        if extra is not None:
            pieces.append(extra[x])
        wide.append(jnp.concatenate(pieces, axis=0))
    return dot6(table[...], jnp.concatenate(wide, axis=1))


def first_kernel(
    pos, mom, species, ghost_rows, scale, mass_table, all_last, all_gains,
    out, ghosts, last, gains,
    pos_in, mom_in, species_in, scale_in, mass_in, sems,
):
    bead, domain = lax.axis_index("bead"), lax.axis_index("space")
    place = jnp.where(domain == 0, 0, jnp.where(domain == N_SPACE - 1, 2, 1))
    copies = [
        pltpu.make_async_copy(source, target, sems.at[i])
        for i, (source, target) in enumerate(
            (
                (scale, scale_in), (mass_table, mass_in), (species, species_in), (mom, mom_in), (pos, pos_in),
                (ghost_rows, ghosts), (all_last.at[3 * bead + place], last), (all_gains.at[bead], gains),
            )
        )
    ]
    for copy in copies:
        copy.start()
    for copy in copies[:5]:
        copy.wait()
    mass = by_species(species_in[...], mass_in)
    for x in range(3):
        out[x : x + 1] = pos_in[x]
        out[3 + x : 4 + x] = mom_in[x] / mass
    out[6:7] = by_species(species_in[...], scale_in)
    out[7:8] = mass
    for copy in copies[5:]:
        copy.wait()


def send_kernel(pair, ghost_rows, down, up, rows):
    rows[0:3] = pair[0, 0:3]
    rows[3:6] = pair[1, 0:3]
    rows[6:8] = pair[0, 6:8]
    chunk = lambda k: rows[:, 128 * k : 128 * k + 128]
    down[...] = ghosts_of(chunk, ghost_rows[0:1])
    up[...] = ghosts_of(chunk, ghost_rows[1:2])


def early_pack_kernel(pair, neighbours, early):
    for a in range(CHUNKS):
        for g in range(SLOTS // 8):
            for k in range(2):
                for x in range(3):
                    early[3 * k + x, a, g] = own_lookup(
                        lambda i: pair[k, x : x + 1, 128 * i : 128 * i + 128], neighbours, g, a
                    )
            early[6, a, g] = own_lookup(lambda i: pair[0, 6:7, 128 * i : 128 * i + 128], neighbours, g, a)


def pack_kernel(pair, early, below, above, neighbours, out, weights, block):
    for k in range(2):
        base = 32 * k
        for x in range(3):
            at = base + 6 * x
            block[at : at + 1] = below[3 * k + x : 3 * k + x + 1]
            for i in range(CHUNKS):
                block[at + 1 + i : at + 2 + i] = pair[k, x : x + 1, 128 * i : 128 * i + 128]
            block[at + 5 : at + 6] = above[3 * k + x : 3 * k + x + 1]
        block[base + 30 : base + 32] = jnp.zeros((2, 128), f32)
    for a in range(CHUNKS):
        itself = 128 + 128 * a + lax.broadcasted_iota(jnp.int32, (8, 128), 1)
        for g in range(SLOTS // 8):
            index = neighbours[8 * g : 8 * g + 8, 128 * a : 128 * a + 128]
            q = with_ghosts(early[6, a, g], below[6:7], above[6:7], index)
            weights[8 * g : 8 * g + 8, 128 * a : 128 * a + 128] = jnp.where(index == itself, 0.0, q)
    for a in range(CHUNKS):
        at = slice(128 * a, 128 * a + 128)
        gain = pair[0, 6:7, at] / pair[0, 7:8, at] * (0.5 * inner_step)
        for k in range(2):
            base = 32 * k

            def looked(x, g, index):
                i = 3 * k + x
                return with_ghosts(early[i, a, g], below[i : i + 1], above[i : i + 1], index)

            force = cheap_by_lanes(looked, [pair[k, x : x + 1, at] for x in range(3)], neighbours, weights, a)
            for x in range(3):
                row = base + 18 + 4 * x + a
                block[row : row + 1] = pair[k, 3 + x : 4 + x, at] + gain * force[x]
    for i in range(16):
        out[i] = block[...]


def begin_kernel(
    gathered, neighbours, weights, mine, ghost_rows, w_in, w_out, first, reduce_,
    coords, veloc, down, up,
    window, start, contracted, offsets, messages, radials, slow,
):
    inverse = 1.0 / mine[7:8]
    for z in range(2):
        for x in range(3):
            at = slice(x * BEADS + 16 * z, x * BEADS + 16 * z + 16)
            for k in range(WINDOW):
                window[at, 128 * k : 128 * k + 128] = gathered[:, 32 * z + 6 * x + k, :]
            for k in range(CHUNKS):
                start[at, 128 * k : 128 * k + 128] = gathered[:, 32 * z + 18 + 4 * x + k, :]
    for x in range(3):
        contracted[x] = dot3(reduce_[...], window[x * BEADS : (x + 1) * BEADS, :])
    slow[...] = jnp.zeros_like(slow)

    def store(c, x, a, value):
        slow[x, c : c + 1, 128 * a : 128 * a + 128] = value

    def looked(c, x, a, g):
        rows = [row8(contracted[x, c : c + 1, 128 * k : 128 * k + 128]) for k in range(WINDOW)]
        lane, masks, _ = tile_index(neighbours, g, a)
        return looked_up(rows, lane, masks)

    learned_by_lanes(
        looked, lambda c, x, a: contracted[x, c : c + 1, 128 + 128 * a : 256 + 128 * a], neighbours, weights, w_in, w_out, offsets, messages, radials, store,
    )
    moved = propagated(
        window[:, 128:640], start[...], first, [slow[x] * inverse for x in range(3)]
    )
    finish_step(moved, coords, veloc, ghost_rows, down, up)


def finish_step(moved, coords, veloc, ghost_rows, down, up):
    for x in range(3):
        at = slice(x * BEADS, (x + 1) * BEADS)
        coords[at] = moved[0:BEADS, ATOMS * x : ATOMS * (x + 1)]
        veloc[at] = moved[BEADS : 2 * BEADS, ATOMS * x : ATOMS * (x + 1)]
    for i in range(3 * BEADS // 8):
        chunk = lambda k: coords[8 * i : 8 * i + 8, 128 * k : 128 * k + 128]
        down[8 * i : 8 * i + 8] = ghosts_of(chunk, ghost_rows[0:1])
        up[8 * i : 8 * i + 8] = ghosts_of(chunk, ghost_rows[1:2])


def kicked(coords, veloc, below, above, neighbours, weights, mine, scratch):
    total = scratch[1]
    cheap_of_all(coords, below, above, neighbours, weights, *scratch)
    return veloc[...] + inner_step * mine[6:7] / mine[7:8] * total[...]


def middle_kernel(
    coords, veloc, below, above, neighbours, weights, mine, ghost_rows, later, new_coords, new_veloc, down, up, *scratch
):
    velocities = kicked(coords, veloc, below, above, neighbours, weights, mine, scratch)
    moved = propagated(coords[...], velocities, later)
    finish_step(moved, new_coords, new_veloc, ghost_rows, down, up)


def last_kernel(
    coords, veloc, below, above, neighbours, weights, mine, ghost_rows, last,
    own, contracted, down, up, rows, *scratch,
):
    velocities = kicked(coords, veloc, below, above, neighbours, weights, mine, scratch)
    moved = propagated(coords[...], velocities, last)
    for x in range(3):
        part = moved[:, ATOMS * x : ATOMS * (x + 1)]
        own[x : x + 1] = part[0:1]
        own[3 + x : 4 + x] = part[1:2]
        contracted[4 * x : 4 * x + 4] = part[4:8]
        rows[0, 4 + x : 5 + x] = part[2:3]
        rows[1, 4 + x : 5 + x] = part[3:4]
    own[6:8] = mine[6:8]
    contracted[12:16] = jnp.zeros((4, ATOMS), f32)
    for which, out in ((0, down), (1, up)):
        rows[which, 0:4] = contracted[8:12]
        rows[which, 7:8] = mine[6:7]
        index = ghost_rows[which : which + 1]
        out[0:8] = ghosts_of(lambda k: contracted[0:8, 128 * k : 128 * k + 128], index)
        out[8:16] = ghosts_of(lambda k: rows[which, :, 128 * k : 128 * k + 128], index)


def early_end_kernel(own, contracted, neighbours, early):
    for a in range(CHUNKS):
        for g in range(SLOTS // 8):
            for i in range(15):
                source, row = (contracted, i) if i < 12 else (own, i - 12)
                early[i, a, g] = own_lookup(
                    lambda k: source[row : row + 1, 128 * k : 128 * k + 128], neighbours, g, a
                )


def end_kernel(
    gains, own, contracted, early, below, above, neighbours, weights, w_in, w_out,
    new_pos, new_mom,
    offsets, messages, radials, slow,
):
    charge, mass = own[6:7], own[7:8]

    def store(c, x, a, value):
        slow[c, x, a : a + 1] = value

    def looked_at(i, a, g):
        index = neighbours[8 * g : 8 * g + 8, 128 * a : 128 * a + 128]
        return with_ghosts(early[i, a, g], below[i : i + 1], above[i : i + 1], index)

    learned_by_lanes(
        lambda c, x, a, g: looked_at(4 * x + c, a, g),
        lambda c, x, a: contracted[4 * x + c : 4 * x + c + 1, 128 * a : 128 * a + 128],
        neighbours, weights, w_in, w_out, offsets, messages, radials, store,
    )
    for a in range(CHUNKS):
        at = slice(128 * a, 128 * a + 128)
        force = cheap_by_lanes(
            lambda x, g, index: looked_at(12 + x, a, g), [own[x : x + 1, at] for x in range(3)], neighbours, weights, a
        )
        for x in range(3):
            value = mass[:, at] * own[3 + x : 4 + x, at] + (0.5 * inner_step) * charge[:, at] * force[x]
            for c in range(CB):
                value = value + gains[c : c + 1] * slow[c, x, a : a + 1]
            new_mom[x, :, at] = value
            new_pos[x, :, at] = own[x : x + 1, at]


def call(kernel, outs, scratch, args, scalars=(), space=pltpu.VMEM, cost=None):
    specs = [pl.BlockSpec(memory_space=pltpu.SMEM if i in scalars else space) for i in range(len(args))]
    shapes = [s if isinstance(s, jax.ShapeDtypeStruct) else jax.ShapeDtypeStruct(s, f32) for s in outs]
    return pl.pallas_call(
        kernel,
        out_shape=shapes,
        in_specs=specs,
        out_specs=[pl.BlockSpec(memory_space=pltpu.VMEM)] * len(outs),
        scratch_shapes=[pltpu.VMEM(*s) if isinstance(s, tuple) else s for s in scratch],
        compiler_params=pltpu.CompilerParams(vmem_limit_bytes=VMEM_LIMIT),
        cost_estimate=cost,
    )(*args)


RING = ("bead", "space")


def ring(step):
    pairs = []
    for bead in range(BEADS):
        for domain in range(N_SPACE):
            to = domain + step
            other = bead if 0 <= to < N_SPACE else bead ^ 4
            pairs.append((bead * N_SPACE + domain, other * N_SPACE + to % N_SPACE))
    return pairs


def exchange(down, up):
    below = lax.ppermute(up, RING, ring(1))
    above = lax.ppermute(down, RING, ring(-1))
    return below, above


def body(
    positions, momenta, neighbours, ghost_rows, species, species_scale, mass_table, w_in, w_out
):
    first, later, last, reduce_, gains = (jnp.asarray(t) for t in tables())

    pos = positions.transpose(1, 0, 2)
    mom = momenta.transpose(1, 0, 2)
    kinds = species.reshape(1, ATOMS)
    ghosts = ghost_rows.reshape(2, 128)

    mine, ghosts, last, gains = call(
        first_kernel,
        [
            (8, ATOMS), jax.ShapeDtypeStruct((2, 128), jnp.int32), jax.ShapeDtypeStruct(last.shape[1:], bf16),
            gains.shape[1:],
        ],
        [
            ((3, 1, ATOMS), f32), ((3, 1, ATOMS), f32), ((1, ATOMS), jnp.int32),
            pltpu.SMEM((2,), f32), pltpu.SMEM((2,), f32), pltpu.SemaphoreType.DMA((8,)),
        ],
        tuple(
            pltpu.with_memory_space_constraint(v, pltpu.HBM)
            for v in (pos, mom, kinds, ghosts, species_scale, mass_table, last, gains)
        ),
        space=pltpu.HBM,
    )
    cost = pl.CostEstimate(flops=10**9, bytes_accessed=10**6, transcendentals=0)
    halves = [[x * 8 + z * 4 + y for z in range(2)] for x in range(4) for y in range(4)]
    pair = lax.all_gather(mine, "bead", axis=0, axis_index_groups=halves)
    down, up = call(send_kernel, [(8, 128)] * 2, [((8, ATOMS), f32)], (pair, ghosts), ())
    below, above = exchange(down, up)
    (early,) = call(
        early_pack_kernel, [(7, CHUNKS, SLOTS // 8, 8, 128)], [], (pair, neighbours), cost=cost
    )
    block, weights = call(
        pack_kernel,
        [(16, 64, 128), (SLOTS, ATOMS)],
        [((64, 128), f32)],
        (pair, early, below, above, neighbours),
    )
    groups = [[x * 8 + z * 4 + y for x in range(4) for y in range(4)] for z in range(2)]
    gathered = lax.all_to_all(block, "bead", 0, 0, axis_index_groups=groups, tiled=True)
    offsets = ((CB, CHUNKS, SLOTS // 8, 5, 8, 128), f32)
    network = ((CB, NRBF, ATOMS), f32)
    w_in = w_in.T
    coords, veloc, down, up = call(
        begin_kernel,
        [(96, ATOMS), (96, ATOMS), (96, 128), (96, 128)],
        [
            ((96, 768), f32), ((96, ATOMS), f32), ((3, 16, 768), f32), offsets, network, network,
            ((3, 16, ATOMS), f32),
        ],
        (gathered, neighbours, weights, mine, ghosts, w_in, w_out, first, reduce_),
    )
    big = [((3 * 72 + 8, 512), bf16), ((96, ATOMS), f32), ((24, 768), f32), ((24, 8, ATOMS), f32)]
    below, above = exchange(down, up)
    coords, veloc, down, up = call(
        middle_kernel,
        [(96, ATOMS), (96, ATOMS), (96, 128), (96, 128)],
        big,
        (coords, veloc, below, above, neighbours, weights, mine, ghosts, later),
    )
    below, above = exchange(down, up)
    own, contracted, down, up = call(
        last_kernel,
        [(8, ATOMS), (16, ATOMS), (16, 128), (16, 128)],
        [((2, 8, ATOMS), f32)] + big,
        (coords, veloc, below, above, neighbours, weights, mine, ghosts, last),
    )
    below, above = exchange(down, up)
    (early,) = call(
        early_end_kernel, [(15, CHUNKS, SLOTS // 8, 8, 128)], [], (own, contracted, neighbours), cost=cost
    )
    new_pos, new_mom = call(
        end_kernel,
        [(3, 1, ATOMS), (3, 1, ATOMS)],
        [offsets, network, network, ((CB, 3, CHUNKS, 128), f32)],
        (gains, own, contracted, early, below, above, neighbours, weights, w_in, w_out),
    )
    return new_pos.transpose(1, 0, 2), new_mom.transpose(1, 0, 2)


def solution(mesh):
    in_specs = (
        P("bead", None, "space"),
        P("bead", None, "space"),
        P(None, "space"),
        P("space"),
        P("space"),
        P(),
        P(),
        P(),
        P(),
    )
    out_specs = (P("bead", None, "space"), P("bead", None, "space"))
    return jax.shard_map(body, mesh=mesh, in_specs=in_specs, out_specs=out_specs, check_vma=False)
```

```python
import functools

import jax
import jax.numpy as jnp
import numpy as np
from jax import lax
from jax.experimental import pallas as pl
from jax.experimental.pallas import tpu as pltpu
from jax.sharding import PartitionSpec as P

BEADS = 32
CB = 4
NINNER = 3
NRBF = 8
H = 128
SLOTS = 32
ATOMS = 512
CHUNKS = 4
WINDOW = 6
N_SPACE = 16

polymer_freq = 10.0
outer_step = 6.0
inner_step = outer_step / NINNER
f32 = jnp.float32
bf16 = jnp.bfloat16
VMEM_LIMIT = 12 * 1024 * 1024


def mode_matrix(count):
    beadpos = np.arange(count)[None, :]
    modeidx = np.arange(count)[:, None]
    middle = count // 2
    cosine = np.sqrt(2.0 / count) * np.cos(2.0 * np.pi * beadpos * modeidx / count)
    sine_rows = np.sqrt(2.0 / count) * np.sin(2.0 * np.pi * beadpos * modeidx / count)
    matrix = np.where(modeidx < middle, cosine, sine_rows)
    matrix = np.where(modeidx == 0, 1.0 / np.sqrt(count), matrix)
    matrix = np.where(modeidx == middle, np.cos(np.pi * beadpos) / np.sqrt(count), matrix)
    return matrix


def polymer_tables(count):
    modes = mode_matrix(count)
    frequency = 2.0 * polymer_freq * np.sin(np.pi * np.arange(count) / count)
    nonzero = np.where(frequency > 0, frequency, 1.0)
    cosine = np.cos(frequency * inner_step)
    drift_gain = np.where(frequency > 0, np.sin(frequency * inner_step) / nonzero, inner_step)
    spring = frequency * np.sin(frequency * inner_step)
    persist = modes.T @ (cosine[:, None] * modes)
    coupling = modes.T @ (drift_gain[:, None] * modes)
    restoring = -(modes.T @ (spring[:, None] * modes))
    return persist, coupling, restoring


def contraction(count, fewer):
    full_modes = mode_matrix(count)
    small_modes = mode_matrix(fewer)
    kept = list(range(fewer // 2 + 1)) + list(range(count - fewer // 2 + 1, count))
    contract = np.sqrt(fewer / count) * (small_modes.T @ full_modes[kept])
    expand = count / fewer * contract.T
    return contract, expand


def bf16_terms(matrix):
    out, rest = [], matrix
    for _ in range(3):
        out.append(rest.astype(np.float32).astype(jnp.bfloat16))
        rest = rest - out[-1].astype(np.float64)
    return out


def three_terms(matrix):
    high, low, _ = bf16_terms(matrix)
    return np.concatenate([high, low, high], axis=1)


def six_terms(matrix):
    high, middle, low = bf16_terms(matrix)
    return np.concatenate([high, high, middle, middle, high, low], axis=1)


BEAD_OF_ROW = np.array([x * 8 + z * 4 + y for z in range(2) for x in range(4) for y in range(4)])


def tables():
    persist, coupling, restoring = polymer_tables(BEADS)
    contract, expand = contraction(BEADS, CB)
    order = BEAD_OF_ROW
    persist, coupling, restoring = (m[np.ix_(order, order)] for m in (persist, coupling, restoring))
    contract, expand = contract[:, order], expand[order]
    step = np.block([[persist, coupling], [restoring, persist]])
    padded_expand = np.concatenate([expand, np.zeros((BEADS, 16 - CB))], axis=1)
    kick = np.concatenate([coupling @ padded_expand, persist @ padded_expand], axis=0)
    first = six_terms(np.concatenate([step, 0.5 * outer_step * kick], axis=1))
    later = six_terms(step)
    padded_contract = np.concatenate([contract, np.zeros((16 - CB, BEADS))], axis=0)
    reduce_ = three_terms(padded_contract)
    contracted = contract @ step[:BEADS]
    last = np.zeros((BEADS, 3, 16, 6 * 2 * BEADS), jnp.bfloat16)
    gains = np.zeros((BEADS, 8, 128), np.float32)
    for row, bead in enumerate(order):
        gains[bead, :CB] = 0.5 * outer_step * expand[row][:, None]
        for place in range(3):
            below = row ^ 16 if place == 0 else row
            above = row ^ 16 if place == 2 else row
            last[bead, place, :8] = six_terms(np.concatenate([step[[row, BEADS + row, below, above]], contracted]))
    return first, later, last.reshape(3 * BEADS, 16, -1), reduce_, gains


def lanes(source, index):
    return jnp.take_along_axis(source, index, axis=1)


def row8(row):
    return jnp.broadcast_to(row, (8, 128))


def split_rows(value):
    high = value.astype(bf16)
    low = (value - high.astype(f32)).astype(bf16)
    return jnp.concatenate([high, high, low], axis=0)


def dot3(matrix, value):
    return jnp.dot(matrix, split_rows(value), preferred_element_type=f32)


def dot6(matrix, value):
    high = value.astype(bf16)
    rest = value - high.astype(f32)
    middle = rest.astype(bf16)
    low = (rest - middle.astype(f32)).astype(bf16)
    terms = jnp.concatenate([high, middle, high, middle, low, high], axis=0)
    return jnp.dot(matrix, terms, preferred_element_type=f32)


def by_species(species, table):
    return jnp.where(species == 0, table[0], table[1])


def ghosts_of(chunk, index):
    first = chunk(0)
    rows = first.shape[0]
    lane = jnp.broadcast_to(index & 127, (rows, 128))
    part = jnp.broadcast_to(index >> 7, (rows, 128))
    out = lanes(first, lane)
    for k in range(1, CHUNKS):
        out = jnp.where(part == k, lanes(chunk(k), lane), out)
    return out


def tile_index(neighbours, g, a):
    index = neighbours[8 * g : 8 * g + 8, 128 * a : 128 * a + 128]
    return index & 127, [(index >> 7) == k for k in range(1, WINDOW)], index


def looked_up(rows, lane, masks):
    out = lanes(rows[0], lane)
    for k in range(1, WINDOW):
        out = jnp.where(masks[k - 1], lanes(rows[k], lane), out)
    return out


def own_lookup(row, neighbours, g, a):
    index = neighbours[8 * g : 8 * g + 8, 128 * a : 128 * a + 128]
    lane, part = index & 127, index >> 7
    out = lanes(row8(row(0)), lane)
    for k in range(1, CHUNKS):
        out = jnp.where(part == k + 1, lanes(row8(row(k)), lane), out)
    return out


def with_ghosts(early, low, high, index):
    lane, part = index & 127, index >> 7
    out = jnp.where(part == 0, lanes(row8(low), lane), early)
    return jnp.where(part == WINDOW - 1, lanes(row8(high), lane), out)


def cheap_by_lanes(looked, centre, neighbours, weights, a):
    centre = [row8(row) for row in centre]
    total = [jnp.zeros((8, 128), f32) for _ in range(3)]
    for g in range(SLOTS // 8):
        index = neighbours[8 * g : 8 * g + 8, 128 * a : 128 * a + 128]
        offset = [looked(x, g, index) - centre[x] for x in range(3)]
        squared = offset[0] * offset[0] + offset[1] * offset[1] + offset[2] * offset[2]
        w = weights[8 * g : 8 * g + 8, 128 * a : 128 * a + 128] * jnp.exp2(-LOG2E * squared)
        for x in range(3):
            total[x] = total[x] + w * offset[x]
    return [jnp.sum(t, axis=0, keepdims=True) for t in total]


LOG2E = 1.4426950408889634


def roots(squared):
    return jnp.exp2((-0.2 * LOG2E) * squared), jnp.exp2((-0.2 * 2.0**0.5 * LOG2E) * squared)


def powers(even, odd):
    out = [even, odd]
    for _ in range(3):
        even, odd = even * even, odd * odd
        out += [even, odd]
    return out


def learned_by_lanes(looked, centre, neighbours, weights, w_in, w_out, offsets, messages, radials, store):
    high = w_in[...].astype(bf16).astype(f32)
    first = jnp.concatenate([high, w_in[...] - high, high, jnp.zeros_like(high)], axis=0).astype(bf16)
    high = w_out[...].astype(bf16).astype(f32)
    second = jnp.concatenate([high, w_out[...] - high, high], axis=1)
    second = jnp.concatenate([second, jnp.zeros_like(second)], axis=0).astype(bf16)

    def message(c):
        for a in range(CHUNKS):
            middle = [row8(centre(c, x, a)) for x in range(3)]
            total = [jnp.zeros((8, 128), f32) for _ in range(NRBF)]
            for g in range(SLOTS // 8):
                offset = [looked(c, x, a, g) - middle[x] for x in range(3)]
                squared = offset[0] * offset[0] + offset[1] * offset[1] + offset[2] * offset[2]
                even, odd = roots(squared)
                for x in range(3):
                    offsets[c, a, g, x] = offset[x]
                offsets[c, a, g, 3] = even
                offsets[c, a, g, 4] = odd
                w = weights[8 * g : 8 * g + 8, 128 * a : 128 * a + 128]
                for r, basis in enumerate(powers(even, odd)):
                    total[r] = total[r] + w * basis
            for r in range(NRBF):
                messages[c, r : r + 1, 128 * a : 128 * a + 128] = jnp.sum(total[r], axis=0, keepdims=True) * (
                    1.0 / SLOTS
                )

    def network(c):
        value = messages[c]
        high = value.astype(bf16).astype(f32)
        terms = jnp.concatenate([high, high, value - high, jnp.zeros_like(high)], axis=0).astype(bf16)
        hidden = lax.dot_general(first, terms, (((0,), (0,)), ((), ())), preferred_element_type=f32)
        half = 0.5 * hidden
        hidden = half + half * jnp.tanh(half)
        radials[c] = jnp.dot(second, split_rows(hidden), preferred_element_type=f32)[0:NRBF]

    def force(c):
        for a in range(CHUNKS):
            radial = [row8(radials[c, r : r + 1, 128 * a : 128 * a + 128]) for r in range(NRBF)]
            total = [jnp.zeros((8, 128), f32) for _ in range(3)]
            for g in range(SLOTS // 8):
                offset = [offsets[c, a, g, x] for x in range(3)]
                basis = powers(offsets[c, a, g, 3], offsets[c, a, g, 4])
                profile = radial[0] * basis[0]
                for r in range(1, NRBF):
                    profile = profile + radial[r] * basis[r]
                w = weights[8 * g : 8 * g + 8, 128 * a : 128 * a + 128] * profile
                for x in range(3):
                    total[x] = total[x] + w * offset[x]
            for x in range(3):
                store(c, x, a, jnp.sum(total[x], axis=0, keepdims=True))

    message(0)
    for c in range(CB):
        network(c)
        if c + 1 < CB:
            message(c + 1)
        force(c)


EARLY = 4


def cheap_of_all(coords, below, above, neighbours, weights, early, stacked, total, table, sums):
    few = BEADS - 8
    rows = 3 * few

    def of_few(value):
        return jnp.concatenate([value[BEADS * x : BEADS * x + few] for x in range(3)], axis=0)

    own, low, high_ = of_few(coords), of_few(below), of_few(above)
    stack = jnp.concatenate(
        [
            jnp.concatenate([low, own[:, 0:128]], axis=1),
            own[:, 128:384],
            jnp.concatenate([own[:, 384:512], high_], axis=1),
            jnp.zeros((8, 256), f32),
        ],
        axis=0,
    )
    high = stack.astype(bf16)
    stacked[:, 0:256] = high
    stacked[:, 256:512] = (stack - high.astype(f32)).astype(bf16)
    rounded = own.astype(bf16).astype(f32)
    rounded = rounded + (own - rounded).astype(bf16).astype(f32)
    for x in range(3):
        at = slice(BEADS * x + few, BEADS * (x + 1))
        table[8 * x : 8 * x + 8, 0:128] = below[at]
        table[8 * x : 8 * x + 8, 128:640] = coords[at]
        table[8 * x : 8 * x + 8, 640:768] = above[at]
    total[...] = jnp.zeros_like(total)
    sums[...] = jnp.zeros_like(sums)
    place = lax.broadcasted_iota(jnp.int16, (256, ATOMS), 0)

    def by_matmul(slot):
        index = neighbours[slot : slot + 1, :]
        column = jnp.broadcast_to(index & 255, (16, ATOMS)).astype(jnp.int16)
        chosen = jnp.where(place == jnp.tile(column, (16, 1)), bf16(1), bf16(0))
        picked = jnp.dot(stacked[...], jnp.concatenate([chosen, chosen], axis=0), preferred_element_type=f32)
        part = index >> 8
        other = jnp.where(
            part == 0,
            picked[0:rows],
            jnp.where(part == 1, picked[rows : 2 * rows], picked[2 * rows : 3 * rows]),
        )
        offset = other - rounded
        x, y, z = offset[0:few], offset[few : 2 * few], offset[2 * few :]
        w = weights[slot : slot + 1, :] * jnp.exp2(-LOG2E * (x * x + y * y + z * z))
        total[0:few] += w * x
        total[BEADS : BEADS + few] += w * y
        total[2 * BEADS : 2 * BEADS + few] += w * z

    def by_lanes(g, a):
        at = slice(128 * a, 128 * a + 128)
        slots = slice(8 * g, 8 * g + 8)
        index = neighbours[slots, at]
        lane, masks = index & 127, [(index >> 7) == k for k in range(1, WINDOW)]
        weight = weights[slots, at]
        for bead in range(8):
            rows_of = lambda x, k: row8(table[8 * x + bead : 8 * x + bead + 1, 128 * k : 128 * k + 128])
            offset = []
            for x in range(3):
                if bead < EARLY:
                    out = jnp.where(index >> 7 == 0, lanes(rows_of(x, 0), lane), early[EARLY * x + bead, a, g])
                    out = jnp.where(masks[-1], lanes(rows_of(x, WINDOW - 1), lane), out)
                else:
                    out = looked_up([rows_of(x, k) for k in range(WINDOW)], lane, masks)
                offset.append(out - rows_of(x, 1 + a))
            squared = offset[0] * offset[0] + offset[1] * offset[1] + offset[2] * offset[2]
            w = weight * jnp.exp2(-LOG2E * squared)
            for x in range(3):
                sums[8 * x + bead, :, at] += w * offset[x]

    for g in range(SLOTS // 8):
        for j in range(8):
            by_matmul(g * 8 + j)
            if j % 2:
                by_lanes(g, j // 2)
    for x in range(3):
        for bead in range(8):
            row = BEADS * x + few + bead
            total[row : row + 1] = jnp.sum(sums[8 * x + bead], axis=0, keepdims=True)


def propagated(coords, veloc, table, extra=None):
    wide = []
    for x in range(3):
        at = slice(x * BEADS, (x + 1) * BEADS)
        pieces = [coords[at], veloc[at]]
        if extra is not None:
            pieces.append(extra[x])
        wide.append(jnp.concatenate(pieces, axis=0))
    return dot6(table[...], jnp.concatenate(wide, axis=1))


def first_kernel(
    pos, mom, species, ghost_rows, scale, mass_table, all_last, all_gains,
    out, ghosts, last, gains,
    pos_in, mom_in, species_in, scale_in, mass_in, sems,
):
    bead, domain = lax.axis_index("bead"), lax.axis_index("space")
    place = jnp.where(domain == 0, 0, jnp.where(domain == N_SPACE - 1, 2, 1))
    copies = [
        pltpu.make_async_copy(source, target, sems.at[i])
        for i, (source, target) in enumerate(
            (
                (scale, scale_in), (mass_table, mass_in), (species, species_in), (mom, mom_in), (pos, pos_in),
                (ghost_rows, ghosts), (all_last.at[3 * bead + place], last), (all_gains.at[bead], gains),
            )
        )
    ]
    for copy in copies:
        copy.start()
    for copy in copies[:5]:
        copy.wait()
    mass = by_species(species_in[...], mass_in)
    for x in range(3):
        out[x : x + 1] = pos_in[x]
        out[3 + x : 4 + x] = mom_in[x] / mass
    out[6:7] = by_species(species_in[...], scale_in)
    out[7:8] = mass
    for copy in copies[5:]:
        copy.wait()


def send_kernel(pair, ghost_rows, down, up, rows):
    rows[0:3] = pair[0, 0:3]
    rows[3:6] = pair[1, 0:3]
    rows[6:8] = pair[0, 6:8]
    chunk = lambda k: rows[:, 128 * k : 128 * k + 128]
    down[...] = ghosts_of(chunk, ghost_rows[0:1])
    up[...] = ghosts_of(chunk, ghost_rows[1:2])


def early_pack_kernel(pair, neighbours, early):
    for a in range(CHUNKS):
        for g in range(SLOTS // 8):
            for k in range(2):
                for x in range(3):
                    early[3 * k + x, a, g] = own_lookup(
                        lambda i: pair[k, x : x + 1, 128 * i : 128 * i + 128], neighbours, g, a
                    )
            early[6, a, g] = own_lookup(lambda i: pair[0, 6:7, 128 * i : 128 * i + 128], neighbours, g, a)


def pack_kernel(pair, early, below, above, neighbours, out, weights, block):
    for k in range(2):
        base = 32 * k
        for x in range(3):
            at = base + 6 * x
            block[at : at + 1] = below[3 * k + x : 3 * k + x + 1]
            for i in range(CHUNKS):
                block[at + 1 + i : at + 2 + i] = pair[k, x : x + 1, 128 * i : 128 * i + 128]
            block[at + 5 : at + 6] = above[3 * k + x : 3 * k + x + 1]
        block[base + 30 : base + 32] = jnp.zeros((2, 128), f32)
    for a in range(CHUNKS):
        itself = 128 + 128 * a + lax.broadcasted_iota(jnp.int32, (8, 128), 1)
        for g in range(SLOTS // 8):
            index = neighbours[8 * g : 8 * g + 8, 128 * a : 128 * a + 128]
            q = with_ghosts(early[6, a, g], below[6:7], above[6:7], index)
            weights[8 * g : 8 * g + 8, 128 * a : 128 * a + 128] = jnp.where(index == itself, 0.0, q)
    for a in range(CHUNKS):
        at = slice(128 * a, 128 * a + 128)
        gain = pair[0, 6:7, at] / pair[0, 7:8, at] * (0.5 * inner_step)
        for k in range(2):
            base = 32 * k

            def looked(x, g, index):
                i = 3 * k + x
                return with_ghosts(early[i, a, g], below[i : i + 1], above[i : i + 1], index)

            force = cheap_by_lanes(looked, [pair[k, x : x + 1, at] for x in range(3)], neighbours, weights, a)
            for x in range(3):
                row = base + 18 + 4 * x + a
                block[row : row + 1] = pair[k, 3 + x : 4 + x, at] + gain * force[x]
    for i in range(16):
        out[i] = block[...]


def begin_kernel(
    gathered, neighbours, weights, mine, ghost_rows, w_in, w_out, first, reduce_,
    coords, veloc, down, up,
    window, start, contracted, offsets, messages, radials, slow,
):
    inverse = 1.0 / mine[7:8]
    for z in range(2):
        for x in range(3):
            at = slice(x * BEADS + 16 * z, x * BEADS + 16 * z + 16)
            for k in range(WINDOW):
                window[at, 128 * k : 128 * k + 128] = gathered[:, 32 * z + 6 * x + k, :]
            for k in range(CHUNKS):
                start[at, 128 * k : 128 * k + 128] = gathered[:, 32 * z + 18 + 4 * x + k, :]
    for x in range(3):
        contracted[x] = dot3(reduce_[...], window[x * BEADS : (x + 1) * BEADS, :])
    slow[...] = jnp.zeros_like(slow)

    def store(c, x, a, value):
        slow[x, c : c + 1, 128 * a : 128 * a + 128] = value

    def looked(c, x, a, g):
        rows = [row8(contracted[x, c : c + 1, 128 * k : 128 * k + 128]) for k in range(WINDOW)]
        lane, masks, _ = tile_index(neighbours, g, a)
        return looked_up(rows, lane, masks)

    learned_by_lanes(
        looked, lambda c, x, a: contracted[x, c : c + 1, 128 + 128 * a : 256 + 128 * a], neighbours, weights, w_in, w_out, offsets, messages, radials, store,
    )
    moved = propagated(
        window[:, 128:640], start[...], first, [slow[x] * inverse for x in range(3)]
    )
    finish_step(moved, coords, veloc, ghost_rows, down, up)


def finish_step(moved, coords, veloc, ghost_rows, down, up):
    for x in range(3):
        at = slice(x * BEADS, (x + 1) * BEADS)
        coords[at] = moved[0:BEADS, ATOMS * x : ATOMS * (x + 1)]
        veloc[at] = moved[BEADS : 2 * BEADS, ATOMS * x : ATOMS * (x + 1)]
    for i in range(3 * BEADS // 8):
        chunk = lambda k: coords[8 * i : 8 * i + 8, 128 * k : 128 * k + 128]
        down[8 * i : 8 * i + 8] = ghosts_of(chunk, ghost_rows[0:1])
        up[8 * i : 8 * i + 8] = ghosts_of(chunk, ghost_rows[1:2])


def early_middle_kernel(coords, neighbours, early):
    for a in range(CHUNKS):
        for g in range(SLOTS // 8):
            for x in range(3):
                for i in range(EARLY):
                    row = BEADS * x + BEADS - 8 + i
                    early[EARLY * x + i, a, g] = own_lookup(
                        lambda k: coords[row : row + 1, 128 * k : 128 * k + 128], neighbours, g, a
                    )


def kicked(coords, veloc, below, above, neighbours, weights, early, mine, scratch):
    total = scratch[1]
    cheap_of_all(coords, below, above, neighbours, weights, early, *scratch)
    return veloc[...] + inner_step * mine[6:7] / mine[7:8] * total[...]


def middle_kernel(
    coords, veloc, below, above, neighbours, weights, early, mine, ghost_rows, later,
    new_coords, new_veloc, down, up, *scratch,
):
    velocities = kicked(coords, veloc, below, above, neighbours, weights, early, mine, scratch)
    moved = propagated(coords[...], velocities, later)
    finish_step(moved, new_coords, new_veloc, ghost_rows, down, up)


def last_kernel(
    coords, veloc, below, above, neighbours, weights, early, mine, ghost_rows, last,
    own, contracted, down, up, rows, *scratch,
):
    velocities = kicked(coords, veloc, below, above, neighbours, weights, early, mine, scratch)
    moved = propagated(coords[...], velocities, last)
    for x in range(3):
        part = moved[:, ATOMS * x : ATOMS * (x + 1)]
        own[x : x + 1] = part[0:1]
        own[3 + x : 4 + x] = part[1:2]
        contracted[4 * x : 4 * x + 4] = part[4:8]
        rows[0, 4 + x : 5 + x] = part[2:3]
        rows[1, 4 + x : 5 + x] = part[3:4]
    own[6:8] = mine[6:8]
    contracted[12:16] = jnp.zeros((4, ATOMS), f32)
    for which, out in ((0, down), (1, up)):
        rows[which, 0:4] = contracted[8:12]
        rows[which, 7:8] = mine[6:7]
        index = ghost_rows[which : which + 1]
        out[0:8] = ghosts_of(lambda k: contracted[0:8, 128 * k : 128 * k + 128], index)
        out[8:16] = ghosts_of(lambda k: rows[which, :, 128 * k : 128 * k + 128], index)


def early_end_kernel(contracted, neighbours, early):
    for a in range(CHUNKS):
        for g in range(SLOTS // 8):
            for i in range(12):
                early[i, a, g] = own_lookup(
                    lambda k: contracted[i : i + 1, 128 * k : 128 * k + 128], neighbours, g, a
                )


def end_kernel(
    gains, own, contracted, early, below, above, neighbours, weights, w_in, w_out,
    new_pos, new_mom,
    offsets, messages, radials, slow,
):
    charge, mass = own[6:7], own[7:8]

    def store(c, x, a, value):
        slow[c, x, a : a + 1] = value

    def looked_at(i, a, g):
        index = neighbours[8 * g : 8 * g + 8, 128 * a : 128 * a + 128]
        if i < 12:
            out = early[i, a, g]
        else:
            out = own_lookup(lambda k: own[i - 12 : i - 11, 128 * k : 128 * k + 128], neighbours, g, a)
        return with_ghosts(out, below[i : i + 1], above[i : i + 1], index)

    learned_by_lanes(
        lambda c, x, a, g: looked_at(4 * x + c, a, g),
        lambda c, x, a: contracted[4 * x + c : 4 * x + c + 1, 128 * a : 128 * a + 128],
        neighbours, weights, w_in, w_out, offsets, messages, radials, store,
    )
    for a in range(CHUNKS):
        at = slice(128 * a, 128 * a + 128)
        force = cheap_by_lanes(
            lambda x, g, index: looked_at(12 + x, a, g), [own[x : x + 1, at] for x in range(3)], neighbours, weights, a
        )
        for x in range(3):
            value = mass[:, at] * own[3 + x : 4 + x, at] + (0.5 * inner_step) * charge[:, at] * force[x]
            for c in range(CB):
                value = value + gains[c : c + 1] * slow[c, x, a : a + 1]
            new_mom[x, :, at] = value
            new_pos[x, :, at] = own[x : x + 1, at]


def call(kernel, outs, scratch, args, scalars=(), space=pltpu.VMEM, cost=None):
    specs = [pl.BlockSpec(memory_space=pltpu.SMEM if i in scalars else space) for i in range(len(args))]
    shapes = [s if isinstance(s, jax.ShapeDtypeStruct) else jax.ShapeDtypeStruct(s, f32) for s in outs]
    return pl.pallas_call(
        kernel,
        out_shape=shapes,
        in_specs=specs,
        out_specs=[pl.BlockSpec(memory_space=pltpu.VMEM)] * len(outs),
        scratch_shapes=[pltpu.VMEM(*s) if isinstance(s, tuple) else s for s in scratch],
        compiler_params=pltpu.CompilerParams(vmem_limit_bytes=VMEM_LIMIT),
        cost_estimate=cost,
    )(*args)


RING = ("bead", "space")


def ring(step):
    pairs = []
    for bead in range(BEADS):
        for domain in range(N_SPACE):
            to = domain + step
            other = bead if 0 <= to < N_SPACE else bead ^ 4
            pairs.append((bead * N_SPACE + domain, other * N_SPACE + to % N_SPACE))
    return pairs


def exchange(down, up):
    below = lax.ppermute(up, RING, ring(1))
    above = lax.ppermute(down, RING, ring(-1))
    return below, above


def body(
    positions, momenta, neighbours, ghost_rows, species, species_scale, mass_table, w_in, w_out
):
    first, later, last, reduce_, gains = (jnp.asarray(t) for t in tables())

    pos = positions.transpose(1, 0, 2)
    mom = momenta.transpose(1, 0, 2)
    kinds = species.reshape(1, ATOMS)
    ghosts = ghost_rows.reshape(2, 128)

    mine, ghosts, last, gains = call(
        first_kernel,
        [
            (8, ATOMS), jax.ShapeDtypeStruct((2, 128), jnp.int32), jax.ShapeDtypeStruct(last.shape[1:], bf16),
            gains.shape[1:],
        ],
        [
            ((3, 1, ATOMS), f32), ((3, 1, ATOMS), f32), ((1, ATOMS), jnp.int32),
            pltpu.SMEM((2,), f32), pltpu.SMEM((2,), f32), pltpu.SemaphoreType.DMA((8,)),
        ],
        tuple(
            pltpu.with_memory_space_constraint(v, pltpu.HBM)
            for v in (pos, mom, kinds, ghosts, species_scale, mass_table, last, gains)
        ),
        space=pltpu.HBM,
    )
    cost = pl.CostEstimate(flops=10**9, bytes_accessed=10**6, transcendentals=0)
    halves = [[x * 8 + z * 4 + y for z in range(2)] for x in range(4) for y in range(4)]
    pair = lax.all_gather(mine, "bead", axis=0, axis_index_groups=halves)
    down, up = call(send_kernel, [(8, 128)] * 2, [((8, ATOMS), f32)], (pair, ghosts), ())
    below, above = exchange(down, up)
    (early,) = call(
        early_pack_kernel, [(7, CHUNKS, SLOTS // 8, 8, 128)], [], (pair, neighbours), cost=cost
    )
    block, weights = call(
        pack_kernel,
        [(16, 64, 128), (SLOTS, ATOMS)],
        [((64, 128), f32)],
        (pair, early, below, above, neighbours),
    )
    groups = [[x * 8 + z * 4 + y for x in range(4) for y in range(4)] for z in range(2)]
    gathered = lax.all_to_all(block, "bead", 0, 0, axis_index_groups=groups, tiled=True)
    offsets = ((CB, CHUNKS, SLOTS // 8, 5, 8, 128), f32)
    network = ((CB, NRBF, ATOMS), f32)
    w_in = w_in.T
    coords, veloc, down, up = call(
        begin_kernel,
        [(96, ATOMS), (96, ATOMS), (96, 128), (96, 128)],
        [
            ((96, 768), f32), ((96, ATOMS), f32), ((3, 16, 768), f32), offsets, network, network,
            ((3, 16, ATOMS), f32),
        ],
        (gathered, neighbours, weights, mine, ghosts, w_in, w_out, first, reduce_),
    )
    early = lambda coords: call(
        early_middle_kernel, [(3 * EARLY, CHUNKS, SLOTS // 8, 8, 128)], [], (coords, neighbours), cost=cost
    )[0]
    big = [((3 * 72 + 8, 512), bf16), ((96, ATOMS), f32), ((24, 768), f32), ((24, 8, ATOMS), f32)]
    below, above = exchange(down, up)
    coords, veloc, down, up = call(
        middle_kernel,
        [(96, ATOMS), (96, ATOMS), (96, 128), (96, 128)],
        big,
        (coords, veloc, below, above, neighbours, weights, early(coords), mine, ghosts, later),
    )
    below, above = exchange(down, up)
    own, contracted, down, up = call(
        last_kernel,
        [(8, ATOMS), (16, ATOMS), (16, 128), (16, 128)],
        [((2, 8, ATOMS), f32)] + big,
        (coords, veloc, below, above, neighbours, weights, early(coords), mine, ghosts, last),
    )
    below, above = exchange(down, up)
    (early,) = call(
        early_end_kernel, [(12, CHUNKS, SLOTS // 8, 8, 128)], [], (contracted, neighbours), cost=cost
    )
    new_pos, new_mom = call(
        end_kernel,
        [(3, 1, ATOMS), (3, 1, ATOMS)],
        [offsets, network, network, ((CB, 3, CHUNKS, 128), f32)],
        (gains, own, contracted, early, below, above, neighbours, weights, w_in, w_out),
    )
    return new_pos.transpose(1, 0, 2), new_mom.transpose(1, 0, 2)


def solution(mesh):
    in_specs = (
        P("bead", None, "space"),
        P("bead", None, "space"),
        P(None, "space"),
        P("space"),
        P("space"),
        P(),
        P(),
        P(),
        P(),
    )
    out_specs = (P("bead", None, "space"), P("bead", None, "space"))
    return jax.shard_map(body, mesh=mesh, in_specs=in_specs, out_specs=out_specs, check_vma=False)
```

```python
import functools

import jax
import jax.numpy as jnp
import numpy as np
from jax import lax
from jax.experimental import pallas as pl
from jax.experimental.pallas import tpu as pltpu
from jax.sharding import PartitionSpec as P

BEADS = 32
CB = 4
NINNER = 3
NRBF = 8
H = 128
SLOTS = 32
ATOMS = 512
CHUNKS = 4
WINDOW = 6
N_SPACE = 16

polymer_freq = 10.0
outer_step = 6.0
inner_step = outer_step / NINNER
f32 = jnp.float32
bf16 = jnp.bfloat16
VMEM_LIMIT = 12 * 1024 * 1024


def mode_matrix(count):
    beadpos = np.arange(count)[None, :]
    modeidx = np.arange(count)[:, None]
    middle = count // 2
    cosine = np.sqrt(2.0 / count) * np.cos(2.0 * np.pi * beadpos * modeidx / count)
    sine_rows = np.sqrt(2.0 / count) * np.sin(2.0 * np.pi * beadpos * modeidx / count)
    matrix = np.where(modeidx < middle, cosine, sine_rows)
    matrix = np.where(modeidx == 0, 1.0 / np.sqrt(count), matrix)
    matrix = np.where(modeidx == middle, np.cos(np.pi * beadpos) / np.sqrt(count), matrix)
    return matrix


def polymer_tables(count):
    modes = mode_matrix(count)
    frequency = 2.0 * polymer_freq * np.sin(np.pi * np.arange(count) / count)
    nonzero = np.where(frequency > 0, frequency, 1.0)
    cosine = np.cos(frequency * inner_step)
    drift_gain = np.where(frequency > 0, np.sin(frequency * inner_step) / nonzero, inner_step)
    spring = frequency * np.sin(frequency * inner_step)
    persist = modes.T @ (cosine[:, None] * modes)
    coupling = modes.T @ (drift_gain[:, None] * modes)
    restoring = -(modes.T @ (spring[:, None] * modes))
    return persist, coupling, restoring


def contraction(count, fewer):
    full_modes = mode_matrix(count)
    small_modes = mode_matrix(fewer)
    kept = list(range(fewer // 2 + 1)) + list(range(count - fewer // 2 + 1, count))
    contract = np.sqrt(fewer / count) * (small_modes.T @ full_modes[kept])
    expand = count / fewer * contract.T
    return contract, expand


def bf16_terms(matrix):
    out, rest = [], matrix
    for _ in range(3):
        out.append(rest.astype(np.float32).astype(jnp.bfloat16))
        rest = rest - out[-1].astype(np.float64)
    return out


def three_terms(matrix):
    high, low, _ = bf16_terms(matrix)
    return np.concatenate([high, low, high], axis=1)


def six_terms(matrix):
    high, middle, low = bf16_terms(matrix)
    return np.concatenate([high, high, middle, middle, high, low], axis=1)


BEAD_OF_ROW = np.array([x * 8 + z * 4 + y for z in range(2) for x in range(4) for y in range(4)])


def tables():
    persist, coupling, restoring = polymer_tables(BEADS)
    contract, expand = contraction(BEADS, CB)
    order = BEAD_OF_ROW
    persist, coupling, restoring = (m[np.ix_(order, order)] for m in (persist, coupling, restoring))
    contract, expand = contract[:, order], expand[order]
    step = np.block([[persist, coupling], [restoring, persist]])
    padded_expand = np.concatenate([expand, np.zeros((BEADS, 16 - CB))], axis=1)
    kick = np.concatenate([coupling @ padded_expand, persist @ padded_expand], axis=0)
    first = six_terms(np.concatenate([step, 0.5 * outer_step * kick], axis=1))
    later = six_terms(step)
    padded_contract = np.concatenate([contract, np.zeros((16 - CB, BEADS))], axis=0)
    reduce_ = three_terms(padded_contract)
    contracted = contract @ step[:BEADS]
    last = np.zeros((BEADS, 3, 16, 6 * 2 * BEADS), jnp.bfloat16)
    gains = np.zeros((BEADS, 8, 128), np.float32)
    for row, bead in enumerate(order):
        gains[bead, :CB] = 0.5 * outer_step * expand[row][:, None]
        for place in range(3):
            below = row ^ 16 if place == 0 else row
            above = row ^ 16 if place == 2 else row
            last[bead, place, :8] = six_terms(np.concatenate([step[[row, BEADS + row, below, above]], contracted]))
    return first, later, last.reshape(3 * BEADS, 16, -1), reduce_, gains


def lanes(source, index):
    return jnp.take_along_axis(source, index, axis=1)


def row8(row):
    return jnp.broadcast_to(row, (8, 128))


def split_rows(value):
    high = value.astype(bf16)
    low = (value - high.astype(f32)).astype(bf16)
    return jnp.concatenate([high, high, low], axis=0)


def dot3(matrix, value):
    return jnp.dot(matrix, split_rows(value), preferred_element_type=f32)


def dot6(matrix, value):
    high = value.astype(bf16)
    rest = value - high.astype(f32)
    middle = rest.astype(bf16)
    low = (rest - middle.astype(f32)).astype(bf16)
    terms = jnp.concatenate([high, middle, high, middle, low, high], axis=0)
    return jnp.dot(matrix, terms, preferred_element_type=f32)


def by_species(species, table):
    return jnp.where(species == 0, table[0], table[1])


def ghosts_of(chunk, index):
    first = chunk(0)
    rows = first.shape[0]
    lane = jnp.broadcast_to(index & 127, (rows, 128))
    part = jnp.broadcast_to(index >> 7, (rows, 128))
    out = lanes(first, lane)
    for k in range(1, CHUNKS):
        out = jnp.where(part == k, lanes(chunk(k), lane), out)
    return out


def tile_index(neighbours, g, a):
    index = neighbours[8 * g : 8 * g + 8, 128 * a : 128 * a + 128]
    return index & 127, [(index >> 7) == k for k in range(1, WINDOW)], index


def looked_up(rows, lane, masks):
    out = lanes(rows[0], lane)
    for k in range(1, WINDOW):
        out = jnp.where(masks[k - 1], lanes(rows[k], lane), out)
    return out


def own_lookup(row, neighbours, g, a):
    index = neighbours[8 * g : 8 * g + 8, 128 * a : 128 * a + 128]
    lane, part = index & 127, index >> 7
    out = lanes(row8(row(0)), lane)
    for k in range(1, CHUNKS):
        out = jnp.where(part == k + 1, lanes(row8(row(k)), lane), out)
    return out


def with_ghosts(early, low, high, index):
    lane, part = index & 127, index >> 7
    out = jnp.where(part == 0, lanes(row8(low), lane), early)
    return jnp.where(part == WINDOW - 1, lanes(row8(high), lane), out)


def cheap_by_lanes(looked, centre, neighbours, weights, a):
    centre = [row8(row) for row in centre]
    total = [jnp.zeros((8, 128), f32) for _ in range(3)]
    for g in range(SLOTS // 8):
        index = neighbours[8 * g : 8 * g + 8, 128 * a : 128 * a + 128]
        offset = [looked(x, g, index) - centre[x] for x in range(3)]
        squared = offset[0] * offset[0] + offset[1] * offset[1] + offset[2] * offset[2]
        w = weights[8 * g : 8 * g + 8, 128 * a : 128 * a + 128] * jnp.exp2(-LOG2E * squared)
        for x in range(3):
            total[x] = total[x] + w * offset[x]
    return [jnp.sum(t, axis=0, keepdims=True) for t in total]


LOG2E = 1.4426950408889634


def roots(squared):
    return jnp.exp2((-0.2 * LOG2E) * squared), jnp.exp2((-0.2 * 2.0**0.5 * LOG2E) * squared)


def powers(even, odd):
    out = [even, odd]
    for _ in range(3):
        even, odd = even * even, odd * odd
        out += [even, odd]
    return out


def learned_by_lanes(looked, centre, neighbours, weights, w_in, w_out, offsets, messages, radials, store):
    high = w_in[...].astype(bf16).astype(f32)
    first = jnp.concatenate([high, w_in[...] - high, high, jnp.zeros_like(high)], axis=0).astype(bf16)
    high = w_out[...].astype(bf16).astype(f32)
    second = jnp.concatenate([high, w_out[...] - high, high], axis=1)
    second = jnp.concatenate([second, jnp.zeros_like(second)], axis=0).astype(bf16)

    def message(c):
        for a in range(CHUNKS):
            middle = [row8(centre(c, x, a)) for x in range(3)]
            total = [jnp.zeros((8, 128), f32) for _ in range(NRBF)]
            for g in range(SLOTS // 8):
                offset = [looked(c, x, a, g) - middle[x] for x in range(3)]
                squared = offset[0] * offset[0] + offset[1] * offset[1] + offset[2] * offset[2]
                even, odd = roots(squared)
                for x in range(3):
                    offsets[c, a, g, x] = offset[x]
                offsets[c, a, g, 3] = even
                offsets[c, a, g, 4] = odd
                w = weights[8 * g : 8 * g + 8, 128 * a : 128 * a + 128]
                for r, basis in enumerate(powers(even, odd)):
                    total[r] = total[r] + w * basis
            for r in range(NRBF):
                messages[c, r : r + 1, 128 * a : 128 * a + 128] = jnp.sum(total[r], axis=0, keepdims=True) * (
                    1.0 / SLOTS
                )

    def network(c):
        value = messages[c]
        high = value.astype(bf16).astype(f32)
        terms = jnp.concatenate([high, high, value - high, jnp.zeros_like(high)], axis=0).astype(bf16)
        hidden = lax.dot_general(first, terms, (((0,), (0,)), ((), ())), preferred_element_type=f32)
        half = 0.5 * hidden
        hidden = half + half * jnp.tanh(half)
        radials[c] = jnp.dot(second, split_rows(hidden), preferred_element_type=f32)[0:NRBF]

    def force(c):
        for a in range(CHUNKS):
            radial = [row8(radials[c, r : r + 1, 128 * a : 128 * a + 128]) for r in range(NRBF)]
            total = [jnp.zeros((8, 128), f32) for _ in range(3)]
            for g in range(SLOTS // 8):
                offset = [offsets[c, a, g, x] for x in range(3)]
                basis = powers(offsets[c, a, g, 3], offsets[c, a, g, 4])
                profile = radial[0] * basis[0]
                for r in range(1, NRBF):
                    profile = profile + radial[r] * basis[r]
                w = weights[8 * g : 8 * g + 8, 128 * a : 128 * a + 128] * profile
                for x in range(3):
                    total[x] = total[x] + w * offset[x]
            for x in range(3):
                store(c, x, a, jnp.sum(total[x], axis=0, keepdims=True))

    message(0)
    for c in range(CB):
        network(c)
        if c + 1 < CB:
            message(c + 1)
        force(c)


EARLY = 4


def cheap_of_all(coords, below, above, neighbours, weights, early, stacked, total, table, sums, stacked_less):
    few = BEADS - 8
    fewer = BEADS - 16

    def prepared(count, target):
        def of_few(value):
            return jnp.concatenate([value[BEADS * x : BEADS * x + count] for x in range(3)], axis=0)

        own, low, high_ = of_few(coords), of_few(below), of_few(above)
        parts = [
            jnp.concatenate([low, own[:, 0:128]], axis=1),
            own[:, 128:384],
            jnp.concatenate([own[:, 384:512], high_], axis=1),
        ]
        spare = target.shape[0] - 9 * count
        if spare:
            parts.append(jnp.zeros((spare, 256), f32))
        stack = jnp.concatenate(parts, axis=0)
        high = stack.astype(bf16)
        target[:, 0:256] = high
        target[:, 256:512] = (stack - high.astype(f32)).astype(bf16)
        rounded = own.astype(bf16).astype(f32)
        return rounded + (own - rounded).astype(bf16).astype(f32)

    rounded_few, rounded_fewer = prepared(few, stacked), prepared(fewer, stacked_less)
    for x in range(3):
        at = slice(BEADS * x + fewer, BEADS * (x + 1))
        table[16 * x : 16 * x + 16, 0:128] = below[at]
        table[16 * x : 16 * x + 16, 128:640] = coords[at]
        table[16 * x : 16 * x + 16, 640:768] = above[at]
    total[...] = jnp.zeros_like(total)
    sums[...] = jnp.zeros_like(sums)
    place = lax.broadcasted_iota(jnp.int16, (256, ATOMS), 0)

    def by_matmul(slot, count, matrix, rounded):
        rows = 3 * count
        index = neighbours[slot : slot + 1, :]
        column = jnp.broadcast_to(index & 255, (16, ATOMS)).astype(jnp.int16)
        chosen = jnp.where(place == jnp.tile(column, (16, 1)), bf16(1), bf16(0))
        picked = jnp.dot(matrix[...], jnp.concatenate([chosen, chosen], axis=0), preferred_element_type=f32)
        part = index >> 8
        other = jnp.where(
            part == 0,
            picked[0:rows],
            jnp.where(part == 1, picked[rows : 2 * rows], picked[2 * rows : 3 * rows]),
        )
        offset = other - rounded
        x, y, z = offset[0:count], offset[count : 2 * count], offset[2 * count :]
        w = weights[slot : slot + 1, :] * jnp.exp2(-LOG2E * (x * x + y * y + z * z))
        total[0:count] += w * x
        total[BEADS : BEADS + count] += w * y
        total[2 * BEADS : 2 * BEADS + count] += w * z

    def by_lanes(g, a, beads):
        at = slice(128 * a, 128 * a + 128)
        slots = slice(8 * g, 8 * g + 8)
        index = neighbours[slots, at]
        lane, masks = index & 127, [(index >> 7) == k for k in range(1, WINDOW)]
        weight = weights[slots, at]
        for bead in beads:
            rows_of = lambda x, k: row8(table[16 * x + bead : 16 * x + bead + 1, 128 * k : 128 * k + 128])
            offset = []
            for x in range(3):
                if 8 <= bead < 8 + EARLY:
                    out = jnp.where(index >> 7 == 0, lanes(rows_of(x, 0), lane), early[EARLY * x + bead - 8, a, g])
                    out = jnp.where(masks[-1], lanes(rows_of(x, WINDOW - 1), lane), out)
                else:
                    out = looked_up([rows_of(x, k) for k in range(WINDOW)], lane, masks)
                offset.append(out - rows_of(x, 1 + a))
            squared = offset[0] * offset[0] + offset[1] * offset[1] + offset[2] * offset[2]
            w = weight * jnp.exp2(-LOG2E * squared)
            for x in range(3):
                sums[16 * x + bead, :, at] += w * offset[x]

    for g in range(SLOTS // 8):
        less = g == SLOTS // 8 - 1
        for j in range(8):
            if less:
                by_matmul(g * 8 + j, fewer, stacked_less, rounded_fewer)
            else:
                by_matmul(g * 8 + j, few, stacked, rounded_few)
            if j % 2:
                by_lanes(g, j // 2, range(0 if less else 8, 16))
    for x in range(3):
        for bead in range(16):
            row = BEADS * x + fewer + bead
            total[row : row + 1] += jnp.sum(sums[16 * x + bead], axis=0, keepdims=True)


def propagated(coords, veloc, table, extra=None):
    wide = []
    for x in range(3):
        at = slice(x * BEADS, (x + 1) * BEADS)
        pieces = [coords[at], veloc[at]]
        if extra is not None:
            pieces.append(extra[x])
        wide.append(jnp.concatenate(pieces, axis=0))
    return dot6(table[...], jnp.concatenate(wide, axis=1))


def first_kernel(
    pos, mom, species, ghost_rows, scale, mass_table, all_last, all_gains,
    out, ghosts, last, gains,
    pos_in, mom_in, species_in, scale_in, mass_in, sems,
):
    bead, domain = lax.axis_index("bead"), lax.axis_index("space")
    place = jnp.where(domain == 0, 0, jnp.where(domain == N_SPACE - 1, 2, 1))
    copies = [
        pltpu.make_async_copy(source, target, sems.at[i])
        for i, (source, target) in enumerate(
            (
                (scale, scale_in), (mass_table, mass_in), (species, species_in), (mom, mom_in), (pos, pos_in),
                (ghost_rows, ghosts), (all_last.at[3 * bead + place], last), (all_gains.at[bead], gains),
            )
        )
    ]
    for copy in copies:
        copy.start()
    for copy in copies[:5]:
        copy.wait()
    mass = by_species(species_in[...], mass_in)
    for x in range(3):
        out[x : x + 1] = pos_in[x]
        out[3 + x : 4 + x] = mom_in[x] / mass
    out[6:7] = by_species(species_in[...], scale_in)
    out[7:8] = mass
    for copy in copies[5:]:
        copy.wait()


def send_kernel(pair, ghost_rows, down, up, rows):
    rows[0:3] = pair[0, 0:3]
    rows[3:6] = pair[1, 0:3]
    rows[6:8] = pair[0, 6:8]
    chunk = lambda k: rows[:, 128 * k : 128 * k + 128]
    down[...] = ghosts_of(chunk, ghost_rows[0:1])
    up[...] = ghosts_of(chunk, ghost_rows[1:2])


def early_pack_kernel(pair, neighbours, early):
    for a in range(CHUNKS):
        for g in range(SLOTS // 8):
            for k in range(2):
                for x in range(3):
                    early[3 * k + x, a, g] = own_lookup(
                        lambda i: pair[k, x : x + 1, 128 * i : 128 * i + 128], neighbours, g, a
                    )
            early[6, a, g] = own_lookup(lambda i: pair[0, 6:7, 128 * i : 128 * i + 128], neighbours, g, a)


def pack_kernel(pair, early, below, above, neighbours, out, weights, block):
    for k in range(2):
        base = 32 * k
        for x in range(3):
            at = base + 6 * x
            block[at : at + 1] = below[3 * k + x : 3 * k + x + 1]
            for i in range(CHUNKS):
                block[at + 1 + i : at + 2 + i] = pair[k, x : x + 1, 128 * i : 128 * i + 128]
            block[at + 5 : at + 6] = above[3 * k + x : 3 * k + x + 1]
        block[base + 30 : base + 32] = jnp.zeros((2, 128), f32)
    for a in range(CHUNKS):
        itself = 128 + 128 * a + lax.broadcasted_iota(jnp.int32, (8, 128), 1)
        for g in range(SLOTS // 8):
            index = neighbours[8 * g : 8 * g + 8, 128 * a : 128 * a + 128]
            q = with_ghosts(early[6, a, g], below[6:7], above[6:7], index)
            weights[8 * g : 8 * g + 8, 128 * a : 128 * a + 128] = jnp.where(index == itself, 0.0, q)
    for a in range(CHUNKS):
        at = slice(128 * a, 128 * a + 128)
        gain = pair[0, 6:7, at] / pair[0, 7:8, at] * (0.5 * inner_step)
        for k in range(2):
            base = 32 * k

            def looked(x, g, index):
                i = 3 * k + x
                return with_ghosts(early[i, a, g], below[i : i + 1], above[i : i + 1], index)

            force = cheap_by_lanes(looked, [pair[k, x : x + 1, at] for x in range(3)], neighbours, weights, a)
            for x in range(3):
                row = base + 18 + 4 * x + a
                block[row : row + 1] = pair[k, 3 + x : 4 + x, at] + gain * force[x]
    for i in range(16):
        out[i] = block[...]


def begin_kernel(
    gathered, neighbours, weights, mine, ghost_rows, w_in, w_out, first, reduce_,
    coords, veloc, down, up,
    window, start, contracted, offsets, messages, radials, slow,
):
    inverse = 1.0 / mine[7:8]
    for z in range(2):
        for x in range(3):
            at = slice(x * BEADS + 16 * z, x * BEADS + 16 * z + 16)
            for k in range(WINDOW):
                window[at, 128 * k : 128 * k + 128] = gathered[:, 32 * z + 6 * x + k, :]
            for k in range(CHUNKS):
                start[at, 128 * k : 128 * k + 128] = gathered[:, 32 * z + 18 + 4 * x + k, :]
    for x in range(3):
        contracted[x] = dot3(reduce_[...], window[x * BEADS : (x + 1) * BEADS, :])
    slow[...] = jnp.zeros_like(slow)

    def store(c, x, a, value):
        slow[x, c : c + 1, 128 * a : 128 * a + 128] = value

    def looked(c, x, a, g):
        rows = [row8(contracted[x, c : c + 1, 128 * k : 128 * k + 128]) for k in range(WINDOW)]
        lane, masks, _ = tile_index(neighbours, g, a)
        return looked_up(rows, lane, masks)

    learned_by_lanes(
        looked, lambda c, x, a: contracted[x, c : c + 1, 128 + 128 * a : 256 + 128 * a], neighbours, weights, w_in, w_out, offsets, messages, radials, store,
    )
    moved = propagated(
        window[:, 128:640], start[...], first, [slow[x] * inverse for x in range(3)]
    )
    finish_step(moved, coords, veloc, ghost_rows, down, up)


def finish_step(moved, coords, veloc, ghost_rows, down, up):
    for x in range(3):
        at = slice(x * BEADS, (x + 1) * BEADS)
        coords[at] = moved[0:BEADS, ATOMS * x : ATOMS * (x + 1)]
        veloc[at] = moved[BEADS : 2 * BEADS, ATOMS * x : ATOMS * (x + 1)]
    for i in range(3 * BEADS // 8):
        chunk = lambda k: coords[8 * i : 8 * i + 8, 128 * k : 128 * k + 128]
        down[8 * i : 8 * i + 8] = ghosts_of(chunk, ghost_rows[0:1])
        up[8 * i : 8 * i + 8] = ghosts_of(chunk, ghost_rows[1:2])


def early_middle_kernel(coords, neighbours, early):
    for a in range(CHUNKS):
        for g in range(SLOTS // 8):
            for x in range(3):
                for i in range(EARLY):
                    row = BEADS * x + BEADS - 8 + i
                    early[EARLY * x + i, a, g] = own_lookup(
                        lambda k: coords[row : row + 1, 128 * k : 128 * k + 128], neighbours, g, a
                    )


def kicked(coords, veloc, below, above, neighbours, weights, early, mine, scratch):
    total = scratch[1]
    cheap_of_all(coords, below, above, neighbours, weights, early, *scratch)
    return veloc[...] + inner_step * mine[6:7] / mine[7:8] * total[...]


def middle_kernel(
    coords, veloc, below, above, neighbours, weights, early, mine, ghost_rows, later,
    new_coords, new_veloc, down, up, *scratch,
):
    velocities = kicked(coords, veloc, below, above, neighbours, weights, early, mine, scratch)
    moved = propagated(coords[...], velocities, later)
    finish_step(moved, new_coords, new_veloc, ghost_rows, down, up)


def last_kernel(
    coords, veloc, below, above, neighbours, weights, early, mine, ghost_rows, last,
    own, contracted, down, up, rows, *scratch,
):
    velocities = kicked(coords, veloc, below, above, neighbours, weights, early, mine, scratch)
    moved = propagated(coords[...], velocities, last)
    for x in range(3):
        part = moved[:, ATOMS * x : ATOMS * (x + 1)]
        own[x : x + 1] = part[0:1]
        own[3 + x : 4 + x] = part[1:2]
        contracted[4 * x : 4 * x + 4] = part[4:8]
        rows[0, 4 + x : 5 + x] = part[2:3]
        rows[1, 4 + x : 5 + x] = part[3:4]
    own[6:8] = mine[6:8]
    contracted[12:16] = jnp.zeros((4, ATOMS), f32)
    for which, out in ((0, down), (1, up)):
        rows[which, 0:4] = contracted[8:12]
        rows[which, 7:8] = mine[6:7]
        index = ghost_rows[which : which + 1]
        out[0:8] = ghosts_of(lambda k: contracted[0:8, 128 * k : 128 * k + 128], index)
        out[8:16] = ghosts_of(lambda k: rows[which, :, 128 * k : 128 * k + 128], index)


def early_end_kernel(contracted, neighbours, early):
    for a in range(CHUNKS):
        for g in range(SLOTS // 8):
            for i in range(12):
                early[i, a, g] = own_lookup(
                    lambda k: contracted[i : i + 1, 128 * k : 128 * k + 128], neighbours, g, a
                )


def end_kernel(
    gains, own, contracted, early, below, above, neighbours, weights, w_in, w_out,
    new_pos, new_mom,
    offsets, messages, radials, slow,
):
    charge, mass = own[6:7], own[7:8]

    def store(c, x, a, value):
        slow[c, x, a : a + 1] = value

    def looked_at(i, a, g):
        index = neighbours[8 * g : 8 * g + 8, 128 * a : 128 * a + 128]
        if i < 12:
            out = early[i, a, g]
        else:
            out = own_lookup(lambda k: own[i - 12 : i - 11, 128 * k : 128 * k + 128], neighbours, g, a)
        return with_ghosts(out, below[i : i + 1], above[i : i + 1], index)

    learned_by_lanes(
        lambda c, x, a, g: looked_at(4 * x + c, a, g),
        lambda c, x, a: contracted[4 * x + c : 4 * x + c + 1, 128 * a : 128 * a + 128],
        neighbours, weights, w_in, w_out, offsets, messages, radials, store,
    )
    for a in range(CHUNKS):
        at = slice(128 * a, 128 * a + 128)
        force = cheap_by_lanes(
            lambda x, g, index: looked_at(12 + x, a, g), [own[x : x + 1, at] for x in range(3)], neighbours, weights, a
        )
        for x in range(3):
            value = mass[:, at] * own[3 + x : 4 + x, at] + (0.5 * inner_step) * charge[:, at] * force[x]
            for c in range(CB):
                value = value + gains[c : c + 1] * slow[c, x, a : a + 1]
            new_mom[x, :, at] = value
            new_pos[x, :, at] = own[x : x + 1, at]


def call(kernel, outs, scratch, args, scalars=(), space=pltpu.VMEM, cost=None):
    specs = [pl.BlockSpec(memory_space=pltpu.SMEM if i in scalars else space) for i in range(len(args))]
    shapes = [s if isinstance(s, jax.ShapeDtypeStruct) else jax.ShapeDtypeStruct(s, f32) for s in outs]
    return pl.pallas_call(
        kernel,
        out_shape=shapes,
        in_specs=specs,
        out_specs=[pl.BlockSpec(memory_space=pltpu.VMEM)] * len(outs),
        scratch_shapes=[pltpu.VMEM(*s) if isinstance(s, tuple) else s for s in scratch],
        compiler_params=pltpu.CompilerParams(vmem_limit_bytes=VMEM_LIMIT),
        cost_estimate=cost,
    )(*args)


RING = ("bead", "space")


def ring(step):
    pairs = []
    for bead in range(BEADS):
        for domain in range(N_SPACE):
            to = domain + step
            other = bead if 0 <= to < N_SPACE else bead ^ 4
            pairs.append((bead * N_SPACE + domain, other * N_SPACE + to % N_SPACE))
    return pairs


def exchange(down, up):
    below = lax.ppermute(up, RING, ring(1))
    above = lax.ppermute(down, RING, ring(-1))
    return below, above


def body(
    positions, momenta, neighbours, ghost_rows, species, species_scale, mass_table, w_in, w_out
):
    first, later, last, reduce_, gains = (jnp.asarray(t) for t in tables())

    pos = positions.transpose(1, 0, 2)
    mom = momenta.transpose(1, 0, 2)
    kinds = species.reshape(1, ATOMS)
    ghosts = ghost_rows.reshape(2, 128)

    mine, ghosts, last, gains = call(
        first_kernel,
        [
            (8, ATOMS), jax.ShapeDtypeStruct((2, 128), jnp.int32), jax.ShapeDtypeStruct(last.shape[1:], bf16),
            gains.shape[1:],
        ],
        [
            ((3, 1, ATOMS), f32), ((3, 1, ATOMS), f32), ((1, ATOMS), jnp.int32),
            pltpu.SMEM((2,), f32), pltpu.SMEM((2,), f32), pltpu.SemaphoreType.DMA((8,)),
        ],
        tuple(
            pltpu.with_memory_space_constraint(v, pltpu.HBM)
            for v in (pos, mom, kinds, ghosts, species_scale, mass_table, last, gains)
        ),
        space=pltpu.HBM,
    )
    cost = pl.CostEstimate(flops=10**9, bytes_accessed=10**6, transcendentals=0)
    halves = [[x * 8 + z * 4 + y for z in range(2)] for x in range(4) for y in range(4)]
    pair = lax.all_gather(mine, "bead", axis=0, axis_index_groups=halves)
    down, up = call(send_kernel, [(8, 128)] * 2, [((8, ATOMS), f32)], (pair, ghosts), ())
    below, above = exchange(down, up)
    (early,) = call(
        early_pack_kernel, [(7, CHUNKS, SLOTS // 8, 8, 128)], [], (pair, neighbours), cost=cost
    )
    block, weights = call(
        pack_kernel,
        [(16, 64, 128), (SLOTS, ATOMS)],
        [((64, 128), f32)],
        (pair, early, below, above, neighbours),
    )
    groups = [[x * 8 + z * 4 + y for x in range(4) for y in range(4)] for z in range(2)]
    gathered = lax.all_to_all(block, "bead", 0, 0, axis_index_groups=groups, tiled=True)
    offsets = ((CB, CHUNKS, SLOTS // 8, 5, 8, 128), f32)
    network = ((CB, NRBF, ATOMS), f32)
    w_in = w_in.T
    coords, veloc, down, up = call(
        begin_kernel,
        [(96, ATOMS), (96, ATOMS), (96, 128), (96, 128)],
        [
            ((96, 768), f32), ((96, ATOMS), f32), ((3, 16, 768), f32), offsets, network, network,
            ((3, 16, ATOMS), f32),
        ],
        (gathered, neighbours, weights, mine, ghosts, w_in, w_out, first, reduce_),
    )
    early = lambda coords: call(
        early_middle_kernel, [(3 * EARLY, CHUNKS, SLOTS // 8, 8, 128)], [], (coords, neighbours), cost=cost
    )[0]
    big = [((3 * 72 + 8, 512), bf16), ((96, ATOMS), f32), ((48, 768), f32), ((48, 8, ATOMS), f32), ((144, 512), bf16)]
    below, above = exchange(down, up)
    coords, veloc, down, up = call(
        middle_kernel,
        [(96, ATOMS), (96, ATOMS), (96, 128), (96, 128)],
        big,
        (coords, veloc, below, above, neighbours, weights, early(coords), mine, ghosts, later),
    )
    below, above = exchange(down, up)
    own, contracted, down, up = call(
        last_kernel,
        [(8, ATOMS), (16, ATOMS), (16, 128), (16, 128)],
        [((2, 8, ATOMS), f32)] + big,
        (coords, veloc, below, above, neighbours, weights, early(coords), mine, ghosts, last),
    )
    below, above = exchange(down, up)
    (early,) = call(
        early_end_kernel, [(12, CHUNKS, SLOTS // 8, 8, 128)], [], (contracted, neighbours), cost=cost
    )
    new_pos, new_mom = call(
        end_kernel,
        [(3, 1, ATOMS), (3, 1, ATOMS)],
        [offsets, network, network, ((CB, 3, CHUNKS, 128), f32)],
        (gains, own, contracted, early, below, above, neighbours, weights, w_in, w_out),
    )
    return new_pos.transpose(1, 0, 2), new_mom.transpose(1, 0, 2)


def solution(mesh):
    in_specs = (
        P("bead", None, "space"),
        P("bead", None, "space"),
        P(None, "space"),
        P("space"),
        P("space"),
        P(),
        P(),
        P(),
        P(),
    )
    out_specs = (P("bead", None, "space"), P("bead", None, "space"))
    return jax.shard_map(body, mesh=mesh, in_specs=in_specs, out_specs=out_specs, check_vma=False)
```
